32 devices in a mesh: tok: 16 (over z, y, core), head: 2 (over x).
Axes of the slice: x: 2, y: 2, z: 4, core: 2. Of those that a mesh axis runs over, the one named last changes fastest.
Arguments:
- queries: bfloat16 [4096, 4096], P(('tok', 'head')), may hold values from -60 to 60
- key_states: bfloat16 [4096, 1024], P(('tok', 'head')), may hold values from -60 to 60
- value_states: bfloat16 [4096, 1024], P(('tok', 'head')), may hold values from -6 to 6
- query_gain: float32 [128], replicated, may hold values from 0.5 to 6
- key_gain: float32 [128], replicated, may hold values from 0.5 to 6
- lengths: int32 [8], replicated, may hold values from 1 to 1024, as said below
- slot_order: int32 [16, 24], P('tok'), may hold values from 0 to 23, each once within a row
Outputs:
- attention: bfloat16 [4096, 4096], P('tok', 'head')
- page_pool: bfloat16 [384, 16, 8, 256], P('tok', None, 'head')
The draws below stay inside these ranges and needn't reach their ends.
Inputs may be any that keep to these rules, and one draw needn't show every extreme that they name: `lengths`: they sum to 4096; the first is 8 and the second exactly 1024. `slot_order`: each row is a permutation of the 24 slots.
All inputs are finite; a program needn't handle non-finite values.
Results may differ from the reference program's by a relative error of at most 0.0044.
The reference program's roundings to bfloat16 on the way (of `q_rot`, `k_rot` and `weights`) count: a program that leaves them out, or rounds other values in their place, can miss the bound.
Values may be sent and summed in bfloat16 or wider, within the bound.
No kernel may reach another device: no remote copies, remote signals or barrier semaphores. Data moves between devices by JAX's collectives and lax.ppermute only.
A program may use at most 64 MiB of HBM per device.

```python
import math
import jax
import jax.numpy as jnp
from jax import lax

HEADS = 32
KV_HEADS = 8
HEAD_DIM = 128
REACH = 4
PAGE = 16
SHARD = 256
TOKENS = 4096
MOST = 1024
SEGS = 8
POOL = 24
N_TOK = 16


def row_scaled(own, width):
    sample = jax.random.normal(jax.random.fold_in(own, 1), (TOKENS, width), jnp.float32)
    scales = jnp.exp(jax.random.uniform(jax.random.fold_in(own, 2), (TOKENS, 1), jnp.float32, math.log(0.5), math.log(5.0)))
    return sample * scales


def draw_queries(key, part):
    width = HEADS * HEAD_DIM
    own = jax.random.fold_in(key, 1000)
    sample = row_scaled(own, width)
    return jnp.clip(sample, -60.0, 60.0).astype(jnp.bfloat16)


def draw_key_states(key, part):
    width = KV_HEADS * HEAD_DIM
    own = jax.random.fold_in(key, 2000)
    sample = row_scaled(own, width)
    return jnp.clip(sample, -60.0, 60.0).astype(jnp.bfloat16)


def gain_draw(own):
    sample = jnp.exp(jax.random.uniform(jax.random.fold_in(own, 1), (HEAD_DIM,), jnp.float32, math.log(0.5), math.log(2.0)))
    return sample.astype(jnp.float32)


def draw_query_gain(key, part):
    return gain_draw(jax.random.fold_in(key, 3000))


def draw_key_gain(key, part):
    return gain_draw(jax.random.fold_in(key, 4000))


def draw_lengths(key, part):
    others = SEGS - 2
    extra = TOKENS - MOST - PAGE // 2 - others
    power = jax.random.randint(jax.random.fold_in(key, 5000), (others,), 0, 5).astype(jnp.int32)
    weight = jnp.left_shift(jnp.ones((others,), jnp.int32), power)
    room = MOST - 1
    share = jnp.minimum(extra * weight // jnp.sum(weight), room).astype(jnp.int32)
    remain = (extra - jnp.sum(share)).astype(jnp.int32)

    def fill_one(index, carry):
        shares, left = carry
        added = jnp.minimum(room - shares[index], left)
        return (shares.at[index].add(added), left - added)
    share, remain = lax.fori_loop(0, others, fill_one, (share, remain))
    leading = jnp.array([PAGE // 2, MOST], jnp.int32)
    return jnp.concatenate([leading, 1 + share]).astype(jnp.int32)


def level_of(stream_key, extent, cuts, low, top_value):
    loudness, own = 1.0, jax.random.fold_in(stream_key, 6)
    for dim, parts in cuts:
        heights = jnp.exp(jax.random.uniform(jax.random.fold_in(own, dim), (parts,), jnp.float32, low / len(cuts), top_value / len(cuts)))
        loudness = loudness * jnp.repeat(heights, extent[dim] // parts).reshape([-1 if axis == dim else 1 for axis in range(len(extent))])
    return loudness


def scatter_about(own_key, shape, spread, reach, split=(), kind=jnp.bfloat16):
    values = jax.random.normal(own_key, shape, jnp.float32) * spread
    if len(split) > 0:
        values = level_of(own_key, shape, split, -0.22, 0.18) * values
    return jnp.clip(values, min=-reach, max=reach).astype(kind)


def setup_inputs(seed: int = 0) -> dict:
    splits = jax.random.split(jax.random.key(seed), 8)
    queries = draw_queries(jax.random.fold_in(splits[7], 71), 0)
    key_states = draw_key_states(jax.random.fold_in(splits[7], 71), 0)
    value_states = scatter_about(splits[2], (TOKENS, KV_HEADS * HEAD_DIM), 1.0, 6.0, ((0, 32),))
    query_gain = draw_query_gain(jax.random.fold_in(splits[7], 71), 0)
    key_gain = draw_key_gain(jax.random.fold_in(splits[7], 71), 0)
    lengths = draw_lengths(jax.random.fold_in(splits[7], 71), 0)
    slot_order = jax.vmap(lambda own: jax.random.permutation(own, POOL))(jax.random.split(splits[6], N_TOK)).reshape((N_TOK, POOL)).astype(jnp.int32)
    return {"queries": queries, "key_states": key_states, "value_states": value_states, "query_gain": query_gain, "key_gain": key_gain, "lengths": lengths, "slot_order": slot_order}


def seg_table(lengths):
    seg_ends = jnp.cumsum(lengths).astype(jnp.int32)
    seg_starts = (seg_ends - lengths).astype(jnp.int32)
    return (seg_starts, seg_ends)

def locate(points, seg_starts, seg_ends):
    segment = lax.optimization_barrier(jnp.sum((points[:, None] >= seg_starts[None, :]).astype(jnp.int32), axis=1)) - 1
    onehot = segment[:, None] == jnp.arange(seg_starts.shape[0], dtype=jnp.int32)[None, :]
    first = lax.optimization_barrier(jnp.sum(jnp.where(onehot, seg_starts[None, :], 0), axis=1)).astype(jnp.int32)
    finish = lax.optimization_barrier(jnp.sum(jnp.where(onehot, seg_ends[None, :], 0), axis=1)).astype(jnp.int32)
    return (segment.astype(jnp.int32), first, finish)

def rms_scale(tensor, gain_vec):
    power_mean = lax.optimization_barrier(jnp.mean(tensor * tensor, axis=-1, keepdims=True))
    return tensor * lax.rsqrt(power_mean + 1e-06) * gain_vec

def rotary(tensor, offset):
    half_dim = tensor.shape[-1] // 2
    frequency = jnp.exp(jnp.arange(half_dim, dtype=jnp.float32) * (-2.0 * math.log(1000000.0) / tensor.shape[-1]))
    angles = offset.astype(jnp.float32)[:, None] * frequency[None, :]
    cosine = jnp.concatenate([jnp.cos(angles), jnp.cos(angles)], axis=-1)[:, None, :]
    sine_rows = jnp.concatenate([jnp.sin(angles), jnp.sin(angles)], axis=-1)[:, None, :]
    turned = jnp.concatenate([-tensor[..., half_dim:], tensor[..., :half_dim]], axis=-1)
    return tensor * cosine + turned * sine_rows

def reference(queries, key_states, value_states, query_gain, key_gain, lengths, slot_order):
    head_dim = HEAD_DIM
    group_size = HEADS // KV_HEADS
    seg_starts, seg_ends = seg_table(lengths)
    points = jnp.arange(TOKENS, dtype=jnp.int32)
    segment, first, finish = locate(points, seg_starts, seg_ends)
    offset = points - first
    q_rot = rotary(rms_scale(queries.astype(jnp.float32).reshape(TOKENS, HEADS, head_dim), query_gain), offset).astype(jnp.bfloat16)
    k_rot = rotary(rms_scale(key_states.astype(jnp.float32).reshape(TOKENS, KV_HEADS, head_dim), key_gain), offset).astype(jnp.bfloat16)
    v_all = value_states.reshape(TOKENS, KV_HEADS, head_dim)
    margin = REACH * SHARD
    span_len = (REACH + 1) * SHARD
    k_pad = jnp.concatenate([jnp.zeros((margin, KV_HEADS, head_dim), jnp.bfloat16), k_rot], axis=0)
    v_pad = jnp.concatenate([jnp.zeros((margin, KV_HEADS, head_dim), jnp.bfloat16), v_all], axis=0)
    seg_pad = jnp.concatenate([jnp.full((margin,), -1, jnp.int32), segment], axis=0)
    score_scale = 1.0 / math.sqrt(head_dim)

    def one_shard(shard_index):
        row_first = (shard_index * SHARD).astype(jnp.int32)
        q_part = lax.dynamic_slice_in_dim(q_rot, row_first, SHARD, 0).reshape(SHARD, KV_HEADS, group_size, head_dim)
        k_part = lax.dynamic_slice_in_dim(k_pad, row_first, span_len, 0)
        v_part = lax.dynamic_slice_in_dim(v_pad, row_first, span_len, 0)
        seg_keys = lax.dynamic_slice_in_dim(seg_pad, row_first, span_len, 0)
        seg_query = lax.dynamic_slice_in_dim(segment, row_first, SHARD, 0)
        query_pos = row_first + jnp.arange(SHARD, dtype=jnp.int32)
        key_pos = row_first - margin + jnp.arange(span_len, dtype=jnp.int32)
        visible = (seg_query[:, None] == seg_keys[None, :]) & (key_pos[None, :] <= query_pos[:, None])

        def one_group(group_index):
            q_group = lax.dynamic_index_in_dim(q_part, group_index, 1, keepdims=False)
            k_group = lax.dynamic_index_in_dim(k_part, group_index, 1, keepdims=False)
            v_group = lax.dynamic_index_in_dim(v_part, group_index, 1, keepdims=False)
            scores = jnp.einsum('qrd,kd->qrk', q_group.astype(jnp.float32), k_group.astype(jnp.float32)) * score_scale
            scores = jnp.where(visible[:, None, :], scores, -1e+30)
            top_row = lax.optimization_barrier(jnp.max(scores, axis=-1, keepdims=True))
            expo = jnp.where(visible[:, None, :], jnp.exp(scores - top_row), 0.0)
            denom = lax.optimization_barrier(jnp.sum(expo, axis=-1))
            weights = expo.astype(jnp.bfloat16)
            mixed = jnp.einsum('qrk,kd->qrd', weights.astype(jnp.float32), v_group.astype(jnp.float32))
            return mixed / denom[..., None]
        per_group = lax.map(one_group, jnp.arange(KV_HEADS, dtype=jnp.int32))
        return jnp.transpose(per_group, (1, 0, 2, 3)).reshape(SHARD, HEADS * head_dim).astype(jnp.bfloat16)
    attention = lax.map(one_shard, jnp.arange(N_TOK, dtype=jnp.int32)).reshape(TOKENS, HEADS * head_dim)
    page_last = jnp.minimum(first + (offset // PAGE + 1) * PAGE, finish) - 1
    page_ends = (offset % PAGE == PAGE - 1) | (points == finish - 1)
    flags = page_ends.astype(jnp.int32)
    before = jnp.cumsum(flags).astype(jnp.int32) - flags
    owner = (page_last // SHARD).astype(jnp.int32)
    rank_rows = before[page_last] - before[owner * SHARD]
    page_id = owner * POOL + slot_order[owner, rank_rows]
    target = page_id * PAGE + offset % PAGE
    paired = jnp.concatenate([k_rot, v_all], axis=-1)
    page_pool = jnp.zeros((N_TOK * POOL * PAGE, KV_HEADS, 2 * head_dim), jnp.bfloat16).at[target].set(paired)
    page_pool = page_pool.reshape(N_TOK * POOL, PAGE, KV_HEADS, 2 * head_dim)
    return (attention, page_pool)
```

```python
import functools
import math

import jax
import jax.numpy as jnp
from jax import lax
from jax.experimental import pallas as pl
from jax.experimental.pallas import tpu as pltpu
from jax.sharding import PartitionSpec as P

D = 128
REACH = 4
PAGE = 16
HIDE = -2e30
FLOOR = -1e30
MIB = 1024 * 1024


def around(x, axis, by):
    peers = lax.axis_size(axis)
    return lax.ppermute(x, axis, [(i, (i + by) % peers) for i in range(peers)])


def core_swap(x):
    peers = lax.axis_size("tok")
    return lax.ppermute(x, "tok", [(i, i ^ 1) for i in range(peers)])


def seg_first(pos, lengths, segs):
    first = jnp.zeros_like(pos)
    start = jnp.int32(0)
    for s in range(segs):
        first = jnp.where(pos >= start, start, first)
        start = start + lengths[s]
    return first


def rotate(x, gain, cosine, sine):
    power = jnp.mean(x * x, axis=-1, keepdims=True)
    x = x * lax.rsqrt(power + 1e-06) * gain
    return x * cosine + pltpu.roll(x, D // 2, 1) * sine


def lanes(ref, index, width):
    return ref[:, pl.ds(pl.multiple_of(index * width, width), width)]


def kv_prep_body(heads, segs, lengths, k_ref, v_ref, gain_ref, cos_ref, sin_ref, *outs):
    rows = k_ref.shape[0]
    kvl = k_ref.shape[1] // D // heads
    x = lax.axis_index("head")
    base = (lax.axis_index("tok") * heads + x) * rows
    pos = base + lax.broadcasted_iota(jnp.int32, (rows, D), 0)
    offset = (pos - seg_first(pos, lengths, segs)).astype(jnp.float32)
    lane = lax.broadcasted_iota(jnp.int32, (rows, D), 1)
    lower = lane < D // 2
    half = jnp.where(lower, lane, lane - D // 2).astype(jnp.float32)
    angles = offset * jnp.exp(half * (-2.0 * math.log(1000000.0) / D))
    cosine = jnp.cos(angles)
    sine = jnp.where(lower, -1.0, 1.0) * jnp.sin(angles)
    cos_ref[...] = cosine
    sin_ref[...] = sine
    gain = gain_ref[...]
    for d in range(heads):
        peer = lax.rem(x + d, heads)
        for j in range(kvl):
            head = peer * kvl + j
            key = lanes(k_ref, head, D).astype(jnp.float32)
            outs[d][:, 2 * j * D : (2 * j + 1) * D] = rotate(key, gain, cosine, sine).astype(
                jnp.bfloat16
            )
            outs[d][:, (2 * j + 1) * D : (2 * j + 2) * D] = lanes(v_ref, head, D)


def q_prep_body(heads, q_ref, gain_ref, cos_ref, sin_ref, *outs):
    ql = q_ref.shape[1] // D // heads
    x = lax.axis_index("head")
    gain, cosine, sine = gain_ref[...], cos_ref[...], sin_ref[...]
    for d in range(heads):
        peer = lax.rem(x + d, heads)
        for j in range(ql):
            query = lanes(q_ref, peer * ql + j, D).astype(jnp.float32)
            outs[d][:, j * D : (j + 1) * D] = rotate(query, gain, cosine, sine).astype(
                jnp.bfloat16
            )


VMEM = pl.BlockSpec(memory_space=pltpu.VMEM)
SMEM = pl.BlockSpec(memory_space=pltpu.SMEM)


def params():
    return pltpu.CompilerParams(vmem_limit_bytes=48 * MIB)


def kv_prep(lengths, keys, values, gain, heads):
    rows, width = keys.shape
    table = jax.ShapeDtypeStruct((rows, D), jnp.float32)
    part = jax.ShapeDtypeStruct((rows, 2 * width // heads), jnp.bfloat16)
    return pl.pallas_call(
        functools.partial(kv_prep_body, heads, lengths.shape[0]),
        out_shape=[table, table] + [part] * heads,
        in_specs=[SMEM, VMEM, VMEM, VMEM],
        out_specs=[VMEM] * (2 + heads),
        compiler_params=params(),
        name="kv_prep",
    )(lengths, keys, values, gain)


def q_prep(queries, gain, cosine, sine, heads):
    rows, width = queries.shape
    part = jax.ShapeDtypeStruct((rows, width // heads), jnp.bfloat16)
    return pl.pallas_call(
        functools.partial(q_prep_body, heads),
        out_shape=[part] * heads,
        in_specs=[VMEM] * 4,
        out_specs=[VMEM] * heads,
        compiler_params=params(),
        name="q_prep",
    )(queries, gain, cosine, sine)


def shard_of(kind, tok):
    core = lax.rem(tok, 2)
    if kind == "own":
        return tok
    if kind == "far":
        return tok - 4
    if kind == "near":
        return tok - 2
    if kind == "near_swap":
        return tok + 1 - 2 * core - 2
    return jnp.where(core == 0, tok - 3, tok - 1)


def attend_body(heads, segs, rows, pieces, first_stage, last_stage, n_q, n_kv, lengths, *refs):
    q_refs, refs = refs[:n_q], refs[n_q:]
    kv_refs, refs = refs[:n_kv], refs[n_kv:]
    if not first_stage:
        m_in, l_in, acc_in = refs[:3]
        refs = refs[3:]
    if last_stage:
        out_ref, refs = refs[0], refs[1:]
    else:
        m_out, l_out, acc_out = refs[:3]
        refs = refs[3:]
    s_scr, bias_scr = refs
    x = lax.axis_index("head")
    tok = lax.axis_index("tok")
    shard_rows = heads * rows
    kvl = kv_refs[0].shape[1] // (2 * D)
    group = q_refs[0].shape[1] // D // kvl
    wide = group * rows
    scale = math.log2(math.e) / math.sqrt(D)
    lane = lax.broadcasted_iota(jnp.int32, (rows, rows), 1)
    sub = lax.broadcasted_iota(jnp.int32, (rows, rows), 0)
    n_piece = len(pieces)

    def one_chunk(d, q_ref, q_row):
        origin = lax.rem(x - d + heads, heads)
        q_pos = tok * shard_rows + origin * rows + lane
        q_first = seg_first(q_pos, lengths, segs)
        for i, (a, row, kind, kd) in enumerate(pieces):
            k_origin = lax.rem(x - kd + heads, heads)
            k_pos = shard_of(kind, tok) * shard_rows + k_origin * rows + sub
            seen = (k_pos >= q_first) & (k_pos <= q_pos)
            bias_scr[i * rows : (i + 1) * rows, :] = jnp.where(seen, 0.0, HIDE)

        def one_group(g, carry):
            q4 = q_ref[pl.ds(q_row, rows), pl.ds(pl.multiple_of(g * group * D, group * D), group * D)]
            q = jnp.concatenate([q4[:, r * D : (r + 1) * D] for r in range(group)], axis=0)
            if first_stage:
                top = jnp.full((8, wide), FLOOR, jnp.float32)
            else:
                top = jnp.broadcast_to(m_in[d, g], (8, wide))
            for i, (a, row, kind, kd) in enumerate(pieces):
                key = kv_refs[a][
                    row * rows : (row + 1) * rows, pl.ds(pl.multiple_of(g * 2 * D, 2 * D), D)
                ]
                score = lax.dot_general(
                    key, q, (((1,), (1,)), ((), ())), preferred_element_type=jnp.float32
                )
                bias = bias_scr[i * rows : (i + 1) * rows, :]
                score = score * scale + jnp.concatenate([bias] * group, axis=1)
                s_scr[i * rows : (i + 1) * rows, :] = score
                top = jnp.maximum(top, jnp.max(score.reshape(rows // 8, 8, wide), axis=0))
            top = jnp.max(top, axis=0, keepdims=True)
            if first_stage:
                total = jnp.zeros((1, wide), jnp.float32)
                acc = jnp.zeros((D, wide), jnp.float32)
            else:
                fade = jnp.exp2(m_in[d, g] - top)
                total = l_in[d, g] * fade
                acc = acc_in[d, g] * fade
            part = jnp.zeros((8, wide), jnp.float32)
            for i, (a, row, kind, kd) in enumerate(pieces):
                value = kv_refs[a][
                    row * rows : (row + 1) * rows, pl.ds(pl.multiple_of(g * 2 * D + D, D), D)
                ]
                expo = jnp.exp2(s_scr[i * rows : (i + 1) * rows, :] - top)
                part = part + jnp.sum(expo.reshape(rows // 8, 8, wide), axis=0)
                acc = acc + lax.dot_general(
                    value,
                    expo.astype(jnp.bfloat16),
                    (((0,), (0,)), ((), ())),
                    preferred_element_type=jnp.float32,
                )
            total = total + jnp.sum(part, axis=0, keepdims=True)
            if last_stage:
                acc = acc * (1.0 / total)
                at = pl.ds(pl.multiple_of(origin * rows, rows), rows)
                for r in range(group):
                    out_ref[at, pl.ds(pl.multiple_of((g * group + r) * D, D), D)] = (
                        acc[:, r * rows : (r + 1) * rows].T.astype(jnp.bfloat16)
                    )
            else:
                m_out[d, g] = top
                l_out[d, g] = total
                acc_out[d, g] = acc
            return carry

        lax.fori_loop(0, kvl, one_group, 0)

    one_chunk(0, q_refs[0], 0)
    if heads == 2:
        one_chunk(1, q_refs[1], 0)
    elif heads > 2:
        def loop_body(d, carry):
            one_chunk(d, q_refs[1], pl.multiple_of((d - 1) * rows, rows))
            return carry

        lax.fori_loop(1, heads, loop_body, 0)


def attend(lengths, qs, kvs, pieces, state, last, heads):
    rows = qs[0].shape[0]
    kvl = kvs[0].shape[1] // (2 * D)
    ql = qs[0].shape[1] // D
    wide = ql // kvl * rows
    if last:
        out_shape = jax.ShapeDtypeStruct((heads * rows, ql * D), jnp.bfloat16)
    else:
        row = jax.ShapeDtypeStruct((heads, kvl, 1, wide), jnp.float32)
        out_shape = [row, row, jax.ShapeDtypeStruct((heads, kvl, D, wide), jnp.float32)]
    inputs = [lengths, *qs, *kvs, *(state or [])]
    work = heads * kvl * wide * len(pieces) * rows
    return pl.pallas_call(
        functools.partial(
            attend_body, heads, lengths.shape[0], rows, pieces, state is None, last,
            len(qs), len(kvs),
        ),
        out_shape=out_shape,
        in_specs=[SMEM] + [VMEM] * (len(inputs) - 1),
        out_specs=VMEM if last else [VMEM] * 3,
        scratch_shapes=[
            pltpu.VMEM((len(pieces) * rows, wide), jnp.float32),
            pltpu.VMEM((len(pieces) * rows, rows), jnp.float32),
        ],
        compiler_params=params(),
        cost_estimate=pl.CostEstimate(
            flops=4 * D * work, bytes_accessed=4 * MIB, transcendentals=work
        ),
        name="attend_last" if last else "attend_part",
    )(*inputs)


def pages_body(heads, segs, pool, lengths, slots, tail_ref, own_ref, rest_ref, out_ref, hot, ends):
    rows = own_ref.shape[0]
    shard_rows = heads * rows
    x = lax.axis_index("head")
    base = lax.axis_index("tok") * shard_rows
    end = jnp.int32(0)
    for s in range(segs):
        end = end + lengths[s]
        ends[s] = end
    hot[...] = jnp.zeros_like(hot)
    width = hot.shape[1]
    lane = lax.broadcasted_iota(jnp.int32, (PAGE, width), 1)
    sub = lax.broadcasted_iota(jnp.int32, (PAGE, width), 0)

    def finish_of(a):
        def look(s, found):
            return jnp.where((found == 0) & (ends[s] > a), ends[s], found)

        return lax.fori_loop(0, segs, look, jnp.int32(0))

    def start_of(a):
        def look(s, found):
            return jnp.where(ends[s] <= a, ends[s], found)

        return lax.fori_loop(0, segs, look, jnp.int32(0))

    first = start_of(base)
    page = first + ((base - first) // PAGE) * PAGE

    def one_page(rank, a):
        stop = jnp.minimum(a + PAGE, finish_of(a))
        owned = (stop > base) & (stop <= base + shard_rows)

        @pl.when(owned)
        def _():
            shift = a - base
            token = sub + shift
            chunk = token // rows
            d = lax.rem(x - chunk + 2 * heads, heads)
            column = jnp.where(token < 0, token + PAGE, 128 + d * rows + token - chunk * rows)
            mark = (lane == column) & (sub < stop - a)
            slot = slots[0, rank]
            hot[pl.ds(pl.multiple_of(slot * PAGE, PAGE), PAGE), :] = mark.astype(hot.dtype)

        return jnp.where(owned, stop, a)

    lax.fori_loop(0, pool, one_page, page)
    mark = hot[...].astype(jnp.bfloat16)
    tail = jnp.concatenate(
        [tail_ref[...], jnp.zeros((128 - PAGE, tail_ref.shape[1]), jnp.bfloat16)], axis=0
    )
    source = jnp.concatenate([tail, own_ref[...], rest_ref[...]], axis=0)
    out_ref[...] = jnp.dot(mark, source, preferred_element_type=jnp.float32).astype(jnp.bfloat16)


def pages(lengths, slots, tail, own, rest, heads):
    rows, width = own.shape
    pool = slots.shape[1]
    return pl.pallas_call(
        functools.partial(pages_body, heads, lengths.shape[0], pool),
        out_shape=jax.ShapeDtypeStruct((pool * PAGE, width), jnp.bfloat16),
        in_specs=[SMEM, SMEM, VMEM, VMEM, VMEM],
        out_specs=VMEM,
        scratch_shapes=[
            pltpu.VMEM((pool * PAGE, 128 + heads * rows), jnp.float32),
            pltpu.SMEM((lengths.shape[0],), jnp.int32),
        ],
        compiler_params=params(),
        name="pages",
    )(lengths, slots, tail, own, rest)


def join(parts):
    return parts[0] if len(parts) == 1 else jnp.concatenate(parts, axis=0)


def on_device(queries, key_states, value_states, query_gain, key_gain, lengths, slot_order):
    heads = lax.axis_size("head")
    rows = queries.shape[0]
    core = lax.rem(lax.axis_index("tok"), 2)
    x = lax.axis_index("head")

    cosine, sine, own, *away = kv_prep(
        lengths, key_states, value_states, key_gain.reshape(1, D), heads
    )
    rest = join([around(part, "head", d) for d, part in enumerate(away, 1)])
    own4, own2 = around(own, "tok", 4), around(own, "tok", 2)
    q_own, *q_away = q_prep(queries, query_gain.reshape(1, D), cosine, sine, heads)
    q_rest = join([around(part, "head", d) for d, part in enumerate(q_away, 1)])
    rest4, rest2 = around(rest, "tok", 4), around(rest, "tok", 2)

    tail_at = lax.rem(x + 1, heads)
    rest_tail = lax.dynamic_slice_in_dim(
        rest, jnp.maximum(tail_at, 1) * rows - PAGE, PAGE, axis=0
    )
    tail = around(jnp.where(tail_at == 0, own[rows - PAGE :], rest_tail), "tok", 1)
    pool2d = pages(lengths, slot_order, tail, own, rest, heads)
    kvl = own.shape[1] // (2 * D)
    page_pool = pool2d.reshape(slot_order.shape[1], PAGE, kvl, 2 * D)

    own_s = core_swap(jnp.concatenate([jnp.where(core == 0, own, own4), own2], axis=0))
    rest_s = core_swap(jnp.concatenate([jnp.where(core == 0, rest, rest4), rest2], axis=0))

    others = range(1, heads)
    many = heads - 1
    early = [own, rest, own4, own2, own_s]
    pieces = [(0, 0, "own", 0)] + [(1, d - 1, "own", d) for d in others]
    pieces += [(2, 0, "far", 0), (3, 0, "near", 0), (4, 0, "mix_swap", 0), (4, 1, "near_swap", 0)]
    state = attend(lengths, [q_own, q_rest], early, tuple(pieces), None, False, heads)
    late = [rest4, rest2, rest_s]
    pieces = [(0, d - 1, "far", d) for d in others]
    pieces += [(1, d - 1, "near", d) for d in others]
    pieces += [(2, d - 1, "mix_swap", d) for d in others]
    pieces += [(2, many + d - 1, "near_swap", d) for d in others]
    attention = attend(lengths, [q_own, q_rest], late, tuple(pieces), state, True, heads)
    return (attention, page_pool)


def solution(mesh):
    in_specs = (
        P(("tok", "head"), None),
        P(("tok", "head"), None),
        P(("tok", "head"), None),
        P(),
        P(),
        P(),
        P("tok", None),
    )
    out_specs = (P("tok", "head"), P("tok", None, "head", None))
    return jax.shard_map(
        on_device, mesh=mesh, in_specs=in_specs, out_specs=out_specs, check_vma=False
    )
```

```python
import functools
import math

import jax
import jax.numpy as jnp
from jax import lax
from jax.experimental import pallas as pl
from jax.experimental.pallas import tpu as pltpu
from jax.sharding import PartitionSpec as P

D = 128
PAGE = 16
HIDE = -2e30
FLOOR = -1e30
MIB = 1024 * 1024
SCALE = math.log2(math.e) / math.sqrt(D)

VMEM = pl.BlockSpec(memory_space=pltpu.VMEM)
SMEM = pl.BlockSpec(memory_space=pltpu.SMEM)
TOKEN = jax.ShapeDtypeStruct((8, D), jnp.float32)
ANY = pl.BlockSpec(memory_space=pl.ANY)
HBM = pl.BlockSpec(memory_space=pltpu.HBM)


def cost(us):
    return pl.CostEstimate(flops=int(us * 1.15e9), bytes_accessed=0, transcendentals=0)


def params(mib=32):
    return pltpu.CompilerParams(vmem_limit_bytes=mib * MIB)


def around(x, axis, by):
    peers = lax.axis_size(axis)
    return lax.ppermute(x, axis, [(i, (i + by) % peers) for i in range(peers)])


def swap(x, bit):
    peers = lax.axis_size("tok")
    return lax.ppermute(x, "tok", [(i, i ^ bit) for i in range(peers)])


def join(parts):
    return parts[0] if len(parts) == 1 else jnp.concatenate(parts, axis=0)


def at(index):
    return pl.ds(index, D) if isinstance(index, int) else pl.ds(pl.multiple_of(index, D), D)


def seg_first(pos, lengths, segs):
    first = jnp.zeros_like(pos)
    start = jnp.int32(0)
    for s in range(segs):
        first = jnp.where(pos >= start, start, first)
        start = start + lengths[s]
    return first


def seg_bounds(axis, lengths, segs):
    index = lax.broadcasted_iota(jnp.int32, (D, D), axis)
    begin = jnp.where(index == segs, -(2**30), 2**30)
    end = jnp.zeros((D, D), jnp.int32)
    here = jnp.int32(0)
    for s in range(segs):
        begin = jnp.where(index == s, here, begin)
        here = here + lengths[s]
        end = jnp.where(index == s, here, end)
    return begin, end


def rotate(x, cos_gain, sin_gain):
    power = jnp.mean(x * x, axis=0, keepdims=True)
    half = D // 2
    turned = jnp.concatenate([x[half:], x[:half]], axis=0)
    return (x * cos_gain + turned * sin_gain) * lax.rsqrt(power + 1e-06)


def gain_tables(cosine, sine, gain_row):
    gain = jnp.broadcast_to(gain_row, (D, D)).T
    half = D // 2
    turned = jnp.concatenate([gain[half:], gain[:half]], axis=0)
    cos_gain = jnp.concatenate([cosine, cosine], axis=0) * gain
    sin_gain = jnp.concatenate([-sine, sine], axis=0) * turned
    return cos_gain, sin_gain


def kv_prep_body(heads, segs, lengths_in, k_in, v_in, gain_in, cos_ref, sin_ref, *refs):
    outs, (lengths, k_ref, v_ref, gain_ref, sems) = refs[:heads], refs[heads:]
    pairs = [(lengths_in, lengths), (gain_in, gain_ref), (k_in, k_ref), (v_in, v_ref)]
    copies = [pltpu.make_async_copy(a, b, sems.at[i]) for i, (a, b) in enumerate(pairs)]
    for copy in copies:
        copy.start()
    rows = k_ref.shape[0]
    kvl = k_ref.shape[1] // D // heads
    x = lax.axis_index("head")
    base = (lax.axis_index("tok") * heads + x) * rows
    half = D // 2
    pos = base + lax.broadcasted_iota(jnp.int32, (half, rows), 1)
    step = lax.broadcasted_iota(jnp.int32, (half, rows), 0).astype(jnp.float32)
    frequency = jnp.exp(step * (-2.0 * math.log(1000000.0) / D))
    copies[0].wait()
    offset = (pos - seg_first(pos, lengths, segs)).astype(jnp.float32)
    angles = offset * frequency
    cosine, sine = jnp.cos(angles), jnp.sin(angles)
    cos_ref[...] = cosine
    sin_ref[...] = sine
    copies[1].wait()
    cos_gain, sin_gain = gain_tables(cosine, sine, gain_ref[...])
    copies[2].wait()
    copies[3].wait()
    for d in reversed(range(heads)):
        peer = lax.rem(x + d, heads)
        for j in range(kvl):
            head = peer * kvl + j
            key = k_ref[:, at(head * D)].astype(jnp.float32).T
            key = rotate(key, cos_gain, sin_gain).T
            outs[d][:, 2 * j * D : (2 * j + 1) * D] = key.astype(jnp.bfloat16)
            value = v_ref[:, at(head * D)]
            outs[d][:, (2 * j + 1) * D : (2 * j + 2) * D] = value.T


def kv_prep(lengths, keys, values, gain, heads):
    rows, width = keys.shape
    table = jax.ShapeDtypeStruct((D // 2, rows), jnp.float32)
    part = jax.ShapeDtypeStruct((rows, 2 * width // heads), jnp.bfloat16)
    return pl.pallas_call(
        functools.partial(kv_prep_body, heads, lengths.shape[0]),
        out_shape=[table, table] + [part] * heads,
        in_specs=[HBM] * 4,
        out_specs=[VMEM] * (2 + heads),
        scratch_shapes=[
            pltpu.SMEM(lengths.shape, jnp.int32),
            pltpu.VMEM(keys.shape, jnp.bfloat16),
            pltpu.VMEM(values.shape, jnp.bfloat16),
            pltpu.VMEM(gain.shape, jnp.float32),
            pltpu.SemaphoreType.DMA((4,)),
        ],
        compiler_params=params(62),
        cost_estimate=cost(0.01),
        name="kv_prep",
    )(lengths, keys, values, gain)


def q_prep_body(heads, q_in, gain_in, cos_in, sin_in, *refs):
    outs, (token, q_ref, gain_ref, cos_ref, sin_ref, sems) = refs[:heads], refs[heads:]
    token[...] = jnp.zeros_like(token)
    ql = q_ref.shape[1] // D // heads
    x = lax.axis_index("head")
    tables = [(gain_in, gain_ref), (cos_in, cos_ref), (sin_in, sin_ref)]
    tables = [
        pltpu.make_async_copy(a, b, sems.at[heads + i]) for i, (a, b) in enumerate(tables)
    ]
    for copy in tables:
        copy.start()
    copies = []
    for d in reversed(range(heads)):
        part = pl.ds(pl.multiple_of(lax.rem(x + d, heads) * ql * D, D), ql * D)
        copy = pltpu.make_async_copy(q_in.at[:, part], q_ref.at[:, part], sems.at[d])
        copy.start()
        copies.append(copy)
    for copy in tables:
        copy.wait()
    cos_gain, sin_gain = gain_tables(cos_ref[...], sin_ref[...], gain_ref[...])
    for d in reversed(range(heads)):
        copies[heads - 1 - d].wait()
        peer = lax.rem(x + d, heads)
        for j in range(ql):
            query = q_ref[:, at((peer * ql + j) * D)].astype(jnp.float32).T
            outs[d][j * D : (j + 1) * D, :] = rotate(query, cos_gain, sin_gain).astype(
                jnp.bfloat16
            )


def q_prep(queries, gain, cosine, sine, heads):
    rows, width = queries.shape
    part = jax.ShapeDtypeStruct((width // heads, rows), jnp.bfloat16)
    return pl.pallas_call(
        functools.partial(q_prep_body, heads),
        out_shape=[part] * heads + [TOKEN],
        in_specs=[HBM] * 4,
        out_specs=[VMEM] * (heads + 1),
        scratch_shapes=[
            pltpu.VMEM(queries.shape, jnp.bfloat16),
            pltpu.VMEM(gain.shape, jnp.float32),
            pltpu.VMEM(cosine.shape, jnp.float32),
            pltpu.VMEM(sine.shape, jnp.float32),
            pltpu.SemaphoreType.DMA((heads + 3,)),
        ],
        compiler_params=params(),
        cost_estimate=cost(0.01),
        name="q_prep",
    )(queries, gain, cosine, sine)


def shard_of(kind, tok):
    core = lax.rem(tok, 2)
    if kind == "own":
        return tok
    if kind == "far":
        return tok - 4
    if kind == "near":
        return tok - 2
    if kind == "near_swap":
        return tok - 1 - 2 * core
    return jnp.where(core == 0, tok - 3, tok - 1)


def attend_body(heads, segs, jobs, last, counts, lengths, *refs):
    n_q, n_kv, n_state, n_earlier = counts
    q_refs, refs = refs[:n_q], refs[n_q:]
    kv_refs, refs = refs[:n_kv], refs[n_kv:]
    states, refs = refs[: 3 * n_state], refs[3 * n_state :]
    earlier, refs = refs[:n_earlier], refs[n_earlier:]
    n_out = 2 if last else 3 * len(jobs)
    outs, (s_scr, p_scr, e_scr, f_scr, *page) = refs[:n_out], refs[n_out:]
    bufs = s_scr.shape[0]
    x = lax.axis_index("head")
    tok = lax.axis_index("tok")
    rows = D
    kvl = kv_refs[0].shape[1] // (2 * D)
    ql = f_scr.shape[2] // D * kvl
    group = ql // kvl
    wide = group * rows
    lane = lax.broadcasted_iota(jnp.int32, (rows, rows), 1)
    sub = lax.broadcasted_iota(jnp.int32, (rows, rows), 0)
    key_begin, key_end = seg_bounds(1, lengths, segs)
    query_begin, query_end = seg_bounds(0, lengths, segs)

    def key_block(pieces, g, side, axis):
        cols = at((2 * g + side) * D)
        return jnp.concatenate(
            [kv_refs[a][row * rows : (row + 1) * rows, cols] for a, row, _, _ in pieces],
            axis=axis,
        )

    def prepare(slot, job, c):
        _, first, _, _, pieces = jobs[job]
        d = first + c
        origin = lax.rem(x - d + heads, heads)
        q_chunk = tok * heads + origin
        q_pos = q_chunk * rows + lane
        outside = jnp.where((q_pos >= query_begin) & (q_pos < query_end), 0.0, HIDE)
        f_scr[slot] = jnp.concatenate([outside.astype(jnp.bfloat16)] * group, axis=1)
        for i, (a, row, kind, kd) in enumerate(pieces):
            k_chunk = shard_of(kind, tok) * heads + lax.rem(x - kd + heads, heads)
            k_pos = jnp.where(k_chunk <= q_chunk, k_chunk * rows + sub, -1)
            inside = (k_pos >= key_begin) & (k_pos < key_end)
            e_scr[slot, i * rows : (i + 1) * rows, :] = jnp.where(inside, 1.0, 0.0).astype(
                jnp.bfloat16
            )
        return origin

    def scores(buf, slot, job, c, g):
        q, first, _, s, pieces = jobs[job]
        d = first + c
        n = len(pieces)
        query = jnp.concatenate(
            [q_refs[q][at((c * ql + g * group + r) * D), :] for r in range(group)], axis=1
        )
        query = jnp.concatenate([query, f_scr[slot]], axis=0)
        keys = jnp.concatenate([key_block(pieces, g, 0, 0), e_scr[slot, : n * rows, :]], axis=1)
        score = jnp.dot(keys, query, preferred_element_type=jnp.float32)
        if s is None:
            top = jnp.full((8, wide), FLOOR, jnp.float32)
        else:
            top = jnp.broadcast_to(states[3 * s][c, g], (8, wide))
        for i, (a, row, kind, kd) in enumerate(pieces):
            block = score[i * rows : (i + 1) * rows]
            if kind == "own" and (not isinstance(d, int) or kd == d):
                late = jnp.where((sub > lane) & (kd == d), HIDE, 0.0)
                block = block + jnp.concatenate([late] * group, axis=1)
            s_scr[buf, i * rows : (i + 1) * rows, :] = block
            top = jnp.maximum(top, jnp.max(block.reshape(rows // 8, 8, wide), axis=0))
        return jnp.max(top, axis=0, keepdims=True)

    def weigh(buf, job, top):
        part = jnp.zeros((8, wide), jnp.float32)
        for i in range(len(jobs[job][4])):
            expo = jnp.exp2((s_scr[buf, i * rows : (i + 1) * rows, :] - top) * SCALE)
            part = part + jnp.sum(expo.reshape(rows // 8, 8, wide), axis=0)
            p_scr[buf, i * rows : (i + 1) * rows, :] = expo.astype(jnp.bfloat16)
        return jnp.sum(part, axis=0, keepdims=True)

    def mix(buf, job, c, g, origin, top, total):
        _, _, _, s, pieces = jobs[job]
        acc = jnp.dot(
            key_block(pieces, g, 1, 1),
            p_scr[buf, : len(pieces) * rows, :],
            preferred_element_type=jnp.float32,
        )
        if s is not None:
            fade = jnp.exp2((states[3 * s][c, g] - top) * SCALE)
            total = total + states[3 * s + 1][c, g] * fade
            acc = acc + states[3 * s + 2][c, g] * fade
        if last:
            acc = (acc * (1.0 / total)).astype(jnp.bfloat16)
            for r in range(group):
                outs[0][at(origin * rows), (g * group + r) * D : (g * group + r + 1) * D] = acc[
                    :, r * rows : (r + 1) * rows
                ].T
        else:
            outs[3 * job][c, g] = top
            outs[3 * job + 1][c, g] = total
            outs[3 * job + 2][c, g] = acc

    def sweep(chunks):
        origins = [prepare(slot, job, c) for slot, (job, c) in enumerate(chunks)]
        units = [(slot, g) for slot in range(len(chunks)) for g in range(kvl)]
        tops, totals = {}, {}
        for i in range(len(units) + 2):
            if i < len(units):
                slot, g = units[i]
                tops[i] = scores(i % bufs, slot, *chunks[slot], g)
            if 0 <= i - 1 < len(units):
                slot, g = units[i - 1]
                totals[i - 1] = weigh((i - 1) % bufs, chunks[slot][0], tops[i - 1])
            if 0 <= i - 2 < len(units):
                slot, g = units[i - 2]
                job, c = chunks[slot]
                mix((i - 2) % bufs, job, c, g, origins[slot], tops[i - 2], totals[i - 2])

    if last:
        slots, own_s, head_ref, _ = earlier
        first_page = (slots, own_s, kv_refs[0], head_ref, outs[1], *page)
        send = partial_page(heads, segs, lengths, *first_page)
    if max(job[2] for job in jobs) == 1:
        sweep([(job, 0) for job in range(len(jobs))])
    else:
        for job in range(len(jobs)):
            def body(c, carry, job=job):
                sweep([(job, c)])
                return carry

            lax.fori_loop(0, jobs[job][2], body, 0)
    if last:
        send()


def partial_page(heads, segs, lengths, slots, own_s, rest_s, head_ref, pool_ref, page, sem):
    x = lax.axis_index("head")
    tok = lax.axis_index("tok")
    core = lax.rem(tok, 2)
    base = tok * heads * D
    first = jnp.int32(0)
    end = jnp.int32(0)
    for s in range(segs):
        end = end + lengths[s]
        first = jnp.where(end <= base, end, first)
    before = lax.rem(base - first, PAGE)
    kvl = head_ref.shape[1]
    d = lax.rem(x + 1, heads)
    lane = lax.broadcasted_iota(jnp.int32, (PAGE, PAGE), 1)
    sub = lax.broadcasted_iota(jnp.int32, (PAGE, PAGE), 0)
    move = jnp.where((lane == sub + PAGE - before) & (sub < before), 1.0, 0.0).astype(jnp.bfloat16)
    copy = pltpu.make_async_copy(page, pool_ref.at[slots[0, 0]], sem)

    def write(ref, row):
        moved = []
        for g in range(kvl):
            at_row = pl.ds(pl.multiple_of(row + D - PAGE, PAGE), PAGE)
            key = ref[at_row, 2 * g * D : (2 * g + 1) * D]
            value = ref[at(row), (2 * g + 1) * D : (2 * g + 2) * D].T[D - PAGE :]
            both = jnp.concatenate([key, value], axis=1)
            moved.append(jnp.dot(move, both, preferred_element_type=jnp.float32))
        moved = jnp.stack(moved, axis=1)
        index = lax.broadcasted_iota(jnp.int32, moved.shape, 0)
        page[...] = jnp.where(index < before, moved, head_ref[...].astype(jnp.float32)).astype(
            jnp.bfloat16
        )
        copy.start()

    @pl.when((before > 0) & (d == 0))
    def _():
        write(own_s, (1 - core) * D)

    @pl.when((before > 0) & (d > 0))
    def _():
        write(rest_s, jnp.maximum(d - 1, 0) * D + (1 - core) * (heads - 1) * D)

    def finish():
        @pl.when(before > 0)
        def _():
            copy.wait()

    return finish


def attend(lengths, qs, kvs, jobs, last, heads, *earlier):
    kvl = kvs[0].shape[1] // (2 * D)
    states, plan = [], []
    for q, first, state, pieces in jobs:
        many = 1 if first == 0 else heads - 1
        plan.append((q, first, many, None if state is None else len(states), tuple(pieces)))
        if state is not None:
            states.append(state)
    ql = qs[plan[0][0]].shape[0] // D // plan[0][2]
    wide = ql // kvl * D
    if last:
        pool = earlier[3]
        out_shape = [jax.ShapeDtypeStruct((heads * D, ql * D), jnp.bfloat16)]
        out_shape += [jax.ShapeDtypeStruct(pool.shape, pool.dtype)]
    else:
        out_shape = []
        for _, _, many, _, _ in plan:
            row = jax.ShapeDtypeStruct((many, kvl, 1, wide), jnp.float32)
            out_shape += [row, row, jax.ShapeDtypeStruct((many, kvl, D, wide), jnp.float32)]
    inputs = [lengths, *qs, *kvs, *[part for state in states for part in state], *earlier]
    more = [SMEM, VMEM, VMEM, ANY] if last else [ANY] * len(earlier)
    keys = max(len(job[4]) for job in plan) * D
    together = len(plan) if heads == 2 else 1
    bufs = min(3, kvl * together)
    result = pl.pallas_call(
        functools.partial(
            attend_body, heads, lengths.shape[0], tuple(plan), last,
            (len(qs), len(kvs), len(states), len(earlier)),
        ),
        out_shape=out_shape,
        in_specs=[SMEM] + [VMEM] * (len(inputs) - 1 - len(earlier)) + more,
        out_specs=[VMEM, ANY] if last else [VMEM] * len(out_shape),
        input_output_aliases={len(inputs) - 1: 1} if last else {},
        scratch_shapes=[
            pltpu.VMEM((bufs, keys, wide), jnp.float32),
            pltpu.VMEM((bufs, keys, wide), jnp.bfloat16),
            pltpu.VMEM((together, keys, D), jnp.bfloat16),
            pltpu.VMEM((together, D, wide), jnp.bfloat16),
        ]
        + ([pltpu.VMEM(pool.shape[1:], pool.dtype), pltpu.SemaphoreType.DMA] if last else []),
        compiler_params=params(),
        cost_estimate=cost(0.01),
        name="attend_last" if last else "attend_part",
    )(*inputs)
    return result if last else [result[i : i + 3] for i in range(0, len(result), 3)]


def pages_body(heads, segs, pool, lengths, slots, own_ref, rest_ref, out_ref, head_ref, hot, ends):
    rows = D
    shard_rows = heads * rows
    x = lax.axis_index("head")
    base = lax.axis_index("tok") * shard_rows
    end = jnp.int32(0)
    for s in range(segs):
        end = end + lengths[s]
        ends[s] = end
    hot[...] = jnp.zeros_like(hot)
    width = hot.shape[1]
    lane = lax.broadcasted_iota(jnp.int32, (PAGE, width), 1)
    sub = lax.broadcasted_iota(jnp.int32, (PAGE, width), 0)

    def finish_of(a):
        found = jnp.int32(0)
        for s in reversed(range(segs)):
            found = jnp.where(ends[s] > a, ends[s], found)
        return found

    first = jnp.int32(0)
    for s in range(segs):
        first = jnp.where(ends[s] <= base, ends[s], first)
    page = first + ((base - first) // PAGE) * PAGE

    def one_page(rank, a):
        stop = jnp.minimum(a + PAGE, finish_of(a))
        owned = (stop > base) & (stop <= base + shard_rows)

        @pl.when(owned)
        def _():
            token = sub + (a - base)
            piece = token // rows
            d = lax.rem(x - piece + 2 * heads, heads)
            column = jnp.where(token < 0, -1, (d - piece) * rows + token)
            mark = (lane == column) & (sub < stop - a)
            slot = slots[0, rank]
            hot[pl.ds(pl.multiple_of(slot * PAGE, PAGE), PAGE), :] = mark.astype(hot.dtype)

        return jnp.where(owned, stop, a)

    lax.fori_loop(0, pool, one_page, page)
    mark = hot[...].astype(jnp.bfloat16)
    kvl = own_ref.shape[1] // (2 * D)
    moved = []
    for g in range(kvl):
        key_at, value_at = at(2 * g * D), at((2 * g + 1) * D)
        others = [rest_ref[i * D : (i + 1) * D, value_at].T for i in range(heads - 1)]
        key = jnp.concatenate([own_ref[:, key_at], rest_ref[:, key_at]], axis=0)
        value = jnp.concatenate([own_ref[:, value_at].T, *others], axis=0)
        both = jnp.concatenate([key, value], axis=1)
        moved.append(jnp.dot(mark, both, preferred_element_type=jnp.float32))
    out_ref[...] = jnp.stack(moved, axis=1).astype(jnp.bfloat16).reshape(out_ref.shape)
    head_ref[...] = out_ref[slots[0, 0]]


def pages(lengths, slots, own, rest, heads):
    pool = slots.shape[1]
    kvl = own.shape[1] // (2 * D)
    return pl.pallas_call(
        functools.partial(pages_body, heads, lengths.shape[0], pool),
        out_shape=[
            jax.ShapeDtypeStruct((pool, PAGE, kvl, 2 * D), jnp.bfloat16),
            jax.ShapeDtypeStruct((PAGE, kvl, 2 * D), jnp.bfloat16),
        ],
        in_specs=[SMEM, SMEM, VMEM, VMEM],
        out_specs=[VMEM, VMEM],
        scratch_shapes=[
            pltpu.VMEM((pool * PAGE, heads * D), jnp.float32),
            pltpu.SMEM((lengths.shape[0],), jnp.int32),
        ],
        compiler_params=params(),
        cost_estimate=cost(0.01),
        name="pages",
    )(lengths, slots, own, rest)


def pick_body(bit, plan, *refs):
    *ins, out = refs
    side = lax.rem(lax.axis_index("tok") // bit, 2)
    row = 0
    for part in plan:
        rows = ins[part[0]].shape[0]
        to = pl.ds(row, rows)
        if len(part) == 1:
            out[to, :] = ins[part[0]][...]
        else:
            for value, index in enumerate(part):
                @pl.when(side == value)
                def _(index=index, to=to):
                    out[to, :] = ins[index][...]
        row += rows


def pick(bit, plan, *arrays):
    rows = sum(arrays[part[0]].shape[0] for part in plan)
    last = max(max(part) for part in plan)
    return pl.pallas_call(
        functools.partial(pick_body, bit, plan),
        out_shape=jax.ShapeDtypeStruct((rows, arrays[0].shape[1]), jnp.bfloat16),
        in_specs=[ANY if i > last else VMEM for i in range(len(arrays))],
        out_specs=VMEM,
        compiler_params=params(8),
        cost_estimate=cost(0.01),
        name="pick",
    )(*arrays)


def after_body(*refs):
    del refs


def after(x, *earlier):
    return pl.pallas_call(
        after_body,
        out_shape=jax.ShapeDtypeStruct(x.shape, x.dtype),
        in_specs=[ANY] * (1 + len(earlier)),
        out_specs=ANY,
        input_output_aliases={0: 0},
        compiler_params=params(1),
        cost_estimate=cost(0.01),
        name="after",
    )(x, *earlier)


def on_device(queries, key_states, value_states, query_gain, key_gain, lengths, slot_order):
    heads = lax.axis_size("head")
    others = range(1, heads)

    cosine, sine, own, *away = kv_prep(
        lengths, key_states, value_states, key_gain.reshape(1, D), heads
    )
    rest = join([around(part, "head", d) for d, part in enumerate(away, 1)])
    own4 = around(own, "tok", 4)
    q_own, *q_away, turned = q_prep(queries, query_gain.reshape(1, D), cosine, sine, heads)
    q_rest = join([around(part, "head", d) for d, part in enumerate(q_away, 1)])
    qs = [q_own, q_rest]
    rest = after(rest, turned)
    rest4, rest2 = around(rest, "tok", 4), around(rest, "tok", 2)
    own4 = after(own4, rest)
    near = pick(2, ((0, 1),), own, own4)
    own2 = swap(near, 2)

    base = [(0, 0, "own", 0)] + [(1, d - 1, "own", d) for d in others]
    [own_state] = attend(
        lengths, [q_own], [own, rest], [(0, 0, None, base)], False, heads, near
    )
    page_pool, head_page = pages(lengths, slot_order, own, rest, heads)
    own_mixed = pick(1, ((0, 1), (2,)), own, own4, own2, own_state[0], head_page)
    own_s = swap(own_mixed, 1)

    qs = [q_own, q_rest]
    pieces = [(2, 0, "far", 0), (3, 0, "near", 0)]
    own_state, rest_state = attend(
        lengths, qs, [own, rest, own4, own2],
        [(0, 0, own_state, pieces), (1, 1, None, base + pieces)], False, heads, own_mixed,
    )

    rest_mixed = pick(1, ((0, 1), (2,)), rest, rest4, rest2, own_state[0])
    rest_s = swap(rest_mixed, 1)
    pieces = [(0, 0, "mix_swap", 0), (0, 1, "near_swap", 0)]
    pieces += [(1, d - 1, "far", d) for d in others]
    pieces += [(2, d - 1, "near", d) for d in others]
    own_state, rest_state = attend(
        lengths, qs, [own_s, rest4, rest2],
        [(0, 0, own_state, pieces), (1, 1, rest_state, pieces)], False, heads, rest_mixed,
    )
    pieces = [(0, d - 1, "mix_swap", d) for d in others]
    pieces += [(0, heads + d - 2, "near_swap", d) for d in others]
    attention, page_pool = attend(
        lengths, qs, [rest_s],
        [(0, 0, own_state, pieces), (1, 1, rest_state, pieces)], True, heads,
        slot_order, own_s, head_page, page_pool,
    )
    return (attention, page_pool)


def solution(mesh):
    in_specs = (
        P(("tok", "head"), None),
        P(("tok", "head"), None),
        P(("tok", "head"), None),
        P(),
        P(),
        P(),
        P("tok", None),
    )
    out_specs = (P("tok", "head"), P("tok", None, "head", None))
    return jax.shard_map(
        on_device, mesh=mesh, in_specs=in_specs, out_specs=out_specs, check_vma=False
    )
```

```python
import functools
import math

import jax
import jax.numpy as jnp
from jax import lax
from jax.experimental import pallas as pl
from jax.experimental.pallas import tpu as pltpu
from jax.sharding import PartitionSpec as P

D = 128
PAGE = 16
HIDE = -2e30
FLOOR = -1e30
MIB = 1024 * 1024
SCALE = math.log2(math.e) / math.sqrt(D)

VMEM = pl.BlockSpec(memory_space=pltpu.VMEM)
SMEM = pl.BlockSpec(memory_space=pltpu.SMEM)
TOKEN = jax.ShapeDtypeStruct((8, D), jnp.float32)
ANY = pl.BlockSpec(memory_space=pl.ANY)
HBM = pl.BlockSpec(memory_space=pltpu.HBM)


def cost(us):
    return pl.CostEstimate(flops=int(us * 1.15e9), bytes_accessed=0, transcendentals=0)


def params(mib=32):
    return pltpu.CompilerParams(vmem_limit_bytes=mib * MIB)


def around(x, axis, by):
    peers = lax.axis_size(axis)
    return lax.ppermute(x, axis, [(i, (i + by) % peers) for i in range(peers)])


def onward(x, axis, by):
    peers = lax.axis_size(axis)
    return lax.ppermute(x, axis, [(i, i + by) for i in range(peers - by)])


def swap(x, bit):
    peers = lax.axis_size("tok")
    return lax.ppermute(x, "tok", [(i, i ^ bit) for i in range(peers)])


def join(parts):
    return parts[0] if len(parts) == 1 else jnp.concatenate(parts, axis=0)


def at(index):
    return pl.ds(index, D) if isinstance(index, int) else pl.ds(pl.multiple_of(index, D), D)


def seg_first(pos, lengths, segs):
    first = jnp.zeros_like(pos)
    start = jnp.int32(0)
    for s in range(segs):
        first = jnp.where(pos >= start, start, first)
        start = start + lengths[s]
    return first


def seg_bounds(shape, axis, lengths, segs):
    index = lax.broadcasted_iota(jnp.int32, shape, axis)
    begin = jnp.where(index == segs, -(2**30), 2**30)
    end = jnp.zeros(shape, jnp.int32)
    here = jnp.int32(0)
    for s in range(segs):
        begin = jnp.where(index == s, here, begin)
        here = here + lengths[s]
        end = jnp.where(index == s, here, end)
    return begin, end


def rotate(x, cos_gain, sin_gain):
    power = jnp.mean(x * x, axis=0, keepdims=True)
    half = D // 2
    turned = jnp.concatenate([x[half:], x[:half]], axis=0)
    return (x * cos_gain + turned * sin_gain) * lax.rsqrt(power + 1e-06)


def gain_tables(cosine, sine, gain_row):
    gain = jnp.broadcast_to(gain_row, (D, D)).T
    half = D // 2
    turned = jnp.concatenate([gain[half:], gain[:half]], axis=0)
    cos_gain = jnp.concatenate([cosine, cosine], axis=0) * gain
    sin_gain = jnp.concatenate([-sine, sine], axis=0) * turned
    return cos_gain, sin_gain


def kv_prep_body(heads, segs, lengths_in, k_in, v_in, gain_in, table_ref, *refs):
    outs, (lengths, k_ref, v_ref, gain_ref, sems) = refs[:heads], refs[heads:]
    pairs = [(lengths_in, lengths), (gain_in, gain_ref), (k_in, k_ref), (v_in, v_ref)]
    copies = [pltpu.make_async_copy(a, b, sems.at[i]) for i, (a, b) in enumerate(pairs)]
    for copy in copies:
        copy.start()
    rows = k_ref.shape[0]
    kvl = k_ref.shape[1] // D // heads
    x = lax.axis_index("head")
    base = (lax.axis_index("tok") * heads + x) * rows
    half = D // 2
    pos = base + lax.broadcasted_iota(jnp.int32, (half, rows), 1)
    step = lax.broadcasted_iota(jnp.int32, (half, rows), 0).astype(jnp.float32)
    frequency = jnp.exp(step * (-2.0 * math.log(1000000.0) / D))
    copies[0].wait()
    offset = (pos - seg_first(pos, lengths, segs)).astype(jnp.float32)
    angles = offset * frequency
    cosine, sine = jnp.cos(angles), jnp.sin(angles)
    table_ref[:half] = cosine
    table_ref[half:] = sine
    copies[1].wait()
    cos_gain, sin_gain = gain_tables(cosine, sine, gain_ref[...])
    copies[2].wait()
    copies[3].wait()
    for d in reversed(range(heads)):
        peer = lax.rem(x + d, heads)
        for j in range(kvl):
            head = peer * kvl + j
            key = k_ref[:, at(head * D)].astype(jnp.float32).T
            key = rotate(key, cos_gain, sin_gain).T
            outs[d][:, 2 * j * D : (2 * j + 1) * D] = key.astype(jnp.bfloat16)
            value = v_ref[:, at(head * D)]
            outs[d][:, (2 * j + 1) * D : (2 * j + 2) * D] = value.T


def kv_prep(lengths, keys, values, gain, heads):
    rows, width = keys.shape
    table = jax.ShapeDtypeStruct((D, rows), jnp.float32)
    part = jax.ShapeDtypeStruct((rows, 2 * width // heads), jnp.bfloat16)
    return pl.pallas_call(
        functools.partial(kv_prep_body, heads, lengths.shape[0]),
        out_shape=[table] + [part] * heads,
        in_specs=[HBM] * 4,
        out_specs=[VMEM] * (1 + heads),
        scratch_shapes=[
            pltpu.SMEM(lengths.shape, jnp.int32),
            pltpu.VMEM(keys.shape, jnp.bfloat16),
            pltpu.VMEM(values.shape, jnp.bfloat16),
            pltpu.VMEM(gain.shape, jnp.float32),
            pltpu.SemaphoreType.DMA((4,)),
        ],
        compiler_params=params(62),
        cost_estimate=cost(0.01),
        name="kv_prep",
    )(lengths, keys, values, gain)


def q_prep_body(heads, q_ref, gain_ref, table_ref, *refs):
    *outs, token = refs
    token[...] = jnp.zeros_like(token)
    ql = q_ref.shape[1] // D // heads
    x = lax.axis_index("head")
    half = D // 2
    cos_gain, sin_gain = gain_tables(table_ref[:half], table_ref[half:], gain_ref[...])
    for d in reversed(range(heads)):
        peer = lax.rem(x + d, heads)
        for j in range(ql):
            query = q_ref[:, at((peer * ql + j) * D)].astype(jnp.float32).T
            outs[d][j * D : (j + 1) * D, :] = rotate(query, cos_gain, sin_gain).astype(
                jnp.bfloat16
            )


def q_prep(queries, gain, table, heads):
    rows, width = queries.shape
    part = jax.ShapeDtypeStruct((width // heads, rows), jnp.bfloat16)
    return pl.pallas_call(
        functools.partial(q_prep_body, heads),
        out_shape=[part] * heads + [TOKEN],
        in_specs=[VMEM] * 3,
        out_specs=[VMEM] * (heads + 1),
        compiler_params=params(),
        cost_estimate=cost(0.01),
        name="q_prep",
    )(queries, gain, table)


def shard_of(kind, tok):
    core = lax.rem(tok, 2)
    if kind == "own":
        return tok
    if kind == "far":
        return tok - 4
    if kind == "near":
        return tok - 2
    if kind == "near_swap":
        return tok - 1 - 2 * core
    return jnp.where(core == 0, tok - 3, tok - 1)


def attend_body(heads, segs, jobs, last, counts, lengths, *refs):
    n_q, n_kv, n_state, n_earlier = counts
    q_refs, refs = refs[:n_q], refs[n_q:]
    kv_refs, refs = refs[:n_kv], refs[n_kv:]
    states, refs = refs[: 3 * n_state], refs[3 * n_state :]
    earlier, refs = refs[:n_earlier], refs[n_earlier:]
    n_out = 2 if last else 3 * len(jobs)
    outs, (s_scr, p_scr, e_scr, f_scr, *page) = refs[:n_out], refs[n_out:]
    if last:
        out_scr, out_sems, *page = page
    bufs = s_scr.shape[0]
    x = lax.axis_index("head")
    tok = lax.axis_index("tok")
    rows = D
    kvl = kv_refs[0].shape[1] // (2 * D)
    ql = f_scr.shape[2] // D * kvl
    group = ql // kvl
    wide = group * rows
    lane = lax.broadcasted_iota(jnp.int32, (rows, rows), 1)
    sub = lax.broadcasted_iota(jnp.int32, (rows, rows), 0)
    key_begin, key_end = seg_bounds((1, D), 1, lengths, segs)
    used = (segs + 16) // 16 * 16
    query_begin, query_end = seg_bounds((used, D), 0, lengths, segs)

    def key_block(pieces, g, side, axis):
        cols = at((2 * g + side) * D)
        return jnp.concatenate(
            [kv_refs[a][row * rows : (row + 1) * rows, cols] for a, row, _, _ in pieces],
            axis=axis,
        )

    def out_part(origin, g):
        part = at(origin * rows), pl.ds(g * group * D, group * D)
        sem = out_sems.at[origin, g]
        return pltpu.make_async_copy(out_scr.at[part], outs[0].at[part], sem)

    def prepare(slot, job, c, known):
        _, first, _, _, pieces = jobs[job]
        d = first + c
        origin = lax.rem(x - d + heads, heads)
        q_chunk = tok * heads + origin
        q_pos = q_chunk * rows + lane[:used]
        outside = jnp.where((q_pos >= query_begin) & (q_pos < query_end), 0.0, HIDE)
        outside = jnp.concatenate([outside, jnp.zeros((D - used, D), jnp.float32)], axis=0)
        f_scr[slot] = jnp.concatenate([outside.astype(jnp.bfloat16)] * group, axis=1)
        for i, (a, row, kind, kd) in enumerate(pieces):
            if kind != "own" and (a, row, kind, kd) in known:
                from_slot, j = known[a, row, kind, kd]
                e_scr[slot, i * rows : (i + 1) * rows, :] = e_scr[
                    from_slot, j * rows : (j + 1) * rows, :
                ]
                continue
            known[a, row, kind, kd] = (slot, i)
            k_chunk = shard_of(kind, tok) * heads + lax.rem(x - kd + heads, heads)
            k_pos = jnp.where(k_chunk <= q_chunk, k_chunk * rows + sub, -1)
            inside = (k_pos >= key_begin) & (k_pos < key_end)
            e_scr[slot, i * rows : (i + 1) * rows, :] = jnp.where(inside, 1.0, 0.0).astype(
                jnp.bfloat16
            )
        return origin

    def scores(buf, slot, job, c, g):
        q, first, _, s, pieces = jobs[job]
        d = first + c
        n = len(pieces)
        query = jnp.concatenate(
            [q_refs[q][at((c * ql + g * group + r) * D), :] for r in range(group)], axis=1
        )
        query = jnp.concatenate([query, f_scr[slot]], axis=0)
        keys = jnp.concatenate([key_block(pieces, g, 0, 0), e_scr[slot, : n * rows, :]], axis=1)
        score = jnp.dot(keys, query, preferred_element_type=jnp.float32)
        if s is None:
            top = jnp.full((8, wide), FLOOR, jnp.float32)
        else:
            top = jnp.broadcast_to(states[3 * s][c, g], (8, wide))
        for i, (a, row, kind, kd) in enumerate(pieces):
            block = score[i * rows : (i + 1) * rows]
            if kind == "own" and (not isinstance(d, int) or kd == d):
                late = jnp.where((sub > lane) & (kd == d), HIDE, 0.0)
                block = block + jnp.concatenate([late] * group, axis=1)
            s_scr[buf, i * rows : (i + 1) * rows, :] = block
            top = jnp.maximum(top, jnp.max(block.reshape(rows // 8, 8, wide), axis=0))
        return jnp.max(top, axis=0, keepdims=True)

    def weigh(buf, job, top):
        part = jnp.zeros((8, wide), jnp.float32)
        for i in range(len(jobs[job][4])):
            expo = jnp.exp2((s_scr[buf, i * rows : (i + 1) * rows, :] - top) * SCALE)
            part = part + jnp.sum(expo.reshape(rows // 8, 8, wide), axis=0)
            p_scr[buf, i * rows : (i + 1) * rows, :] = expo.astype(jnp.bfloat16)
        return jnp.sum(part, axis=0, keepdims=True)

    def mix(buf, job, c, g, origin, top, total):
        _, _, _, s, pieces = jobs[job]
        acc = jnp.dot(
            key_block(pieces, g, 1, 1),
            p_scr[buf, : len(pieces) * rows, :],
            preferred_element_type=jnp.float32,
        )
        if s is not None:
            fade = jnp.exp2((states[3 * s][c, g] - top) * SCALE)
            total = total + states[3 * s + 1][c, g] * fade
            acc = acc + states[3 * s + 2][c, g] * fade
        if last:
            acc = (acc * (1.0 / total)).astype(jnp.bfloat16)
            for r in range(group):
                out_scr[at(origin * rows), (g * group + r) * D : (g * group + r + 1) * D] = acc[
                    :, r * rows : (r + 1) * rows
                ].T
            part = out_part(origin, g)
            part.start()
        else:
            outs[3 * job][c, g] = top
            outs[3 * job + 1][c, g] = total
            outs[3 * job + 2][c, g] = acc

    def sweep(chunks):
        known = {}
        origins = [prepare(slot, job, c, known) for slot, (job, c) in enumerate(chunks)]
        units = [(slot, g) for slot in range(len(chunks)) for g in range(kvl)]
        tops, totals = {}, {}
        for i in range(len(units) + 2):
            if i < len(units):
                slot, g = units[i]
                tops[i] = scores(i % bufs, slot, *chunks[slot], g)
            if 0 <= i - 1 < len(units):
                slot, g = units[i - 1]
                totals[i - 1] = weigh((i - 1) % bufs, chunks[slot][0], tops[i - 1])
            if 0 <= i - 2 < len(units):
                slot, g = units[i - 2]
                job, c = chunks[slot]
                mix((i - 2) % bufs, job, c, g, origins[slot], tops[i - 2], totals[i - 2])

    if last:
        slots, own_s, head_ref, _ = earlier
        first_page = (slots, own_s, kv_refs[0], head_ref, outs[1], *page)
        send = partial_page(heads, segs, lengths, *first_page)
    if max(job[2] for job in jobs) == 1:
        sweep([(job, 0) for job in range(len(jobs))])
    else:
        for job in range(len(jobs)):
            def body(c, carry, job=job):
                sweep([(job, c)])
                return carry

            lax.fori_loop(0, jobs[job][2], body, 0)
    if last:
        for origin in range(heads):
            for g in range(kvl):
                out_part(origin, g).wait()
        send()


def partial_page(heads, segs, lengths, slots, own_s, rest_s, head_ref, pool_ref, page, sem):
    x = lax.axis_index("head")
    tok = lax.axis_index("tok")
    core = lax.rem(tok, 2)
    base = tok * heads * D
    first = jnp.int32(0)
    end = jnp.int32(0)
    for s in range(segs):
        end = end + lengths[s]
        first = jnp.where(end <= base, end, first)
    before = lax.rem(base - first, PAGE)
    kvl = head_ref.shape[1]
    d = lax.rem(x + 1, heads)
    lane = lax.broadcasted_iota(jnp.int32, (PAGE, PAGE), 1)
    sub = lax.broadcasted_iota(jnp.int32, (PAGE, PAGE), 0)
    move = jnp.where((lane == sub + PAGE - before) & (sub < before), 1.0, 0.0).astype(jnp.bfloat16)
    copy = pltpu.make_async_copy(page, pool_ref.at[slots[0, 0]], sem)

    def write(ref, row):
        moved = []
        for g in range(kvl):
            at_row = pl.ds(pl.multiple_of(row + D - PAGE, PAGE), PAGE)
            key = ref[at_row, 2 * g * D : (2 * g + 1) * D]
            value = ref[at(row), (2 * g + 1) * D : (2 * g + 2) * D].T[D - PAGE :]
            both = jnp.concatenate([key, value], axis=1)
            moved.append(jnp.dot(move, both, preferred_element_type=jnp.float32))
        moved = jnp.stack(moved, axis=1)
        index = lax.broadcasted_iota(jnp.int32, moved.shape, 0)
        page[...] = jnp.where(index < before, moved, head_ref[...].astype(jnp.float32)).astype(
            jnp.bfloat16
        )
        copy.start()

    @pl.when((before > 0) & (d == 0))
    def _():
        write(own_s, (1 - core) * D)

    @pl.when((before > 0) & (d > 0))
    def _():
        write(rest_s, jnp.maximum(d - 1, 0) * D + (1 - core) * (heads - 1) * D)

    def finish():
        @pl.when(before > 0)
        def _():
            copy.wait()

    return finish


def attend(lengths, qs, kvs, jobs, last, heads, *earlier):
    kvl = kvs[0].shape[1] // (2 * D)
    states, plan = [], []
    for q, first, state, pieces in jobs:
        many = 1 if first == 0 else heads - 1
        plan.append((q, first, many, None if state is None else len(states), tuple(pieces)))
        if state is not None:
            states.append(state)
    ql = qs[plan[0][0]].shape[0] // D // plan[0][2]
    wide = ql // kvl * D
    if last:
        pool = earlier[3]
        out_shape = [jax.ShapeDtypeStruct((heads * D, ql * D), jnp.bfloat16)]
        out_shape += [jax.ShapeDtypeStruct(pool.shape, pool.dtype)]
    else:
        out_shape = []
        for _, _, many, _, _ in plan:
            row = jax.ShapeDtypeStruct((many, kvl, 1, wide), jnp.float32)
            out_shape += [row, row, jax.ShapeDtypeStruct((many, kvl, D, wide), jnp.float32)]
    inputs = [lengths, *qs, *kvs, *[part for state in states for part in state], *earlier]
    more = [SMEM, VMEM, VMEM, ANY] if last else [ANY] * len(earlier)
    keys = max(len(job[4]) for job in plan) * D
    together = len(plan) if heads == 2 else 1
    bufs = min(3, kvl * together)
    result = pl.pallas_call(
        functools.partial(
            attend_body, heads, lengths.shape[0], tuple(plan), last,
            (len(qs), len(kvs), len(states), len(earlier)),
        ),
        out_shape=out_shape,
        in_specs=[SMEM] + [VMEM] * (len(inputs) - 1 - len(earlier)) + more,
        out_specs=[ANY, ANY] if last else [VMEM] * len(out_shape),
        input_output_aliases={len(inputs) - 1: 1} if last else {},
        scratch_shapes=[
            pltpu.VMEM((bufs, keys, wide), jnp.float32),
            pltpu.VMEM((bufs, keys, wide), jnp.bfloat16),
            pltpu.VMEM((together, keys, D), jnp.bfloat16),
            pltpu.VMEM((together, D, wide), jnp.bfloat16),
        ]
        + (
            [
                pltpu.VMEM(out_shape[0].shape, jnp.bfloat16),
                pltpu.SemaphoreType.DMA((heads, kvl)),
                pltpu.VMEM(pool.shape[1:], pool.dtype),
                pltpu.SemaphoreType.DMA,
            ]
            if last
            else []
        ),
        compiler_params=params(),
        cost_estimate=cost(0.01),
        name="attend_last" if last else "attend_part",
    )(*inputs)
    return result if last else [result[i : i + 3] for i in range(0, len(result), 3)]


def pages_body(
    heads, segs, pool, lengths, slots, own_ref, rest_ref, pool_ref, head_ref, hot, ends,
    wide_scr, out_scr, sems,
):
    rows = D
    shard_rows = heads * rows
    x = lax.axis_index("head")
    base = lax.axis_index("tok") * shard_rows
    end = jnp.int32(0)
    for s in range(segs):
        end = end + lengths[s]
        ends[s] = end
    hot[...] = jnp.zeros_like(hot)
    width = hot.shape[1]
    lane = lax.broadcasted_iota(jnp.int32, (PAGE, width), 1)
    sub = lax.broadcasted_iota(jnp.int32, (PAGE, width), 0)

    def finish_of(a):
        found = jnp.int32(0)
        for s in reversed(range(segs)):
            found = jnp.where(ends[s] > a, ends[s], found)
        return found

    first = jnp.int32(0)
    for s in range(segs):
        first = jnp.where(ends[s] <= base, ends[s], first)
    page = first + ((base - first) // PAGE) * PAGE

    def one_page(rank, a):
        stop = jnp.minimum(a + PAGE, finish_of(a))
        owned = (stop > base) & (stop <= base + shard_rows)

        @pl.when(owned)
        def _():
            token = sub + (a - base)
            piece = token // rows
            d = lax.rem(x - piece + 2 * heads, heads)
            column = jnp.where(token < 0, -1, (d - piece) * rows + token)
            mark = (lane == column) & (sub < stop - a)
            slot = slots[0, rank]
            hot[pl.ds(pl.multiple_of(slot * PAGE, PAGE), PAGE), :] = mark.astype(hot.dtype)

        return jnp.where(owned, stop, a)

    lax.fori_loop(0, pool, one_page, page)
    kvl = own_ref.shape[1] // (2 * D)
    both = []
    for g in range(kvl):
        key_at, value_at = at(2 * g * D), at((2 * g + 1) * D)
        others = [rest_ref[i * D : (i + 1) * D, value_at].T for i in range(heads - 1)]
        key = jnp.concatenate([own_ref[:, key_at], rest_ref[:, key_at]], axis=0)
        value = jnp.concatenate([own_ref[:, value_at].T, *others], axis=0)
        both.append(jnp.concatenate([key, value], axis=1))
    step = 8
    copies = []
    for i, page in enumerate(range(0, pool, step)):
        mark = hot[page * PAGE : (page + step) * PAGE, :].astype(jnp.bfloat16)
        for g in range(kvl):
            wide_scr[i % 2, :, g, :] = jnp.dot(mark, both[g], preferred_element_type=jnp.float32)
        block = pl.ds(page, step)
        out_scr[block] = (
            wide_scr[i % 2].astype(jnp.bfloat16).reshape(step, PAGE, kvl, 2 * D)
        )
        copies.append(pltpu.make_async_copy(out_scr.at[block], pool_ref.at[block], sems.at[i]))
        copies[-1].start()
    head_ref[...] = out_scr[slots[0, 0]]
    for copy in copies:
        copy.wait()


def pages(lengths, slots, own, rest, heads):
    pool = slots.shape[1]
    kvl = own.shape[1] // (2 * D)
    return pl.pallas_call(
        functools.partial(pages_body, heads, lengths.shape[0], pool),
        out_shape=[
            jax.ShapeDtypeStruct((pool, PAGE, kvl, 2 * D), jnp.bfloat16),
            jax.ShapeDtypeStruct((PAGE, kvl, 2 * D), jnp.bfloat16),
        ],
        in_specs=[SMEM, SMEM, VMEM, VMEM],
        out_specs=[ANY, VMEM],
        scratch_shapes=[
            pltpu.VMEM((pool * PAGE, heads * D), jnp.float32),
            pltpu.SMEM((lengths.shape[0],), jnp.int32),
            pltpu.VMEM((2, 8 * PAGE, kvl, 2 * D), jnp.float32),
            pltpu.VMEM((pool, PAGE, kvl, 2 * D), jnp.bfloat16),
            pltpu.SemaphoreType.DMA((pool // 8,)),
        ],
        compiler_params=params(),
        cost_estimate=cost(0.01),
        name="pages",
    )(lengths, slots, own, rest)


def pick_body(bit, plan, *refs):
    *ins, out = refs
    side = lax.rem(lax.axis_index("tok") // bit, 2)
    row = 0
    for part in plan:
        rows = ins[part[0]].shape[0]
        to = pl.ds(row, rows)
        if len(part) == 1:
            out[to, :] = ins[part[0]][...]
        else:
            for value, index in enumerate(part):
                @pl.when(side == value)
                def _(index=index, to=to):
                    out[to, :] = ins[index][...]
        row += rows


def pick(bit, plan, *arrays):
    rows = sum(arrays[part[0]].shape[0] for part in plan)
    last = max(max(part) for part in plan)
    return pl.pallas_call(
        functools.partial(pick_body, bit, plan),
        out_shape=jax.ShapeDtypeStruct((rows, arrays[0].shape[1]), jnp.bfloat16),
        in_specs=[ANY if i > last else VMEM for i in range(len(arrays))],
        out_specs=VMEM,
        compiler_params=params(8),
        cost_estimate=cost(0.01),
        name="pick",
    )(*arrays)


def after_body(*refs):
    del refs


def after(x, *earlier):
    return pl.pallas_call(
        after_body,
        out_shape=jax.ShapeDtypeStruct(x.shape, x.dtype),
        in_specs=[ANY] * (1 + len(earlier)),
        out_specs=ANY,
        input_output_aliases={0: 0},
        compiler_params=params(1),
        cost_estimate=cost(0.01),
        name="after",
    )(x, *earlier)


def on_device(queries, key_states, value_states, query_gain, key_gain, lengths, slot_order):
    heads = lax.axis_size("head")
    others = range(1, heads)

    table, own, *away = kv_prep(
        lengths, key_states, value_states, key_gain.reshape(1, D), heads
    )
    rest = join([around(part, "head", d) for d, part in enumerate(away, 1)])
    own4 = around(own, "tok", 4)
    q_own, *q_away, turned = q_prep(queries, query_gain.reshape(1, D), table, heads)
    q_rest = join([around(part, "head", d) for d, part in enumerate(q_away, 1)])
    rest = after(rest, turned)
    rest4, rest2 = around(rest, "tok", 4), onward(rest, "tok", 2)
    base = [(0, 0, "own", 0)] + [(1, d - 1, "own", d) for d in others]
    [own_state] = attend(lengths, [q_own], [own, rest], [(0, 0, None, base)], False, heads)

    own4 = after(own4, own_state[0])
    own2 = swap(pick(2, ((0, 1),), own, own4), 2)
    page_pool, head_page = pages(lengths, slot_order, own, rest, heads)
    own_mixed = pick(1, ((0, 1), (2,)), own, own4, own2, head_page)
    own_s = swap(own_mixed, 1)

    qs = [q_own, q_rest]
    near = [(2, 0, "far", 0), (3, 0, "near", 0)]
    own_state, rest_state = attend(
        lengths, qs, [own, rest, own4, own2],
        [(0, 0, own_state, near), (1, 1, None, base + near)], False, heads,
        own_mixed,
    )

    rest_mixed = pick(1, ((0, 1), (2,)), rest, rest4, rest2, own_state[0])
    rest_s = swap(rest_mixed, 1)
    pieces = [(2, 0, "mix_swap", 0), (2, 1, "near_swap", 0)]
    pieces += [(0, d - 1, "far", d) for d in others] + [(1, d - 1, "near", d) for d in others]
    own_state, rest_state = attend(
        lengths, qs, [rest4, rest2, own_s],
        [(0, 0, own_state, pieces), (1, 1, rest_state, pieces)], False, heads, rest_mixed,
    )
    pieces = [(0, d - 1, "mix_swap", d) for d in others]
    pieces += [(0, heads + d - 2, "near_swap", d) for d in others]
    attention, page_pool = attend(
        lengths, qs, [rest_s],
        [(0, 0, own_state, pieces), (1, 1, rest_state, pieces)], True, heads,
        slot_order, own_s, head_page, page_pool,
    )
    return (attention, page_pool)


def solution(mesh):
    in_specs = (
        P(("tok", "head"), None),
        P(("tok", "head"), None),
        P(("tok", "head"), None),
        P(),
        P(),
        P(),
        P("tok", None),
    )
    out_specs = (P("tok", "head"), P("tok", None, "head", None))
    return jax.shard_map(
        on_device, mesh=mesh, in_specs=in_specs, out_specs=out_specs, check_vma=False
    )
```

```python
import functools
import math

import jax
import jax.numpy as jnp
from jax import lax
from jax.experimental import pallas as pl
from jax.experimental.pallas import tpu as pltpu
from jax.sharding import PartitionSpec as P

D = 128
PAGE = 16
HIDE = -2e30
FLOOR = -1e30
MIB = 1024 * 1024
SCALE = math.log2(math.e) / math.sqrt(D)

VMEM = pl.BlockSpec(memory_space=pltpu.VMEM)
SMEM = pl.BlockSpec(memory_space=pltpu.SMEM)
TOKEN = jax.ShapeDtypeStruct((8, D), jnp.float32)
ANY = pl.BlockSpec(memory_space=pl.ANY)
HBM = pl.BlockSpec(memory_space=pltpu.HBM)


def cost(us):
    return pl.CostEstimate(flops=int(us * 1.15e9), bytes_accessed=0, transcendentals=0)


def params(mib=32):
    return pltpu.CompilerParams(vmem_limit_bytes=mib * MIB)


def around(x, axis, by):
    peers = lax.axis_size(axis)
    return lax.ppermute(x, axis, [(i, (i + by) % peers) for i in range(peers)])


def onward(x, axis, by):
    peers = lax.axis_size(axis)
    return lax.ppermute(x, axis, [(i, i + by) for i in range(peers - by)])


def swap(x, bit):
    peers = lax.axis_size("tok")
    return lax.ppermute(x, "tok", [(i, i ^ bit) for i in range(peers)])


def join(parts):
    return parts[0] if len(parts) == 1 else jnp.concatenate(parts, axis=0)


def at(index):
    return pl.ds(index, D) if isinstance(index, int) else pl.ds(pl.multiple_of(index, D), D)


def seg_first(pos, lengths, segs):
    first = jnp.zeros_like(pos)
    start = jnp.int32(0)
    for s in range(segs):
        first = jnp.where(pos >= start, start, first)
        start = start + lengths[s]
    return first


def seg_bounds(shape, axis, lengths, segs):
    index = lax.broadcasted_iota(jnp.int32, shape, axis)
    begin = jnp.where(index == segs, -(2**30), 2**30)
    end = jnp.zeros(shape, jnp.int32)
    here = jnp.int32(0)
    for s in range(segs):
        begin = jnp.where(index == s, here, begin)
        here = here + lengths[s]
        end = jnp.where(index == s, here, end)
    return begin, end


def rotate(x, cos_gain, sin_gain):
    power = jnp.mean(x * x, axis=0, keepdims=True)
    half = D // 2
    turned = jnp.concatenate([x[half:], x[:half]], axis=0)
    return (x * cos_gain + turned * sin_gain) * lax.rsqrt(power + 1e-06)


def gain_tables(cosine, sine, gain_row):
    gain = jnp.broadcast_to(gain_row, (D, D)).T
    half = D // 2
    turned = jnp.concatenate([gain[half:], gain[:half]], axis=0)
    cos_gain = jnp.concatenate([cosine, cosine], axis=0) * gain
    sin_gain = jnp.concatenate([-sine, sine], axis=0) * turned
    return cos_gain, sin_gain


def table_rows(segs):
    used = (segs + 16) // 16 * 16
    starts = [D]
    for rows in (used, used, 8, 8, 8):
        starts.append(starts[-1] + rows)
    return starts


def kv_prep_body(heads, segs, lengths_in, k_in, v_in, gain_in, q_gain_in, table_ref, *refs):
    outs, (lengths, k_ref, v_ref, gain_ref, q_gain_ref, sems) = refs[:heads], refs[heads:]
    pairs = [(lengths_in, lengths), (gain_in, gain_ref), (k_in, k_ref), (v_in, v_ref)]
    pairs += [(q_gain_in, q_gain_ref)]
    copies = [pltpu.make_async_copy(a, b, sems.at[i]) for i, (a, b) in enumerate(pairs)]
    for copy in copies:
        copy.start()
    rows = k_ref.shape[0]
    kvl = k_ref.shape[1] // D // heads
    x = lax.axis_index("head")
    base = (lax.axis_index("tok") * heads + x) * rows
    half = D // 2
    pos = base + lax.broadcasted_iota(jnp.int32, (half, rows), 1)
    step = lax.broadcasted_iota(jnp.int32, (half, rows), 0).astype(jnp.float32)
    frequency = jnp.exp(step * (-2.0 * math.log(1000000.0) / D))
    copies[0].wait()
    offset = (pos - seg_first(pos, lengths, segs)).astype(jnp.float32)
    angles = offset * frequency
    cosine, sine = jnp.cos(angles), jnp.sin(angles)
    table_ref[:half] = cosine
    table_ref[half:D] = sine
    down, down_end, along, along_end, gain_at, stop = table_rows(segs)
    begin, end = seg_bounds((down_end - down, D), 0, lengths, segs)
    table_ref[down:down_end] = begin.astype(jnp.float32)
    table_ref[down_end:along] = end.astype(jnp.float32)
    begin, end = seg_bounds((8, D), 1, lengths, segs)
    table_ref[along:along_end] = begin.astype(jnp.float32)
    table_ref[along_end:gain_at] = end.astype(jnp.float32)
    copies[4].wait()
    table_ref[gain_at:stop] = jnp.broadcast_to(q_gain_ref[...], (8, D))
    copies[1].wait()
    cos_gain, sin_gain = gain_tables(cosine, sine, gain_ref[...])
    copies[2].wait()
    copies[3].wait()
    for d in reversed(range(heads)):
        peer = lax.rem(x + d, heads)
        for j in range(kvl):
            head = peer * kvl + j
            key = k_ref[:, at(head * D)].astype(jnp.float32).T
            key = rotate(key, cos_gain, sin_gain).T
            outs[d][:, 2 * j * D : (2 * j + 1) * D] = key.astype(jnp.bfloat16)
            value = v_ref[:, at(head * D)]
            outs[d][:, (2 * j + 1) * D : (2 * j + 2) * D] = value.T


def kv_prep(lengths, keys, values, gain, q_gain, heads):
    rows, width = keys.shape
    table = jax.ShapeDtypeStruct((table_rows(lengths.shape[0])[-1], rows), jnp.float32)
    part = jax.ShapeDtypeStruct((rows, 2 * width // heads), jnp.bfloat16)
    return pl.pallas_call(
        functools.partial(kv_prep_body, heads, lengths.shape[0]),
        out_shape=[table] + [part] * heads,
        in_specs=[HBM] * 5,
        out_specs=[VMEM] * (1 + heads),
        scratch_shapes=[
            pltpu.SMEM(lengths.shape, jnp.int32),
            pltpu.VMEM(keys.shape, jnp.bfloat16),
            pltpu.VMEM(values.shape, jnp.bfloat16),
            pltpu.VMEM(gain.shape, jnp.float32),
            pltpu.VMEM(gain.shape, jnp.float32),
            pltpu.SemaphoreType.DMA((5,)),
        ],
        compiler_params=params(62),
        cost_estimate=cost(0.01),
        name="kv_prep",
    )(lengths, keys, values, gain, q_gain)


def q_prep_body(heads, segs, q_ref, table_ref, own_ref, *refs):
    del own_ref
    *outs, token = refs
    token[...] = jnp.zeros_like(token)
    ql = q_ref.shape[1] // D // heads
    x = lax.axis_index("head")
    half = D // 2
    cos_gain, sin_gain = gain_tables(table_ref[:half], table_ref[half:D], table_ref[pl.ds(table_rows(segs)[4], 1), :])
    for d in reversed(range(heads)):
        peer = lax.rem(x + d, heads)
        for j in range(ql):
            query = q_ref[:, at((peer * ql + j) * D)].astype(jnp.float32).T
            outs[d][j * D : (j + 1) * D, :] = rotate(query, cos_gain, sin_gain).astype(
                jnp.bfloat16
            )


def q_prep(queries, table, own, heads, segs):
    rows, width = queries.shape
    part = jax.ShapeDtypeStruct((width // heads, rows), jnp.bfloat16)
    return pl.pallas_call(
        functools.partial(q_prep_body, heads, segs),
        out_shape=[part] * heads + [TOKEN],
        in_specs=[VMEM] * 3,
        out_specs=[VMEM] * (heads + 1),
        compiler_params=params(),
        cost_estimate=cost(0.01),
        name="q_prep",
    )(queries, table, own)


def shard_of(kind, tok):
    core = lax.rem(tok, 2)
    if kind == "own":
        return tok
    if kind == "far":
        return tok - 4
    if kind == "near":
        return tok - 2
    if kind == "near_swap":
        return tok - 1 - 2 * core
    return jnp.where(core == 0, tok - 3, tok - 1)


def attend_body(heads, segs, jobs, last, counts, table, *refs):
    n_q, n_kv, n_state, n_earlier = counts
    q_refs, refs = refs[:n_q], refs[n_q:]
    kv_refs, refs = refs[:n_kv], refs[n_kv:]
    states, refs = refs[: 3 * n_state], refs[3 * n_state :]
    earlier, refs = refs[:n_earlier], refs[n_earlier:]
    n_out = 2 if last else 3 * len(jobs)
    outs, (s_scr, p_scr, e_scr, f_scr, *page) = refs[:n_out], refs[n_out:]
    if last:
        out_scr, out_sems, *page = page
    bufs = s_scr.shape[0]
    x = lax.axis_index("head")
    tok = lax.axis_index("tok")
    rows = D
    kvl = kv_refs[0].shape[1] // (2 * D)
    ql = f_scr.shape[2] // D * kvl
    group = ql // kvl
    wide = group * rows
    lane = lax.broadcasted_iota(jnp.int32, (rows, rows), 1)
    sub = lax.broadcasted_iota(jnp.int32, (rows, rows), 0)
    down, down_end, along, along_end, _, _ = table_rows(segs)
    used = down_end - down
    query_begin = table[down:down_end].astype(jnp.int32)
    query_end = table[down_end:along].astype(jnp.int32)
    key_begin = table[along : along + 1].astype(jnp.int32)
    key_end = table[along_end : along_end + 1].astype(jnp.int32)

    def key_block(pieces, g, side, axis):
        cols = at((2 * g + side) * D)
        return jnp.concatenate(
            [kv_refs[a][row * rows : (row + 1) * rows, cols] for a, row, _, _ in pieces],
            axis=axis,
        )

    def out_part(origin, g):
        part = at(origin * rows), pl.ds(g * group * D, group * D)
        sem = out_sems.at[origin, g]
        return pltpu.make_async_copy(out_scr.at[part], outs[0].at[part], sem)

    def prepare(slot, job, c, known):
        _, first, _, _, pieces = jobs[job]
        d = first + c
        origin = lax.rem(x - d + heads, heads)
        q_chunk = tok * heads + origin
        q_pos = q_chunk * rows + lane[:used]
        outside = jnp.where((q_pos >= query_begin) & (q_pos < query_end), 0.0, HIDE)
        outside = jnp.concatenate([outside, jnp.zeros((D - used, D), jnp.float32)], axis=0)
        f_scr[slot] = jnp.concatenate([outside.astype(jnp.bfloat16)] * group, axis=1)
        for i, (a, row, kind, kd) in enumerate(pieces):
            if kind != "own" and (a, row, kind, kd) in known:
                from_slot, j = known[a, row, kind, kd]
                e_scr[slot, i * rows : (i + 1) * rows, :] = e_scr[
                    from_slot, j * rows : (j + 1) * rows, :
                ]
                continue
            known[a, row, kind, kd] = (slot, i)
            k_chunk = shard_of(kind, tok) * heads + lax.rem(x - kd + heads, heads)
            k_pos = jnp.where(k_chunk <= q_chunk, k_chunk * rows + sub, -1)
            inside = (k_pos >= key_begin) & (k_pos < key_end)
            e_scr[slot, i * rows : (i + 1) * rows, :] = jnp.where(inside, 1.0, 0.0).astype(
                jnp.bfloat16
            )
        return origin

    def scores(buf, slot, job, c, g):
        q, first, _, s, pieces = jobs[job]
        d = first + c
        n = len(pieces)
        query = jnp.concatenate(
            [q_refs[q][at((c * ql + g * group + r) * D), :] for r in range(group)], axis=1
        )
        query = jnp.concatenate([query, f_scr[slot]], axis=0)
        keys = jnp.concatenate([key_block(pieces, g, 0, 0), e_scr[slot, : n * rows, :]], axis=1)
        score = jnp.dot(keys, query, preferred_element_type=jnp.float32)
        if s is None:
            top = jnp.full((8, wide), FLOOR, jnp.float32)
        else:
            top = jnp.broadcast_to(states[3 * s][c, g], (8, wide))
        for i, (a, row, kind, kd) in enumerate(pieces):
            block = score[i * rows : (i + 1) * rows]
            if kind == "own" and (not isinstance(d, int) or kd == d):
                late = jnp.where((sub > lane) & (kd == d), HIDE, 0.0)
                block = block + jnp.concatenate([late] * group, axis=1)
            s_scr[buf, i * rows : (i + 1) * rows, :] = block
            top = jnp.maximum(top, jnp.max(block.reshape(rows // 8, 8, wide), axis=0))
        return jnp.max(top, axis=0, keepdims=True)

    def weigh(buf, job, top):
        part = jnp.zeros((8, wide), jnp.float32)
        for i in range(len(jobs[job][4])):
            expo = jnp.exp2((s_scr[buf, i * rows : (i + 1) * rows, :] - top) * SCALE)
            part = part + jnp.sum(expo.reshape(rows // 8, 8, wide), axis=0)
            p_scr[buf, i * rows : (i + 1) * rows, :] = expo.astype(jnp.bfloat16)
        return jnp.sum(part, axis=0, keepdims=True)

    def mix(buf, job, c, g, origin, top, total):
        _, _, _, s, pieces = jobs[job]
        acc = jnp.dot(
            key_block(pieces, g, 1, 1),
            p_scr[buf, : len(pieces) * rows, :],
            preferred_element_type=jnp.float32,
        )
        if s is not None:
            fade = jnp.exp2((states[3 * s][c, g] - top) * SCALE)
            total = total + states[3 * s + 1][c, g] * fade
            acc = acc + states[3 * s + 2][c, g] * fade
        if last:
            acc = (acc * (1.0 / total)).astype(jnp.bfloat16)
            for r in range(group):
                out_scr[at(origin * rows), (g * group + r) * D : (g * group + r + 1) * D] = acc[
                    :, r * rows : (r + 1) * rows
                ].T
            part = out_part(origin, g)
            part.start()
        else:
            outs[3 * job][c, g] = top
            outs[3 * job + 1][c, g] = total
            outs[3 * job + 2][c, g] = acc

    def sweep(chunks):
        known = {}
        origins = [prepare(slot, job, c, known) for slot, (job, c) in enumerate(chunks)]
        units = [(slot, g) for slot in range(len(chunks)) for g in range(kvl)]
        tops, totals = {}, {}
        for i in range(len(units) + 2):
            if i < len(units):
                slot, g = units[i]
                tops[i] = scores(i % bufs, slot, *chunks[slot], g)
            if 0 <= i - 1 < len(units):
                slot, g = units[i - 1]
                totals[i - 1] = weigh((i - 1) % bufs, chunks[slot][0], tops[i - 1])
            if 0 <= i - 2 < len(units):
                slot, g = units[i - 2]
                job, c = chunks[slot]
                mix((i - 2) % bufs, job, c, g, origins[slot], tops[i - 2], totals[i - 2])

    if max(job[2] for job in jobs) == 1:
        sweep([(job, 0) for job in range(len(jobs))])
    else:
        for job in range(len(jobs)):
            def body(c, carry, job=job):
                sweep([(job, c)])
                return carry

            lax.fori_loop(0, jobs[job][2], body, 0)
    if last:
        slots, own_s, head_ref, _ = earlier
        first_page = (slots, own_s, kv_refs[0], head_ref, outs[1], *page)
        finish = partial_page(heads, query_begin, query_end, *first_page)
        for origin in range(heads):
            for g in range(kvl):
                out_part(origin, g).wait()
        finish()


def partial_page(heads, begins, ends, slots, own_s, rest_s, head_ref, pool_ref, page, sem):
    x = lax.axis_index("head")
    tok = lax.axis_index("tok")
    core = lax.rem(tok, 2)
    base = tok * heads * D
    here = (begins <= base) & (base < ends)
    first = jnp.max(jnp.where(here, begins.astype(jnp.float32), 0.0)).astype(jnp.int32)
    before = lax.rem(base - first, PAGE)
    slot = jnp.max(slots[:, :1].astype(jnp.float32)).astype(jnp.int32)
    kvl = head_ref.shape[1]
    d = lax.rem(x + 1, heads)
    lane = lax.broadcasted_iota(jnp.int32, (PAGE, PAGE), 1)
    sub = lax.broadcasted_iota(jnp.int32, (PAGE, PAGE), 0)
    move = jnp.where((lane == sub + PAGE - before) & (sub < before), 1.0, 0.0).astype(jnp.bfloat16)
    copy = pltpu.make_async_copy(page, pool_ref.at[slot], sem)

    def write(ref, row):
        moved = []
        for g in range(kvl):
            at_row = pl.ds(pl.multiple_of(row + D - PAGE, PAGE), PAGE)
            key = ref[at_row, 2 * g * D : (2 * g + 1) * D]
            value = ref[at(row), (2 * g + 1) * D : (2 * g + 2) * D].T[D - PAGE :]
            both = jnp.concatenate([key, value], axis=1)
            moved.append(jnp.dot(move, both, preferred_element_type=jnp.float32))
        moved = jnp.stack(moved, axis=1)
        index = lax.broadcasted_iota(jnp.int32, moved.shape, 0)
        page[...] = jnp.where(index < before, moved, head_ref[...].astype(jnp.float32)).astype(
            jnp.bfloat16
        )
        copy.start()

    @pl.when((before > 0) & (d == 0))
    def _():
        write(own_s, (1 - core) * D)

    @pl.when((before > 0) & (d > 0))
    def _():
        write(rest_s, jnp.maximum(d - 1, 0) * D + (1 - core) * (heads - 1) * D)

    def finish():
        @pl.when(before > 0)
        def _():
            copy.wait()

    return finish


def attend(table, qs, kvs, jobs, last, heads, segs, *earlier):
    kvl = kvs[0].shape[1] // (2 * D)
    states, plan = [], []
    for q, first, state, pieces in jobs:
        many = 1 if first == 0 else heads - 1
        plan.append((q, first, many, None if state is None else len(states), tuple(pieces)))
        if state is not None:
            states.append(state)
    ql = qs[plan[0][0]].shape[0] // D // plan[0][2]
    wide = ql // kvl * D
    if last:
        pool = earlier[3]
        out_shape = [jax.ShapeDtypeStruct((heads * D, ql * D), jnp.bfloat16)]
        out_shape += [jax.ShapeDtypeStruct(pool.shape, pool.dtype)]
    else:
        out_shape = []
        for _, _, many, _, _ in plan:
            row = jax.ShapeDtypeStruct((many, kvl, 1, wide), jnp.float32)
            out_shape += [row, row, jax.ShapeDtypeStruct((many, kvl, D, wide), jnp.float32)]
    inputs = [table, *qs, *kvs, *[part for state in states for part in state], *earlier]
    more = [VMEM, VMEM, VMEM, ANY] if last else [ANY] * len(earlier)
    keys = max(len(job[4]) for job in plan) * D
    together = len(plan) if heads == 2 else 1
    bufs = min(3, kvl * together)
    result = pl.pallas_call(
        functools.partial(
            attend_body, heads, segs, tuple(plan), last,
            (len(qs), len(kvs), len(states), len(earlier)),
        ),
        out_shape=out_shape,
        in_specs=[VMEM] * (len(inputs) - len(earlier)) + more,
        out_specs=[ANY, ANY] if last else [VMEM] * len(out_shape),
        input_output_aliases={len(inputs) - 1: 1} if last else {},
        scratch_shapes=[
            pltpu.VMEM((bufs, keys, wide), jnp.float32),
            pltpu.VMEM((bufs, keys, wide), jnp.bfloat16),
            pltpu.VMEM((together, keys, D), jnp.bfloat16),
            pltpu.VMEM((together, D, wide), jnp.bfloat16),
        ]
        + (
            [
                pltpu.VMEM(out_shape[0].shape, jnp.bfloat16),
                pltpu.SemaphoreType.DMA((heads, kvl)),
                pltpu.VMEM(pool.shape[1:], pool.dtype),
                pltpu.SemaphoreType.DMA,
            ]
            if last
            else []
        ),
        compiler_params=params(),
        cost_estimate=cost(0.01),
        name="attend_last" if last else "attend_part",
    )(*inputs)
    return result if last else [result[i : i + 3] for i in range(0, len(result), 3)]


def pages_body(
    heads, segs, pool, table, slots, own_ref, rest_ref, pool_ref, head_ref,
    slot_scr, wide_scr, out_scr, sems,
):
    x = lax.axis_index("head")
    base = lax.axis_index("tok") * heads * D
    down, down_end, along, _, _, _ = table_rows(segs)
    begins, ends = table[down:down_end], table[down_end:along]
    lane = lax.broadcasted_iota(jnp.int32, (1, D), 1)
    sub = lax.broadcasted_iota(jnp.int32, (D, D), 0)
    starts = [base + lax.rem(x - d + heads, heads) * D for d in range(heads)]
    flags, rows, owned = [], [], []
    for start in starts:
        pos = start + lane
        point = pos.astype(jnp.float32)
        here = (point >= begins) & (point < ends)
        first = jnp.sum(jnp.where(here, begins, 0.0), axis=0, keepdims=True).astype(jnp.int32)
        finish = jnp.sum(jnp.where(here, ends, 0.0), axis=0, keepdims=True).astype(jnp.int32)
        offset = pos - first
        rows.append(lax.rem(offset, PAGE))
        page_last = jnp.minimum(pos - rows[-1] + PAGE, finish) - 1
        owned.append(page_last < base + heads * D)
        flags.append(jnp.where(pos == page_last, 1.0, 0.0))
    flags = jnp.broadcast_to(jnp.concatenate(flags, axis=1), (16, heads * D)).astype(jnp.bfloat16)
    slot_scr[...] = jnp.zeros_like(slot_scr)
    slot_scr[0:1, 0:pool] = slots[...].astype(jnp.float32)
    slot_row = slot_scr[...].astype(jnp.bfloat16)
    ranks, targets = [], []
    for d, start in enumerate(starts):
        ahead = [jnp.where(other + sub < start + lane, 1.0, 0.0) for other in starts]
        ahead = jnp.concatenate(ahead, axis=0).astype(jnp.bfloat16)
        rank = jnp.dot(flags, ahead, preferred_element_type=jnp.float32)[:1].astype(jnp.int32)
        pick_slot = jnp.where(sub == rank, 1.0, 0.0).astype(jnp.bfloat16)
        slot = jnp.dot(slot_row, pick_slot, preferred_element_type=jnp.float32)[:1]
        row = slot.astype(jnp.int32) * PAGE + rows[d]
        targets.append(jnp.where(owned[d], row, -1))
        ranks.append(jnp.where(owned[d] & (rank == 0), rows[d], -1))
    target = jnp.concatenate(targets, axis=1)
    head_target = jnp.concatenate(ranks, axis=1)

    def marks(first_row, rows, target):
        row = first_row + lax.broadcasted_iota(jnp.int32, (rows, heads * D), 0)
        return jnp.where(row == target, 1.0, 0.0).astype(jnp.bfloat16)

    kvl = own_ref.shape[1] // (2 * D)
    both = []
    for g in range(kvl):
        key_at, value_at = at(2 * g * D), at((2 * g + 1) * D)
        others = [rest_ref[i * D : (i + 1) * D, value_at].T for i in range(heads - 1)]
        key = jnp.concatenate([own_ref[:, key_at], rest_ref[:, key_at]], axis=0)
        value = jnp.concatenate([own_ref[:, value_at].T, *others], axis=0)
        both.append(jnp.concatenate([key, value], axis=1))
    step = 8
    copies = []
    for i, page in enumerate(range(0, pool, step)):
        mark = marks(page * PAGE, step * PAGE, target)
        for g in range(kvl):
            wide_scr[i % 2, :, g, :] = jnp.dot(mark, both[g], preferred_element_type=jnp.float32)
        block = pl.ds(page, step)
        out_scr[block] = (
            wide_scr[i % 2].astype(jnp.bfloat16).reshape(step, PAGE, kvl, 2 * D)
        )
        copies.append(pltpu.make_async_copy(out_scr.at[block], pool_ref.at[block], sems.at[i]))
        copies[-1].start()
    mark = marks(0, PAGE, head_target)
    head = [jnp.dot(mark, part, preferred_element_type=jnp.float32) for part in both]
    head_ref[...] = jnp.stack(head, axis=1).astype(jnp.bfloat16)
    for copy in copies:
        copy.wait()


def pages(table, slots, own, rest, heads, segs):
    pool = slots.shape[1]
    kvl = own.shape[1] // (2 * D)
    return pl.pallas_call(
        functools.partial(pages_body, heads, segs, pool),
        out_shape=[
            jax.ShapeDtypeStruct((pool, PAGE, kvl, 2 * D), jnp.bfloat16),
            jax.ShapeDtypeStruct((PAGE, kvl, 2 * D), jnp.bfloat16),
        ],
        in_specs=[VMEM] * 4,
        out_specs=[ANY, VMEM],
        scratch_shapes=[
            pltpu.VMEM((16, D), jnp.float32),
            pltpu.VMEM((2, 8 * PAGE, kvl, 2 * D), jnp.float32),
            pltpu.VMEM((pool, PAGE, kvl, 2 * D), jnp.bfloat16),
            pltpu.SemaphoreType.DMA((pool // 8,)),
        ],
        compiler_params=params(),
        cost_estimate=cost(0.01),
        name="pages",
    )(table, slots, own, rest)


def pick_body(bit, plan, *refs):
    *ins, out = refs
    side = lax.rem(lax.axis_index("tok") // bit, 2)
    row = 0
    for part in plan:
        rows = ins[part[0]].shape[0]
        to = pl.ds(row, rows)
        if len(part) == 1:
            out[to, :] = ins[part[0]][...]
        else:
            for value, index in enumerate(part):
                @pl.when(side == value)
                def _(index=index, to=to):
                    out[to, :] = ins[index][...]
        row += rows


def pick(bit, plan, *arrays):
    rows = sum(arrays[part[0]].shape[0] for part in plan)
    last = max(max(part) for part in plan)
    return pl.pallas_call(
        functools.partial(pick_body, bit, plan),
        out_shape=jax.ShapeDtypeStruct((rows, arrays[0].shape[1]), jnp.bfloat16),
        in_specs=[ANY if i > last else VMEM for i in range(len(arrays))],
        out_specs=VMEM,
        compiler_params=params(8),
        cost_estimate=cost(0.01),
        name="pick",
    )(*arrays)


def after_body(*refs):
    del refs


def after(x, *earlier):
    return pl.pallas_call(
        after_body,
        out_shape=jax.ShapeDtypeStruct(x.shape, x.dtype),
        in_specs=[ANY] * (1 + len(earlier)),
        out_specs=ANY,
        input_output_aliases={0: 0},
        compiler_params=params(1),
        cost_estimate=cost(0.01),
        name="after",
    )(x, *earlier)


def on_device(queries, key_states, value_states, query_gain, key_gain, lengths, slot_order):
    heads = lax.axis_size("head")
    others = range(1, heads)

    table, own, *away = kv_prep(
        lengths, key_states, value_states, key_gain.reshape(1, D), query_gain.reshape(1, D), heads
    )
    segs = lengths.shape[0]
    rest = join([around(part, "head", d) for d, part in enumerate(away, 1)])
    own4 = around(own, "tok", 4)
    q_own, *q_away, turned = q_prep(queries, table, own, heads, segs)
    q_rest = join([around(part, "head", d) for d, part in enumerate(q_away, 1)])
    rest = after(rest, turned)
    rest4, rest2 = around(rest, "tok", 4), onward(rest, "tok", 2)
    base = [(0, 0, "own", 0)] + [(1, d - 1, "own", d) for d in others]
    [own_state] = attend(table, [q_own], [own, rest], [(0, 0, None, base)], False, heads, segs)

    own4 = after(own4, own_state[0])
    own2 = swap(pick(2, ((0, 1),), own, own4), 2)
    page_pool, head_page = pages(table, slot_order, own, rest, heads, segs)
    own_mixed = pick(1, ((0, 1), (2,)), own, own4, own2, head_page)
    own_s = swap(own_mixed, 1)

    qs = [q_own, q_rest]
    near = [(2, 0, "far", 0), (3, 0, "near", 0)]
    own_state, rest_state = attend(
        table, qs, [own, rest, own4, own2],
        [(0, 0, own_state, near), (1, 1, None, base + near)], False, heads, segs,
        own_mixed,
    )

    rest_mixed = pick(1, ((0, 1), (2,)), rest, rest4, rest2, own_state[0])
    rest_s = swap(rest_mixed, 1)
    pieces = [(2, 0, "mix_swap", 0), (2, 1, "near_swap", 0)]
    pieces += [(0, d - 1, "far", d) for d in others] + [(1, d - 1, "near", d) for d in others]
    own_state, rest_state = attend(
        table, qs, [rest4, rest2, own_s],
        [(0, 0, own_state, pieces), (1, 1, rest_state, pieces)], False, heads, segs, rest_mixed,
    )
    pieces = [(0, d - 1, "mix_swap", d) for d in others]
    pieces += [(0, heads + d - 2, "near_swap", d) for d in others]
    attention, page_pool = attend(
        table, qs, [rest_s],
        [(0, 0, own_state, pieces), (1, 1, rest_state, pieces)], True, heads, segs,
        slot_order, own_s, head_page, page_pool,
    )
    return (attention, page_pool)


def solution(mesh):
    in_specs = (
        P(("tok", "head"), None),
        P(("tok", "head"), None),
        P(("tok", "head"), None),
        P(),
        P(),
        P(),
        P("tok", None),
    )
    out_specs = (P("tok", "head"), P("tok", None, "head", None))
    return jax.shard_map(
        on_device, mesh=mesh, in_specs=in_specs, out_specs=out_specs, check_vma=False
    )
```

```python
import functools
import math

import jax
import jax.numpy as jnp
from jax import lax
from jax.experimental import pallas as pl
from jax.experimental.pallas import tpu as pltpu
from jax.sharding import PartitionSpec as P

D = 128
PAGE = 16
HIDE = -2e30
FLOOR = -1e30
MIB = 1024 * 1024
SCALE = math.log2(math.e) / math.sqrt(D)

VMEM = pl.BlockSpec(memory_space=pltpu.VMEM)
SMEM = pl.BlockSpec(memory_space=pltpu.SMEM)
TOKEN = jax.ShapeDtypeStruct((8, D), jnp.float32)
ANY = pl.BlockSpec(memory_space=pl.ANY)
HBM = pl.BlockSpec(memory_space=pltpu.HBM)


def cost(us):
    return pl.CostEstimate(flops=int(us * 1.15e9), bytes_accessed=0, transcendentals=0)


def params(mib=32):
    return pltpu.CompilerParams(vmem_limit_bytes=mib * MIB)


def around(x, axis, by):
    peers = lax.axis_size(axis)
    return lax.ppermute(x, axis, [(i, (i + by) % peers) for i in range(peers)])


def onward(x, axis, by):
    peers = lax.axis_size(axis)
    return lax.ppermute(x, axis, [(i, i + by) for i in range(peers - by)])


def swap(x, bit):
    peers = lax.axis_size("tok")
    return lax.ppermute(x, "tok", [(i, i ^ bit) for i in range(peers)])


def join(parts):
    return parts[0] if len(parts) == 1 else jnp.concatenate(parts, axis=0)


def at(index):
    return pl.ds(index, D) if isinstance(index, int) else pl.ds(pl.multiple_of(index, D), D)


def seg_first(pos, lengths, segs):
    first = jnp.zeros_like(pos)
    start = jnp.int32(0)
    for s in range(segs):
        first = jnp.where(pos >= start, start, first)
        start = start + lengths[s]
    return first


def seg_bounds(shape, axis, lengths, segs):
    index = lax.broadcasted_iota(jnp.int32, shape, axis)
    begin = jnp.where(index == segs, -(2**30), 2**30)
    end = jnp.zeros(shape, jnp.int32)
    here = jnp.int32(0)
    for s in range(segs):
        begin = jnp.where(index == s, here, begin)
        here = here + lengths[s]
        end = jnp.where(index == s, here, end)
    return begin, end


def rotate(x, cos_gain, sin_gain):
    power = jnp.mean(x * x, axis=0, keepdims=True)
    half = D // 2
    turned = jnp.concatenate([x[half:], x[:half]], axis=0)
    return (x * cos_gain + turned * sin_gain) * lax.rsqrt(power + 1e-06)


def gain_tables(cosine, sine, gain_row):
    gain = jnp.broadcast_to(gain_row, (D, D)).T
    half = D // 2
    turned = jnp.concatenate([gain[half:], gain[:half]], axis=0)
    cos_gain = jnp.concatenate([cosine, cosine], axis=0) * gain
    sin_gain = jnp.concatenate([-sine, sine], axis=0) * turned
    return cos_gain, sin_gain


def table_rows(segs):
    used = (segs + 16) // 16 * 16
    starts = [D]
    for rows in (used, used, 8, 8, 8):
        starts.append(starts[-1] + rows)
    return starts


def kv_prep_body(heads, segs, lengths_in, k_in, v_in, gain_in, q_gain_in, table_ref, *refs):
    outs, (lengths, k_ref, v_ref, gain_ref, q_gain_ref, sems) = refs[:heads], refs[heads:]
    pairs = [(lengths_in, lengths), (gain_in, gain_ref), (k_in, k_ref), (v_in, v_ref)]
    pairs += [(q_gain_in, q_gain_ref)]
    copies = [pltpu.make_async_copy(a, b, sems.at[i]) for i, (a, b) in enumerate(pairs)]
    for copy in copies:
        copy.start()
    rows = k_ref.shape[0]
    kvl = k_ref.shape[1] // D // heads
    x = lax.axis_index("head")
    base = (lax.axis_index("tok") * heads + x) * rows
    half = D // 2
    pos = base + lax.broadcasted_iota(jnp.int32, (half, rows), 1)
    step = lax.broadcasted_iota(jnp.int32, (half, rows), 0).astype(jnp.float32)
    frequency = jnp.exp(step * (-2.0 * math.log(1000000.0) / D))
    copies[0].wait()
    offset = (pos - seg_first(pos, lengths, segs)).astype(jnp.float32)
    angles = offset * frequency
    cosine, sine = jnp.cos(angles), jnp.sin(angles)
    table_ref[:half] = cosine
    table_ref[half:D] = sine
    down, down_end, along, along_end, gain_at, stop = table_rows(segs)
    begin, end = seg_bounds((down_end - down, D), 0, lengths, segs)
    table_ref[down:down_end] = begin.astype(jnp.float32)
    table_ref[down_end:along] = end.astype(jnp.float32)
    begin, end = seg_bounds((8, D), 1, lengths, segs)
    table_ref[along:along_end] = begin.astype(jnp.float32)
    table_ref[along_end:gain_at] = end.astype(jnp.float32)
    copies[4].wait()
    table_ref[gain_at:stop] = jnp.broadcast_to(q_gain_ref[...], (8, D))
    copies[1].wait()
    cos_gain, sin_gain = gain_tables(cosine, sine, gain_ref[...])
    copies[2].wait()
    copies[3].wait()
    for d in reversed(range(heads)):
        peer = lax.rem(x + d, heads)
        for j in range(kvl):
            head = peer * kvl + j
            key = k_ref[:, at(head * D)].T.astype(jnp.float32)
            key = rotate(key, cos_gain, sin_gain).astype(jnp.bfloat16)
            outs[d][:, 2 * j * D : (2 * j + 1) * D] = key.T
            value = v_ref[:, at(head * D)]
            outs[d][:, (2 * j + 1) * D : (2 * j + 2) * D] = value.T


def kv_prep(lengths, keys, values, gain, q_gain, heads):
    rows, width = keys.shape
    table = jax.ShapeDtypeStruct((table_rows(lengths.shape[0])[-1], rows), jnp.float32)
    part = jax.ShapeDtypeStruct((rows, 2 * width // heads), jnp.bfloat16)
    return pl.pallas_call(
        functools.partial(kv_prep_body, heads, lengths.shape[0]),
        out_shape=[table] + [part] * heads,
        in_specs=[HBM] * 5,
        out_specs=[VMEM] * (1 + heads),
        scratch_shapes=[
            pltpu.SMEM(lengths.shape, jnp.int32),
            pltpu.VMEM(keys.shape, jnp.bfloat16),
            pltpu.VMEM(values.shape, jnp.bfloat16),
            pltpu.VMEM(gain.shape, jnp.float32),
            pltpu.VMEM(gain.shape, jnp.float32),
            pltpu.SemaphoreType.DMA((5,)),
        ],
        compiler_params=params(62),
        cost_estimate=cost(0.01),
        name="kv_prep",
    )(lengths, keys, values, gain, q_gain)


def q_prep_body(heads, segs, q_ref, table_ref, own_ref, *refs):
    del own_ref
    *outs, token = refs
    token[...] = jnp.zeros_like(token)
    ql = q_ref.shape[1] // D // heads
    x = lax.axis_index("head")
    half = D // 2
    cos_gain, sin_gain = gain_tables(table_ref[:half], table_ref[half:D], table_ref[pl.ds(table_rows(segs)[4], 1), :])
    for d in reversed(range(heads)):
        peer = lax.rem(x + d, heads)
        for j in range(ql):
            query = q_ref[:, at((peer * ql + j) * D)].T.astype(jnp.float32)
            outs[d][j * D : (j + 1) * D, :] = rotate(query, cos_gain, sin_gain).astype(
                jnp.bfloat16
            )


def q_prep(queries, table, own, heads, segs):
    rows, width = queries.shape
    part = jax.ShapeDtypeStruct((width // heads, rows), jnp.bfloat16)
    return pl.pallas_call(
        functools.partial(q_prep_body, heads, segs),
        out_shape=[part] * heads + [TOKEN],
        in_specs=[VMEM] * 3,
        out_specs=[VMEM] * (heads + 1),
        compiler_params=params(),
        cost_estimate=cost(0.01),
        name="q_prep",
    )(queries, table, own)


def shard_of(kind, tok):
    core = lax.rem(tok, 2)
    if kind == "own":
        return tok
    if kind == "far":
        return tok - 4
    if kind == "near":
        return tok - 2
    if kind == "near_swap":
        return tok - 1 - 2 * core
    return jnp.where(core == 0, tok - 3, tok - 1)


def attend_body(heads, segs, jobs, last, counts, table, *refs):
    n_q, n_kv, n_state, n_earlier = counts
    q_refs, refs = refs[:n_q], refs[n_q:]
    kv_refs, refs = refs[:n_kv], refs[n_kv:]
    states, refs = refs[: 3 * n_state], refs[3 * n_state :]
    earlier, refs = refs[:n_earlier], refs[n_earlier:]
    n_out = 2 if last else 3 * len(jobs)
    outs, (s_scr, p_scr, e_scr, f_scr, *page) = refs[:n_out], refs[n_out:]
    if last:
        out_scr, out_sems, *page = page
    bufs = s_scr.shape[0]
    x = lax.axis_index("head")
    tok = lax.axis_index("tok")
    rows = D
    kvl = kv_refs[0].shape[1] // (2 * D)
    ql = f_scr.shape[2] // D * kvl
    group = ql // kvl
    wide = group * rows
    lane = lax.broadcasted_iota(jnp.int32, (rows, rows), 1)
    sub = lax.broadcasted_iota(jnp.int32, (rows, rows), 0)
    down, down_end, along, along_end, _, _ = table_rows(segs)
    used = down_end - down
    query_begin = table[down:down_end].astype(jnp.int32)
    query_end = table[down_end:along].astype(jnp.int32)
    key_begin = table[along : along + 1].astype(jnp.int32)
    key_end = table[along_end : along_end + 1].astype(jnp.int32)

    def key_block(pieces, g, side, axis):
        cols = at((2 * g + side) * D)
        return jnp.concatenate(
            [kv_refs[a][row * rows : (row + 1) * rows, cols] for a, row, _, _ in pieces],
            axis=axis,
        )

    def out_part(origin, g):
        part = at(origin * rows), pl.ds(g * group * D, group * D)
        sem = out_sems.at[origin, g]
        return pltpu.make_async_copy(out_scr.at[part], outs[0].at[part], sem)

    def prepare(slot, job, c, known):
        _, first, _, _, pieces = jobs[job]
        d = first + c
        origin = lax.rem(x - d + heads, heads)
        q_chunk = tok * heads + origin
        q_pos = q_chunk * rows + lane[:used]
        outside = jnp.where((q_pos >= query_begin) & (q_pos < query_end), 0.0, HIDE)
        outside = jnp.concatenate([outside, jnp.zeros((D - used, D), jnp.float32)], axis=0)
        f_scr[slot] = jnp.concatenate([outside.astype(jnp.bfloat16)] * group, axis=1)
        for i, (a, row, kind, kd) in enumerate(pieces):
            if kind != "own" and (a, row, kind, kd) in known:
                from_slot, j = known[a, row, kind, kd]
                e_scr[slot, i * rows : (i + 1) * rows, :] = e_scr[
                    from_slot, j * rows : (j + 1) * rows, :
                ]
                continue
            known[a, row, kind, kd] = (slot, i)
            k_chunk = shard_of(kind, tok) * heads + lax.rem(x - kd + heads, heads)
            k_pos = jnp.where(k_chunk <= q_chunk, k_chunk * rows + sub, -1)
            inside = (k_pos >= key_begin) & (k_pos < key_end)
            e_scr[slot, i * rows : (i + 1) * rows, :] = jnp.where(inside, 1.0, 0.0).astype(
                jnp.bfloat16
            )
        return origin

    def scores(buf, slot, job, c, g):
        q, first, _, s, pieces = jobs[job]
        d = first + c
        n = len(pieces)
        query = jnp.concatenate(
            [q_refs[q][at((c * ql + g * group + r) * D), :] for r in range(group)], axis=1
        )
        query = jnp.concatenate([query, f_scr[slot]], axis=0)
        keys = jnp.concatenate([key_block(pieces, g, 0, 0), e_scr[slot, : n * rows, :]], axis=1)
        score = jnp.dot(keys, query, preferred_element_type=jnp.float32)
        if s is None:
            top = jnp.full((8, wide), FLOOR, jnp.float32)
        else:
            top = jnp.broadcast_to(states[3 * s][c, g], (8, wide))
        for i, (a, row, kind, kd) in enumerate(pieces):
            block = score[i * rows : (i + 1) * rows]
            if kind == "own" and (not isinstance(d, int) or kd == d):
                late = jnp.where((sub > lane) & (kd == d), HIDE, 0.0)
                block = block + jnp.concatenate([late] * group, axis=1)
            s_scr[buf, i * rows : (i + 1) * rows, :] = block
            top = jnp.maximum(top, jnp.max(block.reshape(rows // 8, 8, wide), axis=0))
        return jnp.max(top, axis=0, keepdims=True)

    def weigh(buf, job, top):
        part = jnp.zeros((8, wide), jnp.float32)
        for i in range(len(jobs[job][4])):
            expo = jnp.exp2((s_scr[buf, i * rows : (i + 1) * rows, :] - top) * SCALE)
            part = part + jnp.sum(expo.reshape(rows // 8, 8, wide), axis=0)
            p_scr[buf, i * rows : (i + 1) * rows, :] = expo.astype(jnp.bfloat16)
        return jnp.sum(part, axis=0, keepdims=True)

    def mix(buf, job, c, g, origin, top, total):
        _, _, _, s, pieces = jobs[job]
        acc = jnp.dot(
            key_block(pieces, g, 1, 1),
            p_scr[buf, : len(pieces) * rows, :],
            preferred_element_type=jnp.float32,
        )
        if s is not None:
            fade = jnp.exp2((states[3 * s][c, g] - top) * SCALE)
            total = total + states[3 * s + 1][c, g] * fade
            acc = acc + states[3 * s + 2][c, g] * fade
        if last:
            acc = (acc * (1.0 / total)).astype(jnp.bfloat16)
            for r in range(group):
                out_scr[at(origin * rows), (g * group + r) * D : (g * group + r + 1) * D] = acc[
                    :, r * rows : (r + 1) * rows
                ].T
            part = out_part(origin, g)
            part.start()
        else:
            outs[3 * job][c, g] = top
            outs[3 * job + 1][c, g] = total
            outs[3 * job + 2][c, g] = acc

    def sweep(chunks):
        known = {}
        origins = [prepare(slot, job, c, known) for slot, (job, c) in enumerate(chunks)]
        units = [(slot, g) for slot in range(len(chunks)) for g in range(kvl)]
        tops, totals = {}, {}
        for i in range(len(units) + 2):
            if i < len(units):
                slot, g = units[i]
                tops[i] = scores(i % bufs, slot, *chunks[slot], g)
            if 0 <= i - 1 < len(units):
                slot, g = units[i - 1]
                totals[i - 1] = weigh((i - 1) % bufs, chunks[slot][0], tops[i - 1])
            if 0 <= i - 2 < len(units):
                slot, g = units[i - 2]
                job, c = chunks[slot]
                mix((i - 2) % bufs, job, c, g, origins[slot], tops[i - 2], totals[i - 2])

    if last:
        before, slot = partial_place(heads, query_begin, query_end, earlier[0])
    if max(job[2] for job in jobs) == 1:
        sweep([(job, 0) for job in range(len(jobs))])
    else:
        for job in range(len(jobs)):
            def body(c, carry, job=job):
                sweep([(job, c)])
                return carry

            lax.fori_loop(0, jobs[job][2], body, 0)
    if last:
        _, own_s, head_ref, _ = earlier
        finish = partial_page(heads, before, slot, own_s, kv_refs[0], head_ref, outs[1], *page)
        for origin in range(heads):
            for g in range(kvl):
                out_part(origin, g).wait()
        finish()


def partial_place(heads, begins, ends, slots):
    base = lax.axis_index("tok") * heads * D
    here = (begins <= base) & (base < ends)
    first = jnp.max(jnp.where(here, begins.astype(jnp.float32), 0.0)).astype(jnp.int32)
    before = lax.rem(base - first, PAGE)
    slot = jnp.max(slots[:, :1].astype(jnp.float32)).astype(jnp.int32)
    return before, slot


def partial_page(heads, before, slot, own_s, rest_s, head_ref, pool_ref, page, sem):
    x = lax.axis_index("head")
    core = lax.rem(lax.axis_index("tok"), 2)
    kvl = head_ref.shape[1]
    d = lax.rem(x + 1, heads)
    lane = lax.broadcasted_iota(jnp.int32, (PAGE, PAGE), 1)
    sub = lax.broadcasted_iota(jnp.int32, (PAGE, PAGE), 0)
    move = jnp.where((lane == sub + PAGE - before) & (sub < before), 1.0, 0.0).astype(jnp.bfloat16)
    copy = pltpu.make_async_copy(page, pool_ref.at[slot], sem)

    def write(ref, row):
        moved = []
        for g in range(kvl):
            at_row = pl.ds(pl.multiple_of(row + D - PAGE, PAGE), PAGE)
            key = ref[at_row, 2 * g * D : (2 * g + 1) * D]
            value = ref[at(row), (2 * g + 1) * D : (2 * g + 2) * D].T[D - PAGE :]
            both = jnp.concatenate([key, value], axis=1)
            moved.append(jnp.dot(move, both, preferred_element_type=jnp.float32))
        moved = jnp.stack(moved, axis=1)
        index = lax.broadcasted_iota(jnp.int32, moved.shape, 0)
        page[...] = jnp.where(index < before, moved, head_ref[...].astype(jnp.float32)).astype(
            jnp.bfloat16
        )
        copy.start()

    @pl.when((before > 0) & (d == 0))
    def _():
        write(own_s, (1 - core) * D)

    @pl.when((before > 0) & (d > 0))
    def _():
        write(rest_s, jnp.maximum(d - 1, 0) * D + (1 - core) * (heads - 1) * D)

    def finish():
        @pl.when(before > 0)
        def _():
            copy.wait()

    return finish


def attend(table, qs, kvs, jobs, last, heads, segs, *earlier):
    kvl = kvs[0].shape[1] // (2 * D)
    states, plan = [], []
    for q, first, state, pieces in jobs:
        many = 1 if first == 0 else heads - 1
        plan.append((q, first, many, None if state is None else len(states), tuple(pieces)))
        if state is not None:
            states.append(state)
    ql = qs[plan[0][0]].shape[0] // D // plan[0][2]
    wide = ql // kvl * D
    if last:
        pool = earlier[3]
        out_shape = [jax.ShapeDtypeStruct((heads * D, ql * D), jnp.bfloat16)]
        out_shape += [jax.ShapeDtypeStruct(pool.shape, pool.dtype)]
    else:
        out_shape = []
        for _, _, many, _, _ in plan:
            row = jax.ShapeDtypeStruct((many, kvl, 1, wide), jnp.float32)
            out_shape += [row, row, jax.ShapeDtypeStruct((many, kvl, D, wide), jnp.float32)]
    inputs = [table, *qs, *kvs, *[part for state in states for part in state], *earlier]
    more = [VMEM, VMEM, VMEM, ANY] if last else [ANY] * len(earlier)
    keys = max(len(job[4]) for job in plan) * D
    together = len(plan) if heads == 2 else 1
    bufs = min(3, kvl * together)
    result = pl.pallas_call(
        functools.partial(
            attend_body, heads, segs, tuple(plan), last,
            (len(qs), len(kvs), len(states), len(earlier)),
        ),
        out_shape=out_shape,
        in_specs=[VMEM] * (len(inputs) - len(earlier)) + more,
        out_specs=[ANY, ANY] if last else [VMEM] * len(out_shape),
        input_output_aliases={len(inputs) - 1: 1} if last else {},
        scratch_shapes=[
            pltpu.VMEM((bufs, keys, wide), jnp.float32),
            pltpu.VMEM((bufs, keys, wide), jnp.bfloat16),
            pltpu.VMEM((together, keys, D), jnp.bfloat16),
            pltpu.VMEM((together, D, wide), jnp.bfloat16),
        ]
        + (
            [
                pltpu.VMEM(out_shape[0].shape, jnp.bfloat16),
                pltpu.SemaphoreType.DMA((heads, kvl)),
                pltpu.VMEM(pool.shape[1:], pool.dtype),
                pltpu.SemaphoreType.DMA,
            ]
            if last
            else []
        ),
        compiler_params=params(),
        cost_estimate=cost(0.01),
        name="attend_last" if last else "attend_part",
    )(*inputs)
    return result if last else [result[i : i + 3] for i in range(0, len(result), 3)]


def pages_body(
    heads, segs, pool, table, slots, own_ref, rest_ref, pool_ref, head_ref,
    slot_scr, wide_scr, out_scr, sems,
):
    x = lax.axis_index("head")
    base = lax.axis_index("tok") * heads * D
    down, down_end, along, _, _, _ = table_rows(segs)
    begins, ends = table[down:down_end], table[down_end:along]
    lane = lax.broadcasted_iota(jnp.int32, (1, D), 1)
    sub = lax.broadcasted_iota(jnp.int32, (D, D), 0)
    starts = [base + lax.rem(x - d + heads, heads) * D for d in range(heads)]
    flags, rows, owned = [], [], []
    for start in starts:
        pos = start + lane
        point = pos.astype(jnp.float32)
        here = (point >= begins) & (point < ends)
        first = jnp.sum(jnp.where(here, begins, 0.0), axis=0, keepdims=True).astype(jnp.int32)
        finish = jnp.sum(jnp.where(here, ends, 0.0), axis=0, keepdims=True).astype(jnp.int32)
        offset = pos - first
        rows.append(lax.rem(offset, PAGE))
        page_last = jnp.minimum(pos - rows[-1] + PAGE, finish) - 1
        owned.append(page_last < base + heads * D)
        flags.append(jnp.where(pos == page_last, 1.0, 0.0))
    flags = jnp.broadcast_to(jnp.concatenate(flags, axis=1), (16, heads * D)).astype(jnp.bfloat16)
    slot_scr[...] = jnp.zeros_like(slot_scr)
    slot_scr[0:1, 0:pool] = slots[...].astype(jnp.float32)
    slot_row = slot_scr[...].astype(jnp.bfloat16)
    ranks, targets = [], []
    for d, start in enumerate(starts):
        ahead = [jnp.where(other + sub < start + lane, 1.0, 0.0) for other in starts]
        ahead = jnp.concatenate(ahead, axis=0).astype(jnp.bfloat16)
        rank = jnp.dot(flags, ahead, preferred_element_type=jnp.float32)[:1].astype(jnp.int32)
        pick_slot = jnp.where(sub == rank, 1.0, 0.0).astype(jnp.bfloat16)
        slot = jnp.dot(slot_row, pick_slot, preferred_element_type=jnp.float32)[:1]
        row = slot.astype(jnp.int32) * PAGE + rows[d]
        targets.append(jnp.where(owned[d], row, -1))
        ranks.append(jnp.where(owned[d] & (rank == 0), rows[d], -1))
    target = jnp.concatenate(targets, axis=1)
    head_target = jnp.concatenate(ranks, axis=1)

    def marks(first_row, rows, target):
        row = first_row + lax.broadcasted_iota(jnp.int32, (rows, heads * D), 0)
        return jnp.where(row == target, 1.0, 0.0).astype(jnp.bfloat16)

    kvl = own_ref.shape[1] // (2 * D)
    both = []
    for g in range(kvl):
        key_at, value_at = at(2 * g * D), at((2 * g + 1) * D)
        others = [rest_ref[i * D : (i + 1) * D, value_at].T for i in range(heads - 1)]
        key = jnp.concatenate([own_ref[:, key_at], rest_ref[:, key_at]], axis=0)
        value = jnp.concatenate([own_ref[:, value_at].T, *others], axis=0)
        both.append(jnp.concatenate([key, value], axis=1))
    step = 8
    copies = []
    for i, page in enumerate(range(0, pool, step)):
        mark = marks(page * PAGE, step * PAGE, target)
        for g in range(kvl):
            wide_scr[i % 2, :, g, :] = jnp.dot(mark, both[g], preferred_element_type=jnp.float32)
        block = pl.ds(page, step)
        out_scr[block] = (
            wide_scr[i % 2].astype(jnp.bfloat16).reshape(step, PAGE, kvl, 2 * D)
        )
        copies.append(pltpu.make_async_copy(out_scr.at[block], pool_ref.at[block], sems.at[i]))
        copies[-1].start()
    mark = marks(0, PAGE, head_target)
    head = [jnp.dot(mark, part, preferred_element_type=jnp.float32) for part in both]
    head_ref[...] = jnp.stack(head, axis=1).astype(jnp.bfloat16)
    for copy in copies:
        copy.wait()


def pages(table, slots, own, rest, heads, segs):
    pool = slots.shape[1]
    kvl = own.shape[1] // (2 * D)
    return pl.pallas_call(
        functools.partial(pages_body, heads, segs, pool),
        out_shape=[
            jax.ShapeDtypeStruct((pool, PAGE, kvl, 2 * D), jnp.bfloat16),
            jax.ShapeDtypeStruct((PAGE, kvl, 2 * D), jnp.bfloat16),
        ],
        in_specs=[VMEM] * 4,
        out_specs=[ANY, VMEM],
        scratch_shapes=[
            pltpu.VMEM((16, D), jnp.float32),
            pltpu.VMEM((2, 8 * PAGE, kvl, 2 * D), jnp.float32),
            pltpu.VMEM((pool, PAGE, kvl, 2 * D), jnp.bfloat16),
            pltpu.SemaphoreType.DMA((pool // 8,)),
        ],
        compiler_params=params(),
        cost_estimate=cost(0.01),
        name="pages",
    )(table, slots, own, rest)


def pick_body(bit, plan, *refs):
    *ins, out = refs
    side = lax.rem(lax.axis_index("tok") // bit, 2)
    row = 0
    for part in plan:
        rows = ins[part[0]].shape[0]
        to = pl.ds(row, rows)
        if len(part) == 1:
            out[to, :] = ins[part[0]][...]
        else:
            for value, index in enumerate(part):
                @pl.when(side == value)
                def _(index=index, to=to):
                    out[to, :] = ins[index][...]
        row += rows


def pick(bit, plan, *arrays):
    rows = sum(arrays[part[0]].shape[0] for part in plan)
    last = max(max(part) for part in plan)
    return pl.pallas_call(
        functools.partial(pick_body, bit, plan),
        out_shape=jax.ShapeDtypeStruct((rows, arrays[0].shape[1]), jnp.bfloat16),
        in_specs=[ANY if i > last else VMEM for i in range(len(arrays))],
        out_specs=VMEM,
        compiler_params=params(8),
        cost_estimate=cost(0.01),
        name="pick",
    )(*arrays)


def after_body(*refs):
    del refs


def after(x, *earlier):
    return pl.pallas_call(
        after_body,
        out_shape=jax.ShapeDtypeStruct(x.shape, x.dtype),
        in_specs=[ANY] * (1 + len(earlier)),
        out_specs=ANY,
        input_output_aliases={0: 0},
        compiler_params=params(1),
        cost_estimate=cost(0.01),
        name="after",
    )(x, *earlier)


def on_device(queries, key_states, value_states, query_gain, key_gain, lengths, slot_order):
    heads = lax.axis_size("head")
    others = range(1, heads)

    table, own, *away = kv_prep(
        lengths, key_states, value_states, key_gain.reshape(1, D), query_gain.reshape(1, D), heads
    )
    segs = lengths.shape[0]
    rest = join([around(part, "head", d) for d, part in enumerate(away, 1)])
    own4 = around(own, "tok", 4)
    q_own, *q_away, turned = q_prep(queries, table, own, heads, segs)
    q_rest = join([around(part, "head", d) for d, part in enumerate(q_away, 1)])
    rest = after(rest, turned)
    rest4, rest2 = around(rest, "tok", 4), onward(rest, "tok", 2)
    base = [(0, 0, "own", 0)] + [(1, d - 1, "own", d) for d in others]
    [own_state] = attend(table, [q_own], [own, rest], [(0, 0, None, base)], False, heads, segs)

    own4 = after(own4, own_state[0])
    own2 = swap(pick(2, ((0, 1),), own, own4), 2)
    page_pool, head_page = pages(table, slot_order, own, rest, heads, segs)
    own_mixed = pick(1, ((0, 1), (2,)), own, own4, own2, head_page)
    own_s = swap(own_mixed, 1)

    qs = [q_own, q_rest]
    near = [(2, 0, "far", 0), (3, 0, "near", 0)]
    own_state, rest_state = attend(
        table, qs, [own, rest, own4, own2],
        [(0, 0, own_state, near), (1, 1, None, base + near)], False, heads, segs,
        own_mixed,
    )

    rest_mixed = pick(1, ((0, 1), (2,)), rest, rest4, rest2, own_state[0])
    rest_s = swap(rest_mixed, 1)
    pieces = [(2, 0, "mix_swap", 0), (2, 1, "near_swap", 0)]
    pieces += [(0, d - 1, "far", d) for d in others] + [(1, d - 1, "near", d) for d in others]
    own_state, rest_state = attend(
        table, qs, [rest4, rest2, own_s],
        [(0, 0, own_state, pieces), (1, 1, rest_state, pieces)], False, heads, segs, rest_mixed,
    )
    pieces = [(0, d - 1, "mix_swap", d) for d in others]
    pieces += [(0, heads + d - 2, "near_swap", d) for d in others]
    attention, page_pool = attend(
        table, qs, [rest_s],
        [(0, 0, own_state, pieces), (1, 1, rest_state, pieces)], True, heads, segs,
        slot_order, own_s, head_page, page_pool,
    )
    return (attention, page_pool)


def solution(mesh):
    in_specs = (
        P(("tok", "head"), None),
        P(("tok", "head"), None),
        P(("tok", "head"), None),
        P(),
        P(),
        P(),
        P("tok", None),
    )
    out_specs = (P("tok", "head"), P("tok", None, "head", None))
    return jax.shard_map(
        on_device, mesh=mesh, in_specs=in_specs, out_specs=out_specs, check_vma=False
    )
```

```python
import functools
import math

import jax
import jax.numpy as jnp
from jax import lax
from jax.experimental import pallas as pl
from jax.experimental.pallas import tpu as pltpu
from jax.sharding import PartitionSpec as P

D = 128
PAGE = 16
HIDE = -2e30
FLOOR = -1e30
MIB = 1024 * 1024
SCALE = math.log2(math.e) / math.sqrt(D)

VMEM = pl.BlockSpec(memory_space=pltpu.VMEM)
SMEM = pl.BlockSpec(memory_space=pltpu.SMEM)
TOKEN = jax.ShapeDtypeStruct((8, D), jnp.float32)
ANY = pl.BlockSpec(memory_space=pl.ANY)
HBM = pl.BlockSpec(memory_space=pltpu.HBM)


def cost(us):
    return pl.CostEstimate(flops=int(us * 1.15e9), bytes_accessed=0, transcendentals=0)


def params(mib=32):
    return pltpu.CompilerParams(vmem_limit_bytes=mib * MIB)


def around(x, axis, by):
    peers = lax.axis_size(axis)
    return lax.ppermute(x, axis, [(i, (i + by) % peers) for i in range(peers)])


def onward(x, axis, by):
    peers = lax.axis_size(axis)
    return lax.ppermute(x, axis, [(i, i + by) for i in range(peers - by)])


def swap(x, bit):
    peers = lax.axis_size("tok")
    return lax.ppermute(x, "tok", [(i, i ^ bit) for i in range(peers)])


def join(parts):
    return parts[0] if len(parts) == 1 else jnp.concatenate(parts, axis=0)


def at(index):
    return pl.ds(index, D) if isinstance(index, int) else pl.ds(pl.multiple_of(index, D), D)


def seg_first(pos, lengths, segs):
    first = jnp.zeros_like(pos)
    start = jnp.int32(0)
    for s in range(segs):
        first = jnp.where(pos >= start, start, first)
        start = start + lengths[s]
    return first


def seg_bounds(shape, axis, lengths, segs):
    index = lax.broadcasted_iota(jnp.int32, shape, axis)
    begin = jnp.where(index == segs, -(2**30), 2**30)
    end = jnp.zeros(shape, jnp.int32)
    here = jnp.int32(0)
    for s in range(segs):
        begin = jnp.where(index == s, here, begin)
        here = here + lengths[s]
        end = jnp.where(index == s, here, end)
    return begin, end


def rotate(x, cos_gain, sin_gain):
    power = jnp.mean(x * x, axis=0, keepdims=True)
    half = D // 2
    turned = jnp.concatenate([x[half:], x[:half]], axis=0)
    return (x * cos_gain + turned * sin_gain) * lax.rsqrt(power + 1e-06)


def gain_tables(cosine, sine, gain_row):
    gain = jnp.broadcast_to(gain_row, (D, D)).T
    half = D // 2
    turned = jnp.concatenate([gain[half:], gain[:half]], axis=0)
    cos_gain = jnp.concatenate([cosine, cosine], axis=0) * gain
    sin_gain = jnp.concatenate([-sine, sine], axis=0) * turned
    return cos_gain, sin_gain


def table_rows(segs):
    used = (segs + 16) // 16 * 16
    starts = [D]
    for rows in (used, used, 8, 8, 8):
        starts.append(starts[-1] + rows)
    return starts


def kv_prep_body(heads, segs, lengths_in, k_in, v_in, gain_in, q_gain_in, table_ref, *refs):
    outs, (lengths, k_ref, v_ref, gain_ref, q_gain_ref, sems) = refs[:heads], refs[heads:]
    pairs = [(lengths_in, lengths), (gain_in, gain_ref), (k_in, k_ref), (v_in, v_ref)]
    pairs += [(q_gain_in, q_gain_ref)]
    copies = [pltpu.make_async_copy(a, b, sems.at[i]) for i, (a, b) in enumerate(pairs)]
    for copy in copies:
        copy.start()
    rows = k_ref.shape[0]
    kvl = k_ref.shape[1] // D // heads
    x = lax.axis_index("head")
    base = (lax.axis_index("tok") * heads + x) * rows
    half = D // 2
    pos = base + lax.broadcasted_iota(jnp.int32, (half, rows), 1)
    step = lax.broadcasted_iota(jnp.int32, (half, rows), 0).astype(jnp.float32)
    frequency = jnp.exp(step * (-2.0 * math.log(1000000.0) / D))
    copies[0].wait()
    offset = (pos - seg_first(pos, lengths, segs)).astype(jnp.float32)
    angles = offset * frequency
    cosine, sine = jnp.cos(angles), jnp.sin(angles)
    table_ref[:half] = cosine
    table_ref[half:D] = sine
    down, down_end, along, along_end, gain_at, stop = table_rows(segs)
    begin, end = seg_bounds((down_end - down, D), 0, lengths, segs)
    table_ref[down:down_end] = begin.astype(jnp.float32)
    table_ref[down_end:along] = end.astype(jnp.float32)
    begin, end = seg_bounds((8, D), 1, lengths, segs)
    table_ref[along:along_end] = begin.astype(jnp.float32)
    table_ref[along_end:gain_at] = end.astype(jnp.float32)
    copies[4].wait()
    table_ref[gain_at:stop] = jnp.broadcast_to(q_gain_ref[...], (8, D))
    copies[1].wait()
    cos_gain, sin_gain = gain_tables(cosine, sine, gain_ref[...])
    copies[2].wait()
    copies[3].wait()
    for d in reversed(range(heads)):
        peer = lax.rem(x + d, heads)
        for j in range(kvl):
            head = peer * kvl + j
            key = k_ref[:, at(head * D)].T.astype(jnp.float32)
            key = rotate(key, cos_gain, sin_gain).astype(jnp.bfloat16)
            outs[d][:, 2 * j * D : (2 * j + 1) * D] = key.T
            value = v_ref[:, at(head * D)]
            outs[d][:, (2 * j + 1) * D : (2 * j + 2) * D] = value.T


def kv_prep(lengths, keys, values, gain, q_gain, heads):
    rows, width = keys.shape
    table = jax.ShapeDtypeStruct((table_rows(lengths.shape[0])[-1], rows), jnp.float32)
    part = jax.ShapeDtypeStruct((rows, 2 * width // heads), jnp.bfloat16)
    return pl.pallas_call(
        functools.partial(kv_prep_body, heads, lengths.shape[0]),
        out_shape=[table] + [part] * heads,
        in_specs=[HBM] * 5,
        out_specs=[VMEM] * (1 + heads),
        scratch_shapes=[
            pltpu.SMEM(lengths.shape, jnp.int32),
            pltpu.VMEM(keys.shape, jnp.bfloat16),
            pltpu.VMEM(values.shape, jnp.bfloat16),
            pltpu.VMEM(gain.shape, jnp.float32),
            pltpu.VMEM(gain.shape, jnp.float32),
            pltpu.SemaphoreType.DMA((5,)),
        ],
        compiler_params=params(62),
        cost_estimate=cost(0.01),
        name="kv_prep",
    )(lengths, keys, values, gain, q_gain)


def q_prep_body(heads, segs, q_ref, table_ref, own_ref, *refs):
    del own_ref
    *outs, token = refs
    token[...] = jnp.zeros_like(token)
    ql = q_ref.shape[1] // D // heads
    x = lax.axis_index("head")
    half = D // 2
    cos_gain, sin_gain = gain_tables(table_ref[:half], table_ref[half:D], table_ref[pl.ds(table_rows(segs)[4], 1), :])
    for d in reversed(range(heads)):
        peer = lax.rem(x + d, heads)
        for j in range(ql):
            query = q_ref[:, at((peer * ql + j) * D)].T.astype(jnp.float32)
            outs[d][j * D : (j + 1) * D, :] = rotate(query, cos_gain, sin_gain).astype(
                jnp.bfloat16
            )


def q_prep(queries, table, own, heads, segs):
    rows, width = queries.shape
    part = jax.ShapeDtypeStruct((width // heads, rows), jnp.bfloat16)
    return pl.pallas_call(
        functools.partial(q_prep_body, heads, segs),
        out_shape=[part] * heads + [TOKEN],
        in_specs=[VMEM] * 3,
        out_specs=[VMEM] * (heads + 1),
        compiler_params=params(),
        cost_estimate=cost(0.01),
        name="q_prep",
    )(queries, table, own)


def shard_of(kind, tok):
    core = lax.rem(tok, 2)
    if kind == "own":
        return tok
    if kind == "far":
        return tok - 4
    if kind == "near":
        return tok - 2
    if kind == "near_swap":
        return tok - 1 - 2 * core
    return jnp.where(core == 0, tok - 3, tok - 1)


def attend_body(heads, segs, jobs, last, counts, table, *refs):
    n_q, n_kv, n_state, n_earlier = counts
    q_refs, refs = refs[:n_q], refs[n_q:]
    kv_refs, refs = refs[:n_kv], refs[n_kv:]
    states, refs = refs[: 3 * n_state], refs[3 * n_state :]
    earlier, refs = refs[:n_earlier], refs[n_earlier:]
    n_out = 2 if last else 3 * len(jobs)
    outs, (s_scr, p_scr, e_scr, f_scr, *page) = refs[:n_out], refs[n_out:]
    if last:
        out_scr, out_sems, *page = page
    bufs = s_scr.shape[0]
    x = lax.axis_index("head")
    tok = lax.axis_index("tok")
    rows = D
    kvl = kv_refs[0].shape[1] // (2 * D)
    ql = f_scr.shape[2] // D * kvl
    group = ql // kvl
    wide = group * rows
    lane = lax.broadcasted_iota(jnp.int32, (rows, rows), 1)
    sub = lax.broadcasted_iota(jnp.int32, (rows, rows), 0)
    down, down_end, along, along_end, _, _ = table_rows(segs)
    used = down_end - down
    query_begin = table[down:down_end].astype(jnp.int32)
    query_end = table[down_end:along].astype(jnp.int32)
    key_begin = table[along : along + 1].astype(jnp.int32)
    key_end = table[along_end : along_end + 1].astype(jnp.int32)

    def key_block(pieces, g, side, axis):
        cols = at((2 * g + side) * D)
        return jnp.concatenate(
            [kv_refs[a][row * rows : (row + 1) * rows, cols] for a, row, _, _ in pieces],
            axis=axis,
        )

    def out_part(origin, g):
        part = at(origin * rows), pl.ds(g * group * D, group * D)
        sem = out_sems.at[origin, g]
        return pltpu.make_async_copy(out_scr.at[part], outs[0].at[part], sem)

    def prepare(slot, job, c, known):
        _, first, _, _, pieces = jobs[job]
        d = first + c
        origin = lax.rem(x - d + heads, heads)
        q_chunk = tok * heads + origin
        q_pos = q_chunk * rows + lane[:used]
        outside = jnp.where((q_pos >= query_begin) & (q_pos < query_end), 0.0, HIDE)
        outside = jnp.concatenate([outside, jnp.zeros((D - used, D), jnp.float32)], axis=0)
        f_scr[slot] = jnp.concatenate([outside.astype(jnp.bfloat16)] * group, axis=1)
        for i, (a, row, kind, kd) in enumerate(pieces):
            if kind != "own" and (a, row, kind, kd) in known:
                from_slot, j = known[a, row, kind, kd]
                e_scr[slot, i * rows : (i + 1) * rows, :] = e_scr[
                    from_slot, j * rows : (j + 1) * rows, :
                ]
                continue
            known[a, row, kind, kd] = (slot, i)
            k_chunk = shard_of(kind, tok) * heads + lax.rem(x - kd + heads, heads)
            k_pos = jnp.where(k_chunk <= q_chunk, k_chunk * rows + sub, -1)
            inside = (k_pos >= key_begin) & (k_pos < key_end)
            e_scr[slot, i * rows : (i + 1) * rows, :] = jnp.where(inside, 1.0, 0.0).astype(
                jnp.bfloat16
            )
        return origin

    def scores(buf, slot, job, c, g):
        q, first, _, s, pieces = jobs[job]
        d = first + c
        n = len(pieces)
        query = jnp.concatenate(
            [q_refs[q][at((c * ql + g * group + r) * D), :] for r in range(group)], axis=1
        )
        query = jnp.concatenate([query, f_scr[slot]], axis=0)
        keys = jnp.concatenate([key_block(pieces, g, 0, 0), e_scr[slot, : n * rows, :]], axis=1)
        score = jnp.dot(keys, query, preferred_element_type=jnp.float32)
        if s is None:
            top = jnp.full((8, wide), FLOOR, jnp.float32)
        else:
            top = jnp.broadcast_to(states[3 * s][c, g], (8, wide))
        for i, (a, row, kind, kd) in enumerate(pieces):
            block = score[i * rows : (i + 1) * rows]
            if kind == "own" and (not isinstance(d, int) or kd == d):
                late = jnp.where((sub > lane) & (kd == d), HIDE, 0.0)
                block = block + jnp.concatenate([late] * group, axis=1)
            s_scr[buf, i * rows : (i + 1) * rows, :] = block
            top = jnp.maximum(top, jnp.max(block.reshape(rows // 8, 8, wide), axis=0))
        return jnp.max(top, axis=0, keepdims=True)

    def weigh(buf, job, top):
        part = jnp.zeros((8, wide), jnp.float32)
        for i in range(len(jobs[job][4])):
            expo = jnp.exp2((s_scr[buf, i * rows : (i + 1) * rows, :] - top) * SCALE)
            part = part + jnp.sum(expo.reshape(rows // 8, 8, wide), axis=0)
            p_scr[buf, i * rows : (i + 1) * rows, :] = expo.astype(jnp.bfloat16)
        return jnp.sum(part, axis=0, keepdims=True)

    def mix(buf, job, c, g, origin, top, total):
        _, _, _, s, pieces = jobs[job]
        acc = jnp.dot(
            key_block(pieces, g, 1, 1),
            p_scr[buf, : len(pieces) * rows, :],
            preferred_element_type=jnp.float32,
        )
        if s is not None:
            fade = jnp.exp2((states[3 * s][c, g] - top) * SCALE)
            total = total + states[3 * s + 1][c, g] * fade
            acc = acc + states[3 * s + 2][c, g] * fade
        if last:
            acc = (acc * (1.0 / total)).astype(jnp.bfloat16)
            for r in range(group):
                out_scr[at(origin * rows), (g * group + r) * D : (g * group + r + 1) * D] = acc[
                    :, r * rows : (r + 1) * rows
                ].T
            part = out_part(origin, g)
            part.start()
        else:
            outs[3 * job][c, g] = top
            outs[3 * job + 1][c, g] = total
            outs[3 * job + 2][c, g] = acc

    def sweep(chunks):
        known = {}
        origins = [prepare(slot, job, c, known) for slot, (job, c) in enumerate(chunks)]
        units = [(slot, g) for slot in range(len(chunks)) for g in range(kvl)]
        tops, totals = {}, {}
        for i in range(len(units) + 2):
            if i < len(units):
                slot, g = units[i]
                tops[i] = scores(i % bufs, slot, *chunks[slot], g)
            if 0 <= i - 1 < len(units):
                slot, g = units[i - 1]
                totals[i - 1] = weigh((i - 1) % bufs, chunks[slot][0], tops[i - 1])
            if 0 <= i - 2 < len(units):
                slot, g = units[i - 2]
                job, c = chunks[slot]
                mix((i - 2) % bufs, job, c, g, origins[slot], tops[i - 2], totals[i - 2])

    if last:
        before, slot = partial_place(heads, query_begin, query_end, earlier[0])
    if max(job[2] for job in jobs) == 1:
        sweep([(job, 0) for job in range(len(jobs))])
    else:
        for job in range(len(jobs)):
            def body(c, carry, job=job):
                sweep([(job, c)])
                return carry

            lax.fori_loop(0, jobs[job][2], body, 0)
    if last:
        _, own_s, head_ref, _ = earlier
        finish = partial_page(heads, before, slot, own_s, kv_refs[0], head_ref, outs[1], *page)
        for origin in range(heads):
            for g in range(kvl):
                out_part(origin, g).wait()
        finish()


def partial_place(heads, begins, ends, slots):
    base = lax.axis_index("tok") * heads * D
    here = (begins <= base) & (base < ends)
    first = jnp.max(jnp.where(here, begins.astype(jnp.float32), 0.0)).astype(jnp.int32)
    before = lax.rem(base - first, PAGE)
    slot = jnp.max(slots[:, :1].astype(jnp.float32)).astype(jnp.int32)
    return before, slot


def partial_page(heads, before, slot, own_s, rest_s, head_ref, pool_ref, page, sem):
    x = lax.axis_index("head")
    core = lax.rem(lax.axis_index("tok"), 2)
    kvl = head_ref.shape[1]
    d = lax.rem(x + 1, heads)
    lane = lax.broadcasted_iota(jnp.int32, (PAGE, PAGE), 1)
    sub = lax.broadcasted_iota(jnp.int32, (PAGE, PAGE), 0)
    move = jnp.where((lane == sub + PAGE - before) & (sub < before), 1.0, 0.0).astype(jnp.bfloat16)
    copy = pltpu.make_async_copy(page, pool_ref.at[slot], sem)

    def write(ref, row):
        moved = []
        for g in range(kvl):
            at_row = pl.ds(pl.multiple_of(row + D - PAGE, PAGE), PAGE)
            key = ref[at_row, 2 * g * D : (2 * g + 1) * D]
            value = ref[at(row), (2 * g + 1) * D : (2 * g + 2) * D].T[D - PAGE :]
            both = jnp.concatenate([key, value], axis=1)
            moved.append(jnp.dot(move, both, preferred_element_type=jnp.float32))
        moved = jnp.stack(moved, axis=1)
        index = lax.broadcasted_iota(jnp.int32, moved.shape, 0)
        page[...] = jnp.where(index < before, moved, head_ref[...].astype(jnp.float32)).astype(
            jnp.bfloat16
        )
        copy.start()

    @pl.when((before > 0) & (d == 0))
    def _():
        write(own_s, (1 - core) * D)

    @pl.when((before > 0) & (d > 0))
    def _():
        write(rest_s, jnp.maximum(d - 1, 0) * D + (1 - core) * (heads - 1) * D)

    def finish():
        @pl.when(before > 0)
        def _():
            copy.wait()

    return finish


def attend(table, qs, kvs, jobs, last, heads, segs, *earlier):
    kvl = kvs[0].shape[1] // (2 * D)
    states, plan = [], []
    for q, first, state, pieces in jobs:
        many = 1 if first == 0 else heads - 1
        plan.append((q, first, many, None if state is None else len(states), tuple(pieces)))
        if state is not None:
            states.append(state)
    ql = qs[plan[0][0]].shape[0] // D // plan[0][2]
    wide = ql // kvl * D
    if last:
        pool = earlier[3]
        out_shape = [jax.ShapeDtypeStruct((heads * D, ql * D), jnp.bfloat16)]
        out_shape += [jax.ShapeDtypeStruct(pool.shape, pool.dtype)]
    else:
        out_shape = []
        for _, _, many, _, _ in plan:
            row = jax.ShapeDtypeStruct((many, kvl, 1, wide), jnp.float32)
            out_shape += [row, row, jax.ShapeDtypeStruct((many, kvl, D, wide), jnp.float32)]
    inputs = [table, *qs, *kvs, *[part for state in states for part in state], *earlier]
    more = [VMEM, VMEM, VMEM, ANY] if last else [ANY] * len(earlier)
    keys = max(len(job[4]) for job in plan) * D
    together = len(plan) if heads == 2 else 1
    bufs = min(3, kvl * together)
    result = pl.pallas_call(
        functools.partial(
            attend_body, heads, segs, tuple(plan), last,
            (len(qs), len(kvs), len(states), len(earlier)),
        ),
        out_shape=out_shape,
        in_specs=[VMEM] * (len(inputs) - len(earlier)) + more,
        out_specs=[ANY, ANY] if last else [VMEM] * len(out_shape),
        input_output_aliases={len(inputs) - 1: 1} if last else {},
        scratch_shapes=[
            pltpu.VMEM((bufs, keys, wide), jnp.float32),
            pltpu.VMEM((bufs, keys, wide), jnp.bfloat16),
            pltpu.VMEM((together, keys, D), jnp.bfloat16),
            pltpu.VMEM((together, D, wide), jnp.bfloat16),
        ]
        + (
            [
                pltpu.VMEM(out_shape[0].shape, jnp.bfloat16),
                pltpu.SemaphoreType.DMA((heads, kvl)),
                pltpu.VMEM(pool.shape[1:], pool.dtype),
                pltpu.SemaphoreType.DMA,
            ]
            if last
            else []
        ),
        compiler_params=params(),
        cost_estimate=cost(0.01),
        name="attend_last" if last else "attend_part",
    )(*inputs)
    return result if last else [result[i : i + 3] for i in range(0, len(result), 3)]


def pages_body(
    heads, segs, pool, table, slots, own_ref, rest_ref, pool_ref, head_ref,
    slot_scr, wide_scr, out_scr, sems,
):
    x = lax.axis_index("head")
    base = lax.axis_index("tok") * heads * D
    down, down_end, along, _, _, _ = table_rows(segs)
    begins, ends = table[down:down_end], table[down_end:along]
    lane = lax.broadcasted_iota(jnp.int32, (1, D), 1)
    sub = lax.broadcasted_iota(jnp.int32, (D, D), 0)
    starts = [base + lax.rem(x - d + heads, heads) * D for d in range(heads)]
    flags, rows, owned = [], [], []
    for start in starts:
        pos = start + lane
        point = pos.astype(jnp.float32)
        here = (point >= begins) & (point < ends)
        first = jnp.sum(jnp.where(here, begins, 0.0), axis=0, keepdims=True).astype(jnp.int32)
        finish = jnp.sum(jnp.where(here, ends, 0.0), axis=0, keepdims=True).astype(jnp.int32)
        offset = pos - first
        rows.append(lax.rem(offset, PAGE))
        page_last = jnp.minimum(pos - rows[-1] + PAGE, finish) - 1
        owned.append(page_last < base + heads * D)
        flags.append(jnp.where(pos == page_last, 1.0, 0.0))
    flags = jnp.broadcast_to(jnp.concatenate(flags, axis=1), (16, heads * D)).astype(jnp.bfloat16)
    slot_scr[...] = jnp.zeros_like(slot_scr)
    slot_scr[0:1, 0:pool] = slots[...].astype(jnp.float32)
    slot_row = slot_scr[...].astype(jnp.bfloat16)
    ranks, targets = [], []
    for d, start in enumerate(starts):
        ahead = [jnp.where(other + sub < start + lane, 1.0, 0.0) for other in starts]
        ahead = jnp.concatenate(ahead, axis=0).astype(jnp.bfloat16)
        rank = jnp.dot(flags, ahead, preferred_element_type=jnp.float32)[:1].astype(jnp.int32)
        pick_slot = jnp.where(sub == rank, 1.0, 0.0).astype(jnp.bfloat16)
        slot = jnp.dot(slot_row, pick_slot, preferred_element_type=jnp.float32)[:1]
        row = slot.astype(jnp.int32) * PAGE + rows[d]
        targets.append(jnp.where(owned[d], row, -1))
        ranks.append(jnp.where(owned[d] & (rank == 0), rows[d], -1))
    target = jnp.concatenate(targets, axis=1)
    head_target = jnp.concatenate(ranks, axis=1)

    def marks(first_row, rows, target):
        row = first_row + lax.broadcasted_iota(jnp.int32, (rows, heads * D), 0)
        return jnp.where(row == target, 1.0, 0.0).astype(jnp.bfloat16)

    kvl = own_ref.shape[1] // (2 * D)
    both = []
    for g in range(kvl):
        key_at, value_at = at(2 * g * D), at((2 * g + 1) * D)
        others = [rest_ref[i * D : (i + 1) * D, value_at].T for i in range(heads - 1)]
        key = jnp.concatenate([own_ref[:, key_at], rest_ref[:, key_at]], axis=0)
        value = jnp.concatenate([own_ref[:, value_at].T, *others], axis=0)
        both.append(jnp.concatenate([key, value], axis=1))
    step = 8
    copies = []
    for i, page in enumerate(range(0, pool, step)):
        mark = marks(page * PAGE, step * PAGE, target)
        for g in range(kvl):
            wide_scr[i % 2, :, g, :] = jnp.dot(mark, both[g], preferred_element_type=jnp.float32)
        block = pl.ds(page, step)
        out_scr[block] = (
            wide_scr[i % 2].astype(jnp.bfloat16).reshape(step, PAGE, kvl, 2 * D)
        )
        copies.append(pltpu.make_async_copy(out_scr.at[block], pool_ref.at[block], sems.at[i]))
        copies[-1].start()
    mark = marks(0, PAGE, head_target)
    head = [jnp.dot(mark, part, preferred_element_type=jnp.float32) for part in both]
    head_ref[...] = jnp.stack(head, axis=1).astype(jnp.bfloat16)
    for copy in copies:
        copy.wait()


def pages(table, slots, own, rest, heads, segs):
    pool = slots.shape[1]
    kvl = own.shape[1] // (2 * D)
    return pl.pallas_call(
        functools.partial(pages_body, heads, segs, pool),
        out_shape=[
            jax.ShapeDtypeStruct((pool, PAGE, kvl, 2 * D), jnp.bfloat16),
            jax.ShapeDtypeStruct((PAGE, kvl, 2 * D), jnp.bfloat16),
        ],
        in_specs=[VMEM] * 4,
        out_specs=[ANY, VMEM],
        scratch_shapes=[
            pltpu.VMEM((16, D), jnp.float32),
            pltpu.VMEM((2, 8 * PAGE, kvl, 2 * D), jnp.float32),
            pltpu.VMEM((pool, PAGE, kvl, 2 * D), jnp.bfloat16),
            pltpu.SemaphoreType.DMA((pool // 8,)),
        ],
        compiler_params=params(),
        cost_estimate=cost(0.01),
        name="pages",
    )(table, slots, own, rest)


def pick_body(bit, plan, *refs):
    *ins, out = refs
    side = lax.rem(lax.axis_index("tok") // bit, 2)
    row = 0
    for part in plan:
        rows = ins[part[0]].shape[0]
        to = pl.ds(row, rows)
        if len(part) == 1:
            out[to, :] = ins[part[0]][...]
        else:
            for value, index in enumerate(part):
                @pl.when(side == value)
                def _(index=index, to=to):
                    out[to, :] = ins[index][...]
        row += rows


def pick(bit, plan, *arrays):
    rows = sum(arrays[part[0]].shape[0] for part in plan)
    last = max(max(part) for part in plan)
    return pl.pallas_call(
        functools.partial(pick_body, bit, plan),
        out_shape=jax.ShapeDtypeStruct((rows, arrays[0].shape[1]), jnp.bfloat16),
        in_specs=[ANY if i > last else VMEM for i in range(len(arrays))],
        out_specs=VMEM,
        compiler_params=params(8),
        cost_estimate=cost(0.01),
        name="pick",
    )(*arrays)


def after_body(*refs):
    del refs


def after(x, *earlier):
    return pl.pallas_call(
        after_body,
        out_shape=jax.ShapeDtypeStruct(x.shape, x.dtype),
        in_specs=[ANY] * (1 + len(earlier)),
        out_specs=ANY,
        input_output_aliases={0: 0},
        compiler_params=params(1),
        cost_estimate=cost(0.01),
        name="after",
    )(x, *earlier)


def on_device(queries, key_states, value_states, query_gain, key_gain, lengths, slot_order):
    heads = lax.axis_size("head")
    others = range(1, heads)

    table, own, *away = kv_prep(
        lengths, key_states, value_states, key_gain.reshape(1, D), query_gain.reshape(1, D), heads
    )
    segs = lengths.shape[0]
    rest = join([around(part, "head", d) for d, part in enumerate(away, 1)])
    own4 = around(own, "tok", 4)
    q_own, *q_away, turned = q_prep(queries, table, own, heads, segs)
    q_rest = join([around(part, "head", d) for d, part in enumerate(q_away, 1)])
    rest = after(rest, turned)
    rest4, rest2 = around(rest, "tok", 4), onward(rest, "tok", 2)
    base = [(0, 0, "own", 0)] + [(1, d - 1, "own", d) for d in others]
    [own_state] = attend(table, [q_own], [own, rest], [(0, 0, None, base)], False, heads, segs)

    own4 = after(own4, rest)
    own2 = swap(pick(2, ((0, 1),), own, own4), 2)
    page_pool, head_page = pages(table, slot_order, own, rest, heads, segs)
    own_mixed = pick(1, ((0, 1), (2,)), own, own4, own2, head_page, own_state[0])
    own_s = swap(own_mixed, 1)

    qs = [q_own, q_rest]
    near = [(2, 0, "far", 0), (3, 0, "near", 0)]
    own_state, rest_state = attend(
        table, qs, [own, rest, own4, own2],
        [(0, 0, own_state, near), (1, 1, None, base + near)], False, heads, segs,
        own_mixed,
    )

    rest_mixed = pick(1, ((0, 1), (2,)), rest, rest4, rest2, own_state[0])
    rest_s = swap(rest_mixed, 1)
    pieces = [(2, 0, "mix_swap", 0), (2, 1, "near_swap", 0)]
    pieces += [(0, d - 1, "far", d) for d in others] + [(1, d - 1, "near", d) for d in others]
    own_state, rest_state = attend(
        table, qs, [rest4, rest2, own_s],
        [(0, 0, own_state, pieces), (1, 1, rest_state, pieces)], False, heads, segs, rest_mixed,
    )
    pieces = [(0, d - 1, "mix_swap", d) for d in others]
    pieces += [(0, heads + d - 2, "near_swap", d) for d in others]
    attention, page_pool = attend(
        table, qs, [rest_s],
        [(0, 0, own_state, pieces), (1, 1, rest_state, pieces)], True, heads, segs,
        slot_order, own_s, head_page, page_pool,
    )
    return (attention, page_pool)


def solution(mesh):
    in_specs = (
        P(("tok", "head"), None),
        P(("tok", "head"), None),
        P(("tok", "head"), None),
        P(),
        P(),
        P(),
        P("tok", None),
    )
    out_specs = (P("tok", "head"), P("tok", None, "head", None))
    return jax.shard_map(
        on_device, mesh=mesh, in_specs=in_specs, out_specs=out_specs, check_vma=False
    )
```

```python
import functools
import math

import jax
import jax.numpy as jnp
from jax import lax
from jax.experimental import pallas as pl
from jax.experimental.pallas import tpu as pltpu
from jax.sharding import PartitionSpec as P

D = 128
PAGE = 16
HIDE = -2e30
FLOOR = -1e30
MIB = 1024 * 1024
SCALE = math.log2(math.e) / math.sqrt(D)

VMEM = pl.BlockSpec(memory_space=pltpu.VMEM)
SMEM = pl.BlockSpec(memory_space=pltpu.SMEM)
TOKEN = jax.ShapeDtypeStruct((8, D), jnp.float32)
ANY = pl.BlockSpec(memory_space=pl.ANY)
HBM = pl.BlockSpec(memory_space=pltpu.HBM)


def cost(us):
    return pl.CostEstimate(flops=int(us * 1.15e9), bytes_accessed=0, transcendentals=0)


def params(mib=32):
    return pltpu.CompilerParams(vmem_limit_bytes=mib * MIB)


def around(x, axis, by):
    peers = lax.axis_size(axis)
    return lax.ppermute(x, axis, [(i, (i + by) % peers) for i in range(peers)])


def onward(x, axis, by):
    peers = lax.axis_size(axis)
    return lax.ppermute(x, axis, [(i, i + by) for i in range(peers - by)])


def swap(x, bit):
    peers = lax.axis_size("tok")
    return lax.ppermute(x, "tok", [(i, i ^ bit) for i in range(peers)])


def join(parts):
    return parts[0] if len(parts) == 1 else jnp.concatenate(parts, axis=0)


def at(index):
    return pl.ds(index, D) if isinstance(index, int) else pl.ds(pl.multiple_of(index, D), D)


def seg_first(pos, lengths, segs):
    first = jnp.zeros_like(pos)
    start = jnp.int32(0)
    for s in range(segs):
        first = jnp.where(pos >= start, start, first)
        start = start + lengths[s]
    return first


def seg_bounds(shape, axis, lengths, segs):
    index = lax.broadcasted_iota(jnp.int32, shape, axis)
    begin = jnp.where(index == segs, -(2**30), 2**30)
    end = jnp.zeros(shape, jnp.int32)
    here = jnp.int32(0)
    for s in range(segs):
        begin = jnp.where(index == s, here, begin)
        here = here + lengths[s]
        end = jnp.where(index == s, here, end)
    return begin, end


def rotate(x, cos_gain, sin_gain):
    power = jnp.mean(x * x, axis=0, keepdims=True)
    half = D // 2
    turned = jnp.concatenate([x[half:], x[:half]], axis=0)
    return (x * cos_gain + turned * sin_gain) * lax.rsqrt(power + 1e-06)


def gain_tables(cosine, sine, gain_row):
    gain = jnp.broadcast_to(gain_row, (D, D)).T
    half = D // 2
    turned = jnp.concatenate([gain[half:], gain[:half]], axis=0)
    cos_gain = jnp.concatenate([cosine, cosine], axis=0) * gain
    sin_gain = jnp.concatenate([-sine, sine], axis=0) * turned
    return cos_gain, sin_gain


def table_rows(segs):
    used = (segs + 16) // 16 * 16
    starts = [D]
    for rows in (used, used, 8, 8, 8):
        starts.append(starts[-1] + rows)
    return starts


def kv_prep_body(heads, segs, lengths_in, k_in, v_in, gain_in, q_gain_in, table_out, *refs):
    results, refs = refs[:heads], refs[heads:]
    lengths, k_ref, v_ref, gain_ref, q_gain_ref, sems, table_ref, *outs, out_sems = refs
    pairs = [(lengths_in, lengths), (gain_in, gain_ref), (k_in, k_ref), (v_in, v_ref)]
    pairs += [(q_gain_in, q_gain_ref)]
    copies = [pltpu.make_async_copy(a, b, sems.at[i]) for i, (a, b) in enumerate(pairs)]
    for copy in copies:
        copy.start()
    rows = k_ref.shape[0]
    kvl = k_ref.shape[1] // D // heads
    x = lax.axis_index("head")
    base = (lax.axis_index("tok") * heads + x) * rows
    half = D // 2
    pos = base + lax.broadcasted_iota(jnp.int32, (half, rows), 1)
    step = lax.broadcasted_iota(jnp.int32, (half, rows), 0).astype(jnp.float32)
    frequency = jnp.exp(step * (-2.0 * math.log(1000000.0) / D))
    copies[0].wait()
    offset = (pos - seg_first(pos, lengths, segs)).astype(jnp.float32)
    angles = offset * frequency
    cosine, sine = jnp.cos(angles), jnp.sin(angles)
    table_ref[:half] = cosine
    table_ref[half:D] = sine
    down, down_end, along, along_end, gain_at, stop = table_rows(segs)
    begin, end = seg_bounds((down_end - down, D), 0, lengths, segs)
    table_ref[down:down_end] = begin.astype(jnp.float32)
    table_ref[down_end:along] = end.astype(jnp.float32)
    begin, end = seg_bounds((8, D), 1, lengths, segs)
    table_ref[along:along_end] = begin.astype(jnp.float32)
    table_ref[along_end:gain_at] = end.astype(jnp.float32)
    copies[4].wait()
    table_ref[gain_at:stop] = jnp.broadcast_to(q_gain_ref[...], (8, D))
    sends = [pltpu.make_async_copy(table_ref, table_out, out_sems.at[heads])]
    sends[0].start()
    copies[1].wait()
    cos_gain, sin_gain = gain_tables(cosine, sine, gain_ref[...])
    copies[2].wait()
    copies[3].wait()
    for d in reversed(range(heads)):
        peer = lax.rem(x + d, heads)
        for j in range(kvl):
            head = peer * kvl + j
            key = k_ref[:, at(head * D)].T.astype(jnp.float32)
            key = rotate(key, cos_gain, sin_gain).astype(jnp.bfloat16)
            outs[d][:, 2 * j * D : (2 * j + 1) * D] = key.T
            value = v_ref[:, at(head * D)]
            outs[d][:, (2 * j + 1) * D : (2 * j + 2) * D] = value.T
        sends.append(pltpu.make_async_copy(outs[d], results[d], out_sems.at[d]))
        sends[-1].start()
    for send in sends:
        send.wait()


def kv_prep(lengths, keys, values, gain, q_gain, heads):
    rows, width = keys.shape
    table = jax.ShapeDtypeStruct((table_rows(lengths.shape[0])[-1], rows), jnp.float32)
    part = jax.ShapeDtypeStruct((rows, 2 * width // heads), jnp.bfloat16)
    return pl.pallas_call(
        functools.partial(kv_prep_body, heads, lengths.shape[0]),
        out_shape=[table] + [part] * heads,
        in_specs=[HBM] * 5,
        out_specs=[HBM] * (1 + heads),
        scratch_shapes=[
            pltpu.SMEM(lengths.shape, jnp.int32),
            pltpu.VMEM(keys.shape, jnp.bfloat16),
            pltpu.VMEM(values.shape, jnp.bfloat16),
            pltpu.VMEM(gain.shape, jnp.float32),
            pltpu.VMEM(gain.shape, jnp.float32),
            pltpu.SemaphoreType.DMA((5,)),
            pltpu.VMEM(table.shape, jnp.float32),
            *[pltpu.VMEM(part.shape, jnp.bfloat16)] * heads,
            pltpu.SemaphoreType.DMA((heads + 1,)),
        ],
        compiler_params=params(62),
        cost_estimate=cost(0.01),
        name="kv_prep",
    )(lengths, keys, values, gain, q_gain)


def q_prep_body(heads, segs, q_ref, table_ref, own_ref, *refs):
    del own_ref
    *outs, token = refs
    token[...] = jnp.zeros_like(token)
    ql = q_ref.shape[1] // D // heads
    x = lax.axis_index("head")
    half = D // 2
    cos_gain, sin_gain = gain_tables(table_ref[:half], table_ref[half:D], table_ref[pl.ds(table_rows(segs)[4], 1), :])
    for d in reversed(range(heads)):
        peer = lax.rem(x + d, heads)
        for j in range(ql):
            query = q_ref[:, at((peer * ql + j) * D)].T.astype(jnp.float32)
            outs[d][j * D : (j + 1) * D, :] = rotate(query, cos_gain, sin_gain).astype(
                jnp.bfloat16
            )


def q_prep(queries, table, own, heads, segs):
    rows, width = queries.shape
    part = jax.ShapeDtypeStruct((width // heads, rows), jnp.bfloat16)
    return pl.pallas_call(
        functools.partial(q_prep_body, heads, segs),
        out_shape=[part] * heads + [TOKEN],
        in_specs=[VMEM] * 3,
        out_specs=[VMEM] * (heads + 1),
        compiler_params=params(),
        cost_estimate=cost(0.01),
        name="q_prep",
    )(queries, table, own)


def shard_of(kind, tok):
    core = lax.rem(tok, 2)
    if kind == "own":
        return tok
    if kind == "far":
        return tok - 4
    if kind == "near":
        return tok - 2
    if kind == "near_swap":
        return tok - 1 - 2 * core
    return jnp.where(core == 0, tok - 3, tok - 1)


def attend_body(heads, segs, jobs, last, counts, table, *refs):
    n_q, n_kv, n_state, n_earlier = counts
    q_refs, refs = refs[:n_q], refs[n_q:]
    kv_refs, refs = refs[:n_kv], refs[n_kv:]
    states, refs = refs[: 3 * n_state], refs[3 * n_state :]
    earlier, refs = refs[:n_earlier], refs[n_earlier:]
    n_out = 2 if last else 3 * len(jobs)
    outs, (s_scr, p_scr, e_scr, f_scr, *page) = refs[:n_out], refs[n_out:]
    if last:
        out_scr, out_sems, *page = page
    bufs = s_scr.shape[0]
    x = lax.axis_index("head")
    tok = lax.axis_index("tok")
    rows = D
    kvl = kv_refs[0].shape[1] // (2 * D)
    ql = f_scr.shape[2] // D * kvl
    group = ql // kvl
    wide = group * rows
    lane = lax.broadcasted_iota(jnp.int32, (rows, rows), 1)
    sub = lax.broadcasted_iota(jnp.int32, (rows, rows), 0)
    down, down_end, along, along_end, _, _ = table_rows(segs)
    used = down_end - down
    query_begin = table[down:down_end].astype(jnp.int32)
    query_end = table[down_end:along].astype(jnp.int32)
    key_begin = table[along : along + 1].astype(jnp.int32)
    key_end = table[along_end : along_end + 1].astype(jnp.int32)

    def key_block(pieces, g, side, axis):
        cols = at((2 * g + side) * D)
        return jnp.concatenate(
            [kv_refs[a][row * rows : (row + 1) * rows, cols] for a, row, _, _ in pieces],
            axis=axis,
        )

    def out_part(origin, g):
        part = at(origin * rows), pl.ds(g * group * D, group * D)
        sem = out_sems.at[origin, g]
        return pltpu.make_async_copy(out_scr.at[part], outs[0].at[part], sem)

    def prepare(slot, job, c, known):
        _, first, _, _, pieces = jobs[job]
        d = first + c
        origin = lax.rem(x - d + heads, heads)
        q_chunk = tok * heads + origin
        q_pos = q_chunk * rows + lane[:used]
        outside = jnp.where((q_pos >= query_begin) & (q_pos < query_end), 0.0, HIDE)
        outside = jnp.concatenate([outside, jnp.zeros((D - used, D), jnp.float32)], axis=0)
        f_scr[slot] = jnp.concatenate([outside.astype(jnp.bfloat16)] * group, axis=1)
        for i, (a, row, kind, kd) in enumerate(pieces):
            if kind != "own" and (a, row, kind, kd) in known:
                from_slot, j = known[a, row, kind, kd]
                e_scr[slot, i * rows : (i + 1) * rows, :] = e_scr[
                    from_slot, j * rows : (j + 1) * rows, :
                ]
                continue
            known[a, row, kind, kd] = (slot, i)
            k_chunk = shard_of(kind, tok) * heads + lax.rem(x - kd + heads, heads)
            k_pos = jnp.where(k_chunk <= q_chunk, k_chunk * rows + sub, -1)
            inside = (k_pos >= key_begin) & (k_pos < key_end)
            e_scr[slot, i * rows : (i + 1) * rows, :] = jnp.where(inside, 1.0, 0.0).astype(
                jnp.bfloat16
            )
        return origin

    def scores(buf, slot, job, c, g):
        q, first, _, s, pieces = jobs[job]
        d = first + c
        n = len(pieces)
        query = jnp.concatenate(
            [q_refs[q][at((c * ql + g * group + r) * D), :] for r in range(group)], axis=1
        )
        query = jnp.concatenate([query, f_scr[slot]], axis=0)
        keys = jnp.concatenate([key_block(pieces, g, 0, 0), e_scr[slot, : n * rows, :]], axis=1)
        score = jnp.dot(keys, query, preferred_element_type=jnp.float32)
        if s is None:
            top = jnp.full((8, wide), FLOOR, jnp.float32)
        else:
            top = jnp.broadcast_to(states[3 * s][c, g], (8, wide))
        for i, (a, row, kind, kd) in enumerate(pieces):
            block = score[i * rows : (i + 1) * rows]
            if kind == "own" and (not isinstance(d, int) or kd == d):
                late = jnp.where((sub > lane) & (kd == d), HIDE, 0.0)
                block = block + jnp.concatenate([late] * group, axis=1)
            s_scr[buf, i * rows : (i + 1) * rows, :] = block
            top = jnp.maximum(top, jnp.max(block.reshape(rows // 8, 8, wide), axis=0))
        return jnp.max(top, axis=0, keepdims=True)

    def weigh(buf, job, top):
        part = jnp.zeros((8, wide), jnp.float32)
        for i in range(len(jobs[job][4])):
            expo = jnp.exp2((s_scr[buf, i * rows : (i + 1) * rows, :] - top) * SCALE)
            part = part + jnp.sum(expo.reshape(rows // 8, 8, wide), axis=0)
            p_scr[buf, i * rows : (i + 1) * rows, :] = expo.astype(jnp.bfloat16)
        return jnp.sum(part, axis=0, keepdims=True)

    def mix(buf, job, c, g, origin, top, total):
        _, _, _, s, pieces = jobs[job]
        acc = jnp.dot(
            key_block(pieces, g, 1, 1),
            p_scr[buf, : len(pieces) * rows, :],
            preferred_element_type=jnp.float32,
        )
        if s is not None:
            fade = jnp.exp2((states[3 * s][c, g] - top) * SCALE)
            total = total + states[3 * s + 1][c, g] * fade
            acc = acc + states[3 * s + 2][c, g] * fade
        if last:
            acc = (acc * (1.0 / total)).astype(jnp.bfloat16)
            for r in range(group):
                out_scr[at(origin * rows), (g * group + r) * D : (g * group + r + 1) * D] = acc[
                    :, r * rows : (r + 1) * rows
                ].T
            part = out_part(origin, g)
            part.start()
        else:
            outs[3 * job][c, g] = top
            outs[3 * job + 1][c, g] = total
            outs[3 * job + 2][c, g] = acc

    def sweep(chunks):
        known = {}
        origins = [prepare(slot, job, c, known) for slot, (job, c) in enumerate(chunks)]
        units = [(slot, g) for slot in range(len(chunks)) for g in range(kvl)]
        tops, totals = {}, {}
        for i in range(len(units) + 2):
            if i < len(units):
                slot, g = units[i]
                tops[i] = scores(i % bufs, slot, *chunks[slot], g)
            if 0 <= i - 1 < len(units):
                slot, g = units[i - 1]
                totals[i - 1] = weigh((i - 1) % bufs, chunks[slot][0], tops[i - 1])
            if 0 <= i - 2 < len(units):
                slot, g = units[i - 2]
                job, c = chunks[slot]
                mix((i - 2) % bufs, job, c, g, origins[slot], tops[i - 2], totals[i - 2])

    if last:
        before, slot = partial_place(heads, query_begin, query_end, earlier[0])
    if max(job[2] for job in jobs) == 1:
        sweep([(job, 0) for job in range(len(jobs))])
    else:
        for job in range(len(jobs)):
            def body(c, carry, job=job):
                sweep([(job, c)])
                return carry

            lax.fori_loop(0, jobs[job][2], body, 0)
    if last:
        _, own_s, head_ref, _ = earlier
        finish = partial_page(heads, before, slot, own_s, kv_refs[0], head_ref, outs[1], *page)
        for origin in range(heads):
            for g in range(kvl):
                out_part(origin, g).wait()
        finish()


def partial_place(heads, begins, ends, slots):
    base = lax.axis_index("tok") * heads * D
    here = (begins <= base) & (base < ends)
    first = jnp.max(jnp.where(here, begins.astype(jnp.float32), 0.0)).astype(jnp.int32)
    before = lax.rem(base - first, PAGE)
    slot = jnp.max(slots[:, :1].astype(jnp.float32)).astype(jnp.int32)
    return before, slot


def partial_page(heads, before, slot, own_s, rest_s, head_ref, pool_ref, page, sem):
    x = lax.axis_index("head")
    core = lax.rem(lax.axis_index("tok"), 2)
    kvl = head_ref.shape[1]
    d = lax.rem(x + 1, heads)
    lane = lax.broadcasted_iota(jnp.int32, (PAGE, PAGE), 1)
    sub = lax.broadcasted_iota(jnp.int32, (PAGE, PAGE), 0)
    move = jnp.where((lane == sub + PAGE - before) & (sub < before), 1.0, 0.0).astype(jnp.bfloat16)
    copy = pltpu.make_async_copy(page, pool_ref.at[slot], sem)

    def write(ref, row):
        moved = []
        for g in range(kvl):
            at_row = pl.ds(pl.multiple_of(row + D - PAGE, PAGE), PAGE)
            key = ref[at_row, 2 * g * D : (2 * g + 1) * D]
            value = ref[at(row), (2 * g + 1) * D : (2 * g + 2) * D].T[D - PAGE :]
            both = jnp.concatenate([key, value], axis=1)
            moved.append(jnp.dot(move, both, preferred_element_type=jnp.float32))
        moved = jnp.stack(moved, axis=1)
        index = lax.broadcasted_iota(jnp.int32, moved.shape, 0)
        page[...] = jnp.where(index < before, moved, head_ref[...].astype(jnp.float32)).astype(
            jnp.bfloat16
        )
        copy.start()

    @pl.when((before > 0) & (d == 0))
    def _():
        write(own_s, (1 - core) * D)

    @pl.when((before > 0) & (d > 0))
    def _():
        write(rest_s, jnp.maximum(d - 1, 0) * D + (1 - core) * (heads - 1) * D)

    def finish():
        @pl.when(before > 0)
        def _():
            copy.wait()

    return finish


def attend(table, qs, kvs, jobs, last, heads, segs, *earlier):
    kvl = kvs[0].shape[1] // (2 * D)
    states, plan = [], []
    for q, first, state, pieces in jobs:
        many = 1 if first == 0 else heads - 1
        plan.append((q, first, many, None if state is None else len(states), tuple(pieces)))
        if state is not None:
            states.append(state)
    ql = qs[plan[0][0]].shape[0] // D // plan[0][2]
    wide = ql // kvl * D
    if last:
        pool = earlier[3]
        out_shape = [jax.ShapeDtypeStruct((heads * D, ql * D), jnp.bfloat16)]
        out_shape += [jax.ShapeDtypeStruct(pool.shape, pool.dtype)]
    else:
        out_shape = []
        for _, _, many, _, _ in plan:
            row = jax.ShapeDtypeStruct((many, kvl, 1, wide), jnp.float32)
            out_shape += [row, row, jax.ShapeDtypeStruct((many, kvl, D, wide), jnp.float32)]
    inputs = [table, *qs, *kvs, *[part for state in states for part in state], *earlier]
    more = [VMEM, VMEM, VMEM, ANY] if last else [ANY] * len(earlier)
    keys = max(len(job[4]) for job in plan) * D
    together = len(plan) if heads == 2 else 1
    bufs = min(3, kvl * together)
    result = pl.pallas_call(
        functools.partial(
            attend_body, heads, segs, tuple(plan), last,
            (len(qs), len(kvs), len(states), len(earlier)),
        ),
        out_shape=out_shape,
        in_specs=[VMEM] * (len(inputs) - len(earlier)) + more,
        out_specs=[ANY, ANY] if last else [VMEM] * len(out_shape),
        input_output_aliases={len(inputs) - 1: 1} if last else {},
        scratch_shapes=[
            pltpu.VMEM((bufs, keys, wide), jnp.float32),
            pltpu.VMEM((bufs, keys, wide), jnp.bfloat16),
            pltpu.VMEM((together, keys, D), jnp.bfloat16),
            pltpu.VMEM((together, D, wide), jnp.bfloat16),
        ]
        + (
            [
                pltpu.VMEM(out_shape[0].shape, jnp.bfloat16),
                pltpu.SemaphoreType.DMA((heads, kvl)),
                pltpu.VMEM(pool.shape[1:], pool.dtype),
                pltpu.SemaphoreType.DMA,
            ]
            if last
            else []
        ),
        compiler_params=params(),
        cost_estimate=cost(0.01),
        name="attend_last" if last else "attend_part",
    )(*inputs)
    return result if last else [result[i : i + 3] for i in range(0, len(result), 3)]


def pages_body(
    heads, segs, pool, table, slots, own_ref, rest_ref, pool_ref, head_ref,
    slot_scr, wide_scr, out_scr, sems,
):
    x = lax.axis_index("head")
    base = lax.axis_index("tok") * heads * D
    down, down_end, along, _, _, _ = table_rows(segs)
    begins, ends = table[down:down_end], table[down_end:along]
    lane = lax.broadcasted_iota(jnp.int32, (1, D), 1)
    sub = lax.broadcasted_iota(jnp.int32, (D, D), 0)
    starts = [base + lax.rem(x - d + heads, heads) * D for d in range(heads)]
    flags, rows, owned = [], [], []
    for start in starts:
        pos = start + lane
        point = pos.astype(jnp.float32)
        here = (point >= begins) & (point < ends)
        first = jnp.sum(jnp.where(here, begins, 0.0), axis=0, keepdims=True).astype(jnp.int32)
        finish = jnp.sum(jnp.where(here, ends, 0.0), axis=0, keepdims=True).astype(jnp.int32)
        offset = pos - first
        rows.append(lax.rem(offset, PAGE))
        page_last = jnp.minimum(pos - rows[-1] + PAGE, finish) - 1
        owned.append(page_last < base + heads * D)
        flags.append(jnp.where(pos == page_last, 1.0, 0.0))
    flags = jnp.broadcast_to(jnp.concatenate(flags, axis=1), (16, heads * D)).astype(jnp.bfloat16)
    slot_scr[...] = jnp.zeros_like(slot_scr)
    slot_scr[0:1, 0:pool] = slots[...].astype(jnp.float32)
    slot_row = slot_scr[...].astype(jnp.bfloat16)
    ranks, targets = [], []
    for d, start in enumerate(starts):
        ahead = [jnp.where(other + sub < start + lane, 1.0, 0.0) for other in starts]
        ahead = jnp.concatenate(ahead, axis=0).astype(jnp.bfloat16)
        rank = jnp.dot(flags, ahead, preferred_element_type=jnp.float32)[:1].astype(jnp.int32)
        pick_slot = jnp.where(sub == rank, 1.0, 0.0).astype(jnp.bfloat16)
        slot = jnp.dot(slot_row, pick_slot, preferred_element_type=jnp.float32)[:1]
        row = slot.astype(jnp.int32) * PAGE + rows[d]
        targets.append(jnp.where(owned[d], row, -1))
        ranks.append(jnp.where(owned[d] & (rank == 0), rows[d], -1))
    target = jnp.concatenate(targets, axis=1)
    head_target = jnp.concatenate(ranks, axis=1)

    def marks(first_row, rows, target):
        row = first_row + lax.broadcasted_iota(jnp.int32, (rows, heads * D), 0)
        return jnp.where(row == target, 1.0, 0.0).astype(jnp.bfloat16)

    kvl = own_ref.shape[1] // (2 * D)
    both = []
    for g in range(kvl):
        key_at, value_at = at(2 * g * D), at((2 * g + 1) * D)
        others = [rest_ref[i * D : (i + 1) * D, value_at].T for i in range(heads - 1)]
        key = jnp.concatenate([own_ref[:, key_at], rest_ref[:, key_at]], axis=0)
        value = jnp.concatenate([own_ref[:, value_at].T, *others], axis=0)
        both.append(jnp.concatenate([key, value], axis=1))
    step = 8
    copies = []
    for i, page in enumerate(range(0, pool, step)):
        mark = marks(page * PAGE, step * PAGE, target)
        for g in range(kvl):
            wide_scr[i % 2, :, g, :] = jnp.dot(mark, both[g], preferred_element_type=jnp.float32)
        block = pl.ds(page, step)
        out_scr[block] = (
            wide_scr[i % 2].astype(jnp.bfloat16).reshape(step, PAGE, kvl, 2 * D)
        )
        copies.append(pltpu.make_async_copy(out_scr.at[block], pool_ref.at[block], sems.at[i]))
        copies[-1].start()
    mark = marks(0, PAGE, head_target)
    head = [jnp.dot(mark, part, preferred_element_type=jnp.float32) for part in both]
    head_ref[...] = jnp.stack(head, axis=1).astype(jnp.bfloat16)
    for copy in copies:
        copy.wait()


def pages(table, slots, own, rest, heads, segs):
    pool = slots.shape[1]
    kvl = own.shape[1] // (2 * D)
    return pl.pallas_call(
        functools.partial(pages_body, heads, segs, pool),
        out_shape=[
            jax.ShapeDtypeStruct((pool, PAGE, kvl, 2 * D), jnp.bfloat16),
            jax.ShapeDtypeStruct((PAGE, kvl, 2 * D), jnp.bfloat16),
        ],
        in_specs=[VMEM] * 4,
        out_specs=[ANY, VMEM],
        scratch_shapes=[
            pltpu.VMEM((16, D), jnp.float32),
            pltpu.VMEM((2, 8 * PAGE, kvl, 2 * D), jnp.float32),
            pltpu.VMEM((pool, PAGE, kvl, 2 * D), jnp.bfloat16),
            pltpu.SemaphoreType.DMA((pool // 8,)),
        ],
        compiler_params=params(),
        cost_estimate=cost(0.01),
        name="pages",
    )(table, slots, own, rest)


def pick_body(bit, plan, *refs):
    *ins, out = refs
    side = lax.rem(lax.axis_index("tok") // bit, 2)
    row = 0
    for part in plan:
        rows = ins[part[0]].shape[0]
        to = pl.ds(row, rows)
        if len(part) == 1:
            out[to, :] = ins[part[0]][...]
        else:
            for value, index in enumerate(part):
                @pl.when(side == value)
                def _(index=index, to=to):
                    out[to, :] = ins[index][...]
        row += rows


def pick(bit, plan, *arrays):
    rows = sum(arrays[part[0]].shape[0] for part in plan)
    last = max(max(part) for part in plan)
    return pl.pallas_call(
        functools.partial(pick_body, bit, plan),
        out_shape=jax.ShapeDtypeStruct((rows, arrays[0].shape[1]), jnp.bfloat16),
        in_specs=[ANY if i > last else VMEM for i in range(len(arrays))],
        out_specs=VMEM,
        compiler_params=params(8),
        cost_estimate=cost(0.01),
        name="pick",
    )(*arrays)


def after_body(*refs):
    del refs


def after(x, *earlier):
    return pl.pallas_call(
        after_body,
        out_shape=jax.ShapeDtypeStruct(x.shape, x.dtype),
        in_specs=[ANY] * (1 + len(earlier)),
        out_specs=ANY,
        input_output_aliases={0: 0},
        compiler_params=params(1),
        cost_estimate=cost(0.01),
        name="after",
    )(x, *earlier)


def on_device(queries, key_states, value_states, query_gain, key_gain, lengths, slot_order):
    heads = lax.axis_size("head")
    others = range(1, heads)

    table, own, *away = kv_prep(
        lengths, key_states, value_states, key_gain.reshape(1, D), query_gain.reshape(1, D), heads
    )
    segs = lengths.shape[0]
    rest = join([around(part, "head", d) for d, part in enumerate(away, 1)])
    own4 = around(own, "tok", 4)
    q_own, *q_away, turned = q_prep(queries, table, own, heads, segs)
    q_rest = join([around(part, "head", d) for d, part in enumerate(q_away, 1)])
    rest = after(rest, turned)
    rest4, rest2 = around(rest, "tok", 4), onward(rest, "tok", 2)
    base = [(0, 0, "own", 0)] + [(1, d - 1, "own", d) for d in others]
    [own_state] = attend(table, [q_own], [own, rest], [(0, 0, None, base)], False, heads, segs)

    own4 = after(own4, rest)
    own2 = swap(pick(2, ((0, 1),), own, own4), 2)
    page_pool, head_page = pages(table, slot_order, own, rest, heads, segs)
    own_mixed = pick(1, ((0, 1), (2,)), own, own4, own2, head_page, own_state[0])
    own_s = swap(own_mixed, 1)

    qs = [q_own, q_rest]
    near = [(2, 0, "far", 0), (3, 0, "near", 0)]
    own_state, rest_state = attend(
        table, qs, [own, rest, own4, own2],
        [(0, 0, own_state, near), (1, 1, None, base + near)], False, heads, segs,
        own_mixed,
    )

    rest_mixed = pick(1, ((0, 1), (2,)), rest, rest4, rest2, own_state[0])
    rest_s = swap(rest_mixed, 1)
    pieces = [(2, 0, "mix_swap", 0), (2, 1, "near_swap", 0)]
    pieces += [(0, d - 1, "far", d) for d in others] + [(1, d - 1, "near", d) for d in others]
    own_state, rest_state = attend(
        table, qs, [rest4, rest2, own_s],
        [(0, 0, own_state, pieces), (1, 1, rest_state, pieces)], False, heads, segs, rest_mixed,
    )
    pieces = [(0, d - 1, "mix_swap", d) for d in others]
    pieces += [(0, heads + d - 2, "near_swap", d) for d in others]
    attention, page_pool = attend(
        table, qs, [rest_s],
        [(0, 0, own_state, pieces), (1, 1, rest_state, pieces)], True, heads, segs,
        slot_order, own_s, head_page, page_pool,
    )
    return (attention, page_pool)


def solution(mesh):
    in_specs = (
        P(("tok", "head"), None),
        P(("tok", "head"), None),
        P(("tok", "head"), None),
        P(),
        P(),
        P(),
        P("tok", None),
    )
    out_specs = (P("tok", "head"), P("tok", None, "head", None))
    return jax.shard_map(
        on_device, mesh=mesh, in_specs=in_specs, out_specs=out_specs, check_vma=False
    )
```

```python
import functools
import math

import jax
import jax.numpy as jnp
from jax import lax
from jax.experimental import pallas as pl
from jax.experimental.pallas import tpu as pltpu
from jax.sharding import PartitionSpec as P

D = 128
PAGE = 16
HIDE = -2e30
FLOOR = -1e30
MIB = 1024 * 1024
SCALE = math.log2(math.e) / math.sqrt(D)

VMEM = pl.BlockSpec(memory_space=pltpu.VMEM)
SMEM = pl.BlockSpec(memory_space=pltpu.SMEM)
TOKEN = jax.ShapeDtypeStruct((8, D), jnp.float32)
ANY = pl.BlockSpec(memory_space=pl.ANY)
HBM = pl.BlockSpec(memory_space=pltpu.HBM)


def cost(us):
    return pl.CostEstimate(flops=int(us * 1.15e9), bytes_accessed=0, transcendentals=0)


def params(mib=32):
    return pltpu.CompilerParams(vmem_limit_bytes=mib * MIB)


def around(x, axis, by):
    peers = lax.axis_size(axis)
    return lax.ppermute(x, axis, [(i, (i + by) % peers) for i in range(peers)])


def onward(x, axis, by):
    peers = lax.axis_size(axis)
    return lax.ppermute(x, axis, [(i, i + by) for i in range(peers - by)])


def swap(x, bit):
    peers = lax.axis_size("tok")
    return lax.ppermute(x, "tok", [(i, i ^ bit) for i in range(peers)])


def join(parts):
    return parts[0] if len(parts) == 1 else jnp.concatenate(parts, axis=0)


def at(index):
    return pl.ds(index, D) if isinstance(index, int) else pl.ds(pl.multiple_of(index, D), D)


def seg_first(pos, lengths, segs):
    first = jnp.zeros_like(pos)
    start = jnp.int32(0)
    for s in range(segs):
        first = jnp.where(pos >= start, start, first)
        start = start + lengths[s]
    return first


def seg_bounds(shape, axis, lengths, segs):
    index = lax.broadcasted_iota(jnp.int32, shape, axis)
    begin = jnp.where(index == segs, -(2**30), 2**30)
    end = jnp.zeros(shape, jnp.int32)
    here = jnp.int32(0)
    for s in range(segs):
        begin = jnp.where(index == s, here, begin)
        here = here + lengths[s]
        end = jnp.where(index == s, here, end)
    return begin, end


def rotate(x, cos_gain, sin_gain):
    power = jnp.mean(x * x, axis=0, keepdims=True)
    half = D // 2
    turned = jnp.concatenate([x[half:], x[:half]], axis=0)
    return (x * cos_gain + turned * sin_gain) * lax.rsqrt(power + 1e-06)


def gain_tables(cosine, sine, gain_row):
    gain = jnp.broadcast_to(gain_row, (D, D)).T
    half = D // 2
    turned = jnp.concatenate([gain[half:], gain[:half]], axis=0)
    cos_gain = jnp.concatenate([cosine, cosine], axis=0) * gain
    sin_gain = jnp.concatenate([-sine, sine], axis=0) * turned
    return cos_gain, sin_gain


def table_rows(segs):
    used = (segs + 16) // 16 * 16
    starts = [D]
    for rows in (used, used, 8, 8, 8):
        starts.append(starts[-1] + rows)
    return starts


def kv_prep_body(heads, segs, lengths_in, k_in, v_in, gain_in, q_gain_in, table_out, *refs):
    results, refs = refs[:heads], refs[heads:]
    lengths, k_ref, v_ref, gain_ref, q_gain_ref, sems, table_ref, *outs, out_sems = refs
    pairs = [(lengths_in, lengths), (gain_in, gain_ref), (k_in, k_ref), (v_in, v_ref)]
    pairs += [(q_gain_in, q_gain_ref)]
    copies = [pltpu.make_async_copy(a, b, sems.at[i]) for i, (a, b) in enumerate(pairs)]
    for copy in copies:
        copy.start()
    rows = k_ref.shape[0]
    kvl = k_ref.shape[1] // D // heads
    x = lax.axis_index("head")
    base = (lax.axis_index("tok") * heads + x) * rows
    half = D // 2
    pos = base + lax.broadcasted_iota(jnp.int32, (half, rows), 1)
    step = lax.broadcasted_iota(jnp.int32, (half, rows), 0).astype(jnp.float32)
    frequency = jnp.exp(step * (-2.0 * math.log(1000000.0) / D))
    copies[0].wait()
    offset = (pos - seg_first(pos, lengths, segs)).astype(jnp.float32)
    angles = offset * frequency
    cosine, sine = jnp.cos(angles), jnp.sin(angles)
    table_ref[:half] = cosine
    table_ref[half:D] = sine
    down, down_end, along, along_end, gain_at, stop = table_rows(segs)
    begin, end = seg_bounds((down_end - down, D), 0, lengths, segs)
    table_ref[down:down_end] = begin.astype(jnp.float32)
    table_ref[down_end:along] = end.astype(jnp.float32)
    begin, end = seg_bounds((8, D), 1, lengths, segs)
    table_ref[along:along_end] = begin.astype(jnp.float32)
    table_ref[along_end:gain_at] = end.astype(jnp.float32)
    copies[4].wait()
    table_ref[gain_at:stop] = jnp.broadcast_to(q_gain_ref[...], (8, D))
    sends = [pltpu.make_async_copy(table_ref, table_out, out_sems.at[heads])]
    sends[0].start()
    copies[1].wait()
    cos_gain, sin_gain = gain_tables(cosine, sine, gain_ref[...])
    copies[2].wait()
    copies[3].wait()
    for d in reversed(range(heads)):
        peer = lax.rem(x + d, heads)
        for j in range(kvl):
            head = peer * kvl + j
            key = k_ref[:, at(head * D)].T.astype(jnp.float32)
            key = rotate(key, cos_gain, sin_gain).astype(jnp.bfloat16)
            outs[d][:, 2 * j * D : (2 * j + 1) * D] = key.T
            value = v_ref[:, at(head * D)]
            outs[d][:, (2 * j + 1) * D : (2 * j + 2) * D] = value.T
        sends.append(pltpu.make_async_copy(outs[d], results[d], out_sems.at[d]))
        sends[-1].start()
    for send in sends:
        send.wait()


def kv_prep(lengths, keys, values, gain, q_gain, heads):
    rows, width = keys.shape
    table = jax.ShapeDtypeStruct((table_rows(lengths.shape[0])[-1], rows), jnp.float32)
    part = jax.ShapeDtypeStruct((rows, 2 * width // heads), jnp.bfloat16)
    return pl.pallas_call(
        functools.partial(kv_prep_body, heads, lengths.shape[0]),
        out_shape=[table] + [part] * heads,
        in_specs=[HBM] * 5,
        out_specs=[HBM] * (1 + heads),
        scratch_shapes=[
            pltpu.SMEM(lengths.shape, jnp.int32),
            pltpu.VMEM(keys.shape, jnp.bfloat16),
            pltpu.VMEM(values.shape, jnp.bfloat16),
            pltpu.VMEM(gain.shape, jnp.float32),
            pltpu.VMEM(gain.shape, jnp.float32),
            pltpu.SemaphoreType.DMA((5,)),
            pltpu.VMEM(table.shape, jnp.float32),
            *[pltpu.VMEM(part.shape, jnp.bfloat16)] * heads,
            pltpu.SemaphoreType.DMA((heads + 1,)),
        ],
        compiler_params=params(62),
        cost_estimate=cost(0.01),
        name="kv_prep",
    )(lengths, keys, values, gain, q_gain)


def q_prep_body(heads, segs, q_ref, table_ref, own_ref, *refs):
    del own_ref
    *outs, token = refs
    token[...] = jnp.zeros_like(token)
    ql = q_ref.shape[1] // D // heads
    x = lax.axis_index("head")
    half = D // 2
    cos_gain, sin_gain = gain_tables(table_ref[:half], table_ref[half:D], table_ref[pl.ds(table_rows(segs)[4], 1), :])
    for d in reversed(range(heads)):
        peer = lax.rem(x + d, heads)
        for j in range(ql):
            query = q_ref[:, at((peer * ql + j) * D)].T.astype(jnp.float32)
            outs[d][j * D : (j + 1) * D, :] = rotate(query, cos_gain, sin_gain).astype(
                jnp.bfloat16
            )


def q_prep(queries, table, own, heads, segs):
    rows, width = queries.shape
    part = jax.ShapeDtypeStruct((width // heads, rows), jnp.bfloat16)
    return pl.pallas_call(
        functools.partial(q_prep_body, heads, segs),
        out_shape=[part] * heads + [TOKEN],
        in_specs=[VMEM] * 3,
        out_specs=[VMEM] * (heads + 1),
        compiler_params=params(),
        cost_estimate=cost(0.01),
        name="q_prep",
    )(queries, table, own)


def shard_of(kind, tok):
    core = lax.rem(tok, 2)
    if kind == "own":
        return tok
    if kind == "far":
        return tok - 4
    if kind == "near":
        return tok - 2
    if kind == "near_swap":
        return tok - 1 - 2 * core
    return jnp.where(core == 0, tok - 3, tok - 1)


def attend_body(heads, segs, jobs, last, counts, table, *refs):
    n_q, n_kv, n_state, n_earlier = counts
    q_refs, refs = refs[:n_q], refs[n_q:]
    kv_refs, refs = refs[:n_kv], refs[n_kv:]
    states, refs = refs[: 3 * n_state], refs[3 * n_state :]
    earlier, refs = refs[:n_earlier], refs[n_earlier:]
    n_out = 2 if last else 3 * len(jobs)
    outs, (s_scr, p_scr, e_scr, f_scr, *page) = refs[:n_out], refs[n_out:]
    if last:
        out_scr, out_sems, *page = page
    bufs = s_scr.shape[0]
    x = lax.axis_index("head")
    tok = lax.axis_index("tok")
    rows = D
    kvl = kv_refs[0].shape[1] // (2 * D)
    ql = f_scr.shape[2] // D * kvl
    group = ql // kvl
    wide = group * rows
    lane = lax.broadcasted_iota(jnp.int32, (rows, rows), 1)
    sub = lax.broadcasted_iota(jnp.int32, (rows, rows), 0)
    down, down_end, along, along_end, _, _ = table_rows(segs)
    used = down_end - down
    query_begin = table[down:down_end].astype(jnp.int32)
    query_end = table[down_end:along].astype(jnp.int32)
    key_begin = table[along : along + 1].astype(jnp.int32)
    key_end = table[along_end : along_end + 1].astype(jnp.int32)

    def key_block(pieces, g, side, axis):
        cols = at((2 * g + side) * D)
        return jnp.concatenate(
            [kv_refs[a][row * rows : (row + 1) * rows, cols] for a, row, _, _ in pieces],
            axis=axis,
        )

    def out_part(origin, g):
        part = at(origin * rows), pl.ds(g * group * D, group * D)
        sem = out_sems.at[origin, g]
        return pltpu.make_async_copy(out_scr.at[part], outs[0].at[part], sem)

    def prepare(slot, job, c, known):
        _, first, _, _, pieces = jobs[job]
        d = first + c
        origin = lax.rem(x - d + heads, heads)
        q_chunk = tok * heads + origin
        q_pos = q_chunk * rows + lane[:used]
        outside = jnp.where((q_pos >= query_begin) & (q_pos < query_end), 0.0, HIDE)
        outside = jnp.concatenate([outside, jnp.zeros((D - used, D), jnp.float32)], axis=0)
        f_scr[slot] = jnp.concatenate([outside.astype(jnp.bfloat16)] * group, axis=1)
        for i, (a, row, kind, kd) in enumerate(pieces):
            if kind != "own" and (a, row, kind, kd) in known:
                from_slot, j = known[a, row, kind, kd]
                e_scr[slot, i * rows : (i + 1) * rows, :] = e_scr[
                    from_slot, j * rows : (j + 1) * rows, :
                ]
                continue
            known[a, row, kind, kd] = (slot, i)
            k_chunk = shard_of(kind, tok) * heads + lax.rem(x - kd + heads, heads)
            k_pos = jnp.where(k_chunk <= q_chunk, k_chunk * rows + sub, -1)
            inside = (k_pos >= key_begin) & (k_pos < key_end)
            e_scr[slot, i * rows : (i + 1) * rows, :] = jnp.where(inside, 1.0, 0.0).astype(
                jnp.bfloat16
            )
        return origin

    def scores(buf, slot, job, c, g):
        q, first, _, s, pieces = jobs[job]
        d = first + c
        n = len(pieces)
        query = jnp.concatenate(
            [q_refs[q][at((c * ql + g * group + r) * D), :] for r in range(group)], axis=1
        )
        query = jnp.concatenate([query, f_scr[slot]], axis=0)
        keys = jnp.concatenate([key_block(pieces, g, 0, 0), e_scr[slot, : n * rows, :]], axis=1)
        score = jnp.dot(keys, query, preferred_element_type=jnp.float32)
        if s is None:
            top = jnp.full((8, wide), FLOOR, jnp.float32)
        else:
            top = jnp.broadcast_to(states[3 * s][c, g], (8, wide))
        for i, (a, row, kind, kd) in enumerate(pieces):
            block = score[i * rows : (i + 1) * rows]
            if kind == "own" and (not isinstance(d, int) or kd == d):
                late = jnp.where((sub > lane) & (kd == d), HIDE, 0.0)
                block = block + jnp.concatenate([late] * group, axis=1)
            s_scr[buf, i * rows : (i + 1) * rows, :] = block
            top = jnp.maximum(top, jnp.max(block.reshape(rows // 8, 8, wide), axis=0))
        return jnp.max(top, axis=0, keepdims=True)

    def weigh(buf, job, top):
        part = jnp.zeros((8, wide), jnp.float32)
        for i in range(len(jobs[job][4])):
            expo = jnp.exp2((s_scr[buf, i * rows : (i + 1) * rows, :] - top) * SCALE)
            part = part + jnp.sum(expo.reshape(rows // 8, 8, wide), axis=0)
            p_scr[buf, i * rows : (i + 1) * rows, :] = expo.astype(jnp.bfloat16)
        return jnp.sum(part, axis=0, keepdims=True)

    def mix(buf, job, c, g, origin, top, total):
        _, _, _, s, pieces = jobs[job]
        acc = jnp.dot(
            key_block(pieces, g, 1, 1),
            p_scr[buf, : len(pieces) * rows, :],
            preferred_element_type=jnp.float32,
        )
        if s is not None:
            fade = jnp.exp2((states[3 * s][c, g] - top) * SCALE)
            total = total + states[3 * s + 1][c, g] * fade
            acc = acc + states[3 * s + 2][c, g] * fade
        if last:
            acc = (acc * (1.0 / total)).astype(jnp.bfloat16)
            for r in range(group):
                out_scr[at(origin * rows), (g * group + r) * D : (g * group + r + 1) * D] = acc[
                    :, r * rows : (r + 1) * rows
                ].T
            part = out_part(origin, g)
            part.start()
        else:
            outs[3 * job][c, g] = top
            outs[3 * job + 1][c, g] = total
            outs[3 * job + 2][c, g] = acc

    def sweep(chunks):
        known = {}
        origins = [prepare(slot, job, c, known) for slot, (job, c) in enumerate(chunks)]
        units = [(slot, g) for slot in range(len(chunks)) for g in range(kvl)]
        tops, totals = {}, {}
        for i in range(len(units) + 2):
            if i < len(units):
                slot, g = units[i]
                tops[i] = scores(i % bufs, slot, *chunks[slot], g)
            if 0 <= i - 1 < len(units):
                slot, g = units[i - 1]
                totals[i - 1] = weigh((i - 1) % bufs, chunks[slot][0], tops[i - 1])
            if 0 <= i - 2 < len(units):
                slot, g = units[i - 2]
                job, c = chunks[slot]
                mix((i - 2) % bufs, job, c, g, origins[slot], tops[i - 2], totals[i - 2])

    if last:
        before, slot = partial_place(heads, query_begin, query_end, earlier[0])
    if max(job[2] for job in jobs) == 1:
        sweep([(job, 0) for job in range(len(jobs))])
    else:
        for job in range(len(jobs)):
            def body(c, carry, job=job):
                sweep([(job, c)])
                return carry

            lax.fori_loop(0, jobs[job][2], body, 0)
    if last:
        _, own_s, head_ref, _ = earlier
        finish = partial_page(heads, before, slot, own_s, kv_refs[0], head_ref, outs[1], *page)
        for origin in range(heads):
            for g in range(kvl):
                out_part(origin, g).wait()
        finish()


def partial_place(heads, begins, ends, slots):
    base = lax.axis_index("tok") * heads * D
    here = (begins <= base) & (base < ends)
    first = jnp.max(jnp.where(here, begins.astype(jnp.float32), 0.0)).astype(jnp.int32)
    before = lax.rem(base - first, PAGE)
    slot = jnp.max(slots[:, :1].astype(jnp.float32)).astype(jnp.int32)
    return before, slot


def partial_page(heads, before, slot, own_s, rest_s, head_ref, pool_ref, page, sem):
    x = lax.axis_index("head")
    core = lax.rem(lax.axis_index("tok"), 2)
    kvl = head_ref.shape[1]
    d = lax.rem(x + 1, heads)
    lane = lax.broadcasted_iota(jnp.int32, (PAGE, PAGE), 1)
    sub = lax.broadcasted_iota(jnp.int32, (PAGE, PAGE), 0)
    move = jnp.where((lane == sub + PAGE - before) & (sub < before), 1.0, 0.0).astype(jnp.bfloat16)
    copy = pltpu.make_async_copy(page, pool_ref.at[slot], sem)

    def write(ref, row):
        moved = []
        for g in range(kvl):
            at_row = pl.ds(pl.multiple_of(row + D - PAGE, PAGE), PAGE)
            key = ref[at_row, 2 * g * D : (2 * g + 1) * D]
            value = ref[at(row), (2 * g + 1) * D : (2 * g + 2) * D].T[D - PAGE :]
            both = jnp.concatenate([key, value], axis=1)
            moved.append(jnp.dot(move, both, preferred_element_type=jnp.float32))
        moved = jnp.stack(moved, axis=1)
        index = lax.broadcasted_iota(jnp.int32, moved.shape, 0)
        page[...] = jnp.where(index < before, moved, head_ref[...].astype(jnp.float32)).astype(
            jnp.bfloat16
        )
        copy.start()

    @pl.when((before > 0) & (d == 0))
    def _():
        write(own_s, (1 - core) * D)

    @pl.when((before > 0) & (d > 0))
    def _():
        write(rest_s, jnp.maximum(d - 1, 0) * D + (1 - core) * (heads - 1) * D)

    def finish():
        @pl.when(before > 0)
        def _():
            copy.wait()

    return finish


def attend(table, qs, kvs, jobs, last, heads, segs, *earlier):
    kvl = kvs[0].shape[1] // (2 * D)
    states, plan = [], []
    for q, first, state, pieces in jobs:
        many = 1 if first == 0 else heads - 1
        plan.append((q, first, many, None if state is None else len(states), tuple(pieces)))
        if state is not None:
            states.append(state)
    ql = qs[plan[0][0]].shape[0] // D // plan[0][2]
    wide = ql // kvl * D
    if last:
        pool = earlier[3]
        out_shape = [jax.ShapeDtypeStruct((heads * D, ql * D), jnp.bfloat16)]
        out_shape += [jax.ShapeDtypeStruct(pool.shape, pool.dtype)]
    else:
        out_shape = []
        for _, _, many, _, _ in plan:
            row = jax.ShapeDtypeStruct((many, kvl, 1, wide), jnp.float32)
            out_shape += [row, row, jax.ShapeDtypeStruct((many, kvl, D, wide), jnp.float32)]
    inputs = [table, *qs, *kvs, *[part for state in states for part in state], *earlier]
    more = [VMEM, VMEM, VMEM, ANY] if last else [ANY] * len(earlier)
    keys = max(len(job[4]) for job in plan) * D
    together = len(plan) if heads == 2 else 1
    bufs = min(3, kvl * together)
    result = pl.pallas_call(
        functools.partial(
            attend_body, heads, segs, tuple(plan), last,
            (len(qs), len(kvs), len(states), len(earlier)),
        ),
        out_shape=out_shape,
        in_specs=[VMEM] * (len(inputs) - len(earlier)) + more,
        out_specs=[ANY, ANY] if last else [VMEM] * len(out_shape),
        input_output_aliases={len(inputs) - 1: 1} if last else {},
        scratch_shapes=[
            pltpu.VMEM((bufs, keys, wide), jnp.float32),
            pltpu.VMEM((bufs, keys, wide), jnp.bfloat16),
            pltpu.VMEM((together, keys, D), jnp.bfloat16),
            pltpu.VMEM((together, D, wide), jnp.bfloat16),
        ]
        + (
            [
                pltpu.VMEM(out_shape[0].shape, jnp.bfloat16),
                pltpu.SemaphoreType.DMA((heads, kvl)),
                pltpu.VMEM(pool.shape[1:], pool.dtype),
                pltpu.SemaphoreType.DMA,
            ]
            if last
            else []
        ),
        compiler_params=params(),
        cost_estimate=cost(0.01),
        name="attend_last" if last else "attend_part",
    )(*inputs)
    return result if last else [result[i : i + 3] for i in range(0, len(result), 3)]


def pages_body(
    heads, segs, pool, table, slots, own_ref, rest_ref, pool_ref, head_ref,
    slot_scr, wide_scr, out_scr, sems,
):
    x = lax.axis_index("head")
    base = lax.axis_index("tok") * heads * D
    down, down_end, along, _, _, _ = table_rows(segs)
    begins, ends = table[down:down_end], table[down_end:along]
    lane = lax.broadcasted_iota(jnp.int32, (1, D), 1)
    sub = lax.broadcasted_iota(jnp.int32, (D, D), 0)
    starts = [base + lax.rem(x - d + heads, heads) * D for d in range(heads)]
    flags, rows, owned = [], [], []
    for start in starts:
        pos = start + lane
        point = pos.astype(jnp.float32)
        here = (point >= begins) & (point < ends)
        first = jnp.sum(jnp.where(here, begins, 0.0), axis=0, keepdims=True).astype(jnp.int32)
        finish = jnp.sum(jnp.where(here, ends, 0.0), axis=0, keepdims=True).astype(jnp.int32)
        offset = pos - first
        rows.append(lax.rem(offset, PAGE))
        page_last = jnp.minimum(pos - rows[-1] + PAGE, finish) - 1
        owned.append(page_last < base + heads * D)
        flags.append(jnp.where(pos == page_last, 1.0, 0.0))
    flags = jnp.broadcast_to(jnp.concatenate(flags, axis=1), (16, heads * D)).astype(jnp.bfloat16)
    slot_scr[...] = jnp.zeros_like(slot_scr)
    slot_scr[0:1, 0:pool] = slots[...].astype(jnp.float32)
    slot_row = slot_scr[...].astype(jnp.bfloat16)
    ranks, targets = [], []
    for d, start in enumerate(starts):
        ahead = [jnp.where(other + sub < start + lane, 1.0, 0.0) for other in starts]
        ahead = jnp.concatenate(ahead, axis=0).astype(jnp.bfloat16)
        rank = jnp.dot(flags, ahead, preferred_element_type=jnp.float32)[:1].astype(jnp.int32)
        pick_slot = jnp.where(sub == rank, 1.0, 0.0).astype(jnp.bfloat16)
        slot = jnp.dot(slot_row, pick_slot, preferred_element_type=jnp.float32)[:1]
        row = slot.astype(jnp.int32) * PAGE + rows[d]
        targets.append(jnp.where(owned[d], row, -1))
        ranks.append(jnp.where(owned[d] & (rank == 0), rows[d], -1))
    target = jnp.concatenate(targets, axis=1)
    head_target = jnp.concatenate(ranks, axis=1)

    def marks(first_row, rows, target):
        row = first_row + lax.broadcasted_iota(jnp.int32, (rows, heads * D), 0)
        return jnp.where(row == target, 1.0, 0.0).astype(jnp.bfloat16)

    kvl = own_ref.shape[1] // (2 * D)
    both = []
    for g in range(kvl):
        key_at, value_at = at(2 * g * D), at((2 * g + 1) * D)
        others = [rest_ref[i * D : (i + 1) * D, value_at].T for i in range(heads - 1)]
        key = jnp.concatenate([own_ref[:, key_at], rest_ref[:, key_at]], axis=0)
        value = jnp.concatenate([own_ref[:, value_at].T, *others], axis=0)
        both.append(jnp.concatenate([key, value], axis=1))
    step = 8
    copies = []
    for i, page in enumerate(range(0, pool, step)):
        mark = marks(page * PAGE, step * PAGE, target)
        for g in range(kvl):
            wide_scr[i % 2, :, g, :] = jnp.dot(mark, both[g], preferred_element_type=jnp.float32)
        block = pl.ds(page, step)
        out_scr[block] = (
            wide_scr[i % 2].astype(jnp.bfloat16).reshape(step, PAGE, kvl, 2 * D)
        )
        copies.append(pltpu.make_async_copy(out_scr.at[block], pool_ref.at[block], sems.at[i]))
        copies[-1].start()
    mark = marks(0, PAGE, head_target)
    head = [jnp.dot(mark, part, preferred_element_type=jnp.float32) for part in both]
    head_ref[...] = jnp.stack(head, axis=1).astype(jnp.bfloat16)
    for copy in copies:
        copy.wait()


def pages(table, slots, own, rest, heads, segs):
    pool = slots.shape[1]
    kvl = own.shape[1] // (2 * D)
    return pl.pallas_call(
        functools.partial(pages_body, heads, segs, pool),
        out_shape=[
            jax.ShapeDtypeStruct((pool, PAGE, kvl, 2 * D), jnp.bfloat16),
            jax.ShapeDtypeStruct((PAGE, kvl, 2 * D), jnp.bfloat16),
        ],
        in_specs=[VMEM] * 4,
        out_specs=[ANY, VMEM],
        scratch_shapes=[
            pltpu.VMEM((16, D), jnp.float32),
            pltpu.VMEM((2, 8 * PAGE, kvl, 2 * D), jnp.float32),
            pltpu.VMEM((pool, PAGE, kvl, 2 * D), jnp.bfloat16),
            pltpu.SemaphoreType.DMA((pool // 8,)),
        ],
        compiler_params=params(),
        cost_estimate=cost(0.01),
        name="pages",
    )(table, slots, own, rest)


def pick_body(bit, plan, *refs):
    *ins, out = refs
    side = lax.rem(lax.axis_index("tok") // bit, 2)
    row = 0
    for part in plan:
        rows = ins[part[0]].shape[0]
        to = pl.ds(row, rows)
        if len(part) == 1:
            out[to, :] = ins[part[0]][...]
        else:
            for value, index in enumerate(part):
                @pl.when(side == value)
                def _(index=index, to=to):
                    out[to, :] = ins[index][...]
        row += rows


def pick(bit, plan, *arrays):
    rows = sum(arrays[part[0]].shape[0] for part in plan)
    last = max(max(part) for part in plan)
    return pl.pallas_call(
        functools.partial(pick_body, bit, plan),
        out_shape=jax.ShapeDtypeStruct((rows, arrays[0].shape[1]), jnp.bfloat16),
        in_specs=[ANY if i > last else VMEM for i in range(len(arrays))],
        out_specs=VMEM,
        compiler_params=params(8),
        cost_estimate=cost(0.01),
        name="pick",
    )(*arrays)


def after_body(*refs):
    del refs


def after(x, *earlier):
    return pl.pallas_call(
        after_body,
        out_shape=jax.ShapeDtypeStruct(x.shape, x.dtype),
        in_specs=[ANY] * (1 + len(earlier)),
        out_specs=ANY,
        input_output_aliases={0: 0},
        compiler_params=params(1),
        cost_estimate=cost(0.01),
        name="after",
    )(x, *earlier)


def on_device(queries, key_states, value_states, query_gain, key_gain, lengths, slot_order):
    heads = lax.axis_size("head")
    others = range(1, heads)

    table, own, *away = kv_prep(
        lengths, key_states, value_states, key_gain.reshape(1, D), query_gain.reshape(1, D), heads
    )
    segs = lengths.shape[0]
    rest = join([around(part, "head", d) for d, part in enumerate(away, 1)])
    own4 = around(own, "tok", 4)
    q_own, *q_away, turned = q_prep(queries, table, own, heads, segs)
    q_rest = join([around(part, "head", d) for d, part in enumerate(q_away, 1)])
    rest = after(rest, turned)
    rest4, rest2 = around(rest, "tok", 4), onward(rest, "tok", 2)
    base = [(0, 0, "own", 0)] + [(1, d - 1, "own", d) for d in others]
    [own_state] = attend(table, [q_own], [own, rest], [(0, 0, None, base)], False, heads, segs)

    own4 = after(own4, rest)
    own2 = swap(pick(2, ((0, 1),), own, own4), 2)
    page_pool, head_page = pages(table, slot_order, own, rest, heads, segs)
    own_mixed = pick(1, ((0, 1), (2,)), own, own4, own2, head_page)
    own_s = swap(own_mixed, 1)

    qs = [q_own, q_rest]
    near = [(2, 0, "far", 0), (3, 0, "near", 0)]
    own_state, rest_state = attend(
        table, qs, [own, rest, own4, own2],
        [(0, 0, own_state, near), (1, 1, None, base + near)], False, heads, segs,
        own_mixed,
    )

    rest_mixed = pick(1, ((0, 1), (2,)), rest, rest4, rest2, own_state[0])
    rest_s = swap(rest_mixed, 1)
    pieces = [(2, 0, "mix_swap", 0), (2, 1, "near_swap", 0)]
    pieces += [(0, d - 1, "far", d) for d in others] + [(1, d - 1, "near", d) for d in others]
    own_state, rest_state = attend(
        table, qs, [rest4, rest2, own_s],
        [(0, 0, own_state, pieces), (1, 1, rest_state, pieces)], False, heads, segs, rest_mixed,
    )
    pieces = [(0, d - 1, "mix_swap", d) for d in others]
    pieces += [(0, heads + d - 2, "near_swap", d) for d in others]
    attention, page_pool = attend(
        table, qs, [rest_s],
        [(0, 0, own_state, pieces), (1, 1, rest_state, pieces)], True, heads, segs,
        slot_order, own_s, head_page, page_pool,
    )
    return (attention, page_pool)


def solution(mesh):
    in_specs = (
        P(("tok", "head"), None),
        P(("tok", "head"), None),
        P(("tok", "head"), None),
        P(),
        P(),
        P(),
        P("tok", None),
    )
    out_specs = (P("tok", "head"), P("tok", None, "head", None))
    return jax.shard_map(
        on_device, mesh=mesh, in_specs=in_specs, out_specs=out_specs, check_vma=False
    )
```
